768 devices in a mesh: own: 48 (over x, z), grp: 16 (over y, core).
Axes of the slice: x: 4, y: 8, z: 12, core: 2. Of those that a mesh axis runs over, the one named last changes fastest.
Arguments:
- cache: float32 [48, 3072, 128], P('own'), may hold values from -6 to 6
- counts: int32 [48, 16, 48], P('own'), may hold values from 1 to 4, as said below
- hot_rows: int32 [48, 16, 48, 4], P('own'), may hold values from 0 to 511
- lookups: int32 [48, 16, 2048], P('own', 'grp'), may hold values from 0 to 3071, as said below
- bag_lengths: int32 [48, 16, 256], P('own', 'grp'), may hold values from 1 to 32, 2048 in all within a row
- projection: bfloat16 [128, 256], replicated, may hold values from -0.5 to 0.5
- grad_out: bfloat16 [48, 16, 256, 256], P('own', 'grp'), may hold values from -6 to 6
- table: float32 [48, 16, 512, 128], P('own', 'grp'), may hold values from -6 to 6
- accum: float32 [48, 16, 512, 128], P('own', 'grp'), may hold values from 4 to 64
- stale: int32 [48, 16, 48, 4], P('own', 'grp'), may hold values 0 or 1
Outputs:
- projected: bfloat16 [48, 16, 256, 256], P('own', 'grp')
- table_new: float32 [48, 16, 512, 128], P('own', 'grp')
- accum_new: float32 [48, 16, 512, 128], P('own', 'grp')
- cache_new: float32 [48, 3072, 128], P('own')
The draws below stay inside these ranges and needn't reach their ends.
Inputs may be any that keep to these rules, and one draw needn't show every extreme that they name: `counts`: every holder group keeps exactly 4 live slots for the owner device with its own index of own and grp index 0, and for the owner device with the last indices of grp and own. `lookups`: each lookup names a live slot of its holder group: slot (k * 48 + m) * 4 + c with c below counts[o, k, m].
All inputs are finite; a program needn't handle non-finite values. No bound on the sum of `stale` on one device may be relied on, other than what follows from the above.
Results may differ from the reference program's by a relative error of at most 0.0049.
Values sent between devices are 32-bit elements; how exact they have to be, the bound alone decides.
No kernel may reach another device: no remote copies, remote signals or barrier semaphores. Data moves between devices by JAX's collectives and lax.ppermute only.
A program may use at most 32 MiB of HBM per device.

```python
import math
import jax
import jax.numpy as jnp
import numpy as np
from jax import lax

E = 128
P_SIZE = 256
C = 4
MOST_BAG = 32
B = 256
ROWS_DEV = 512
NNZ = 2048
H = 3072
N_OWN = 48
N_GRP = 16


def shared_counts(key):
    counts_key = jax.random.fold_in(key, 11)
    counts_base = jax.random.randint(counts_key, (N_OWN, N_GRP, N_OWN), 1, C + 1)
    hot_owner = jax.random.randint(jax.random.fold_in(key, 12), (N_GRP, N_OWN), 0, 4) == 0
    counts_base = jnp.where(hot_owner[None, :, :], C, counts_base)
    holder = jnp.arange(N_OWN, dtype=jnp.int32)
    grp_ids = jnp.arange(N_GRP, dtype=jnp.int32)
    forced = (holder[:, None, None] == holder[None, None, :]) & (grp_ids[None, :, None] == 0)
    last_owner = (grp_ids[None, :, None] == N_GRP - 1) & (holder[None, None, :] == N_OWN - 1)
    forced = forced | jnp.broadcast_to(last_owner, (N_OWN, N_GRP, N_OWN))
    return jnp.where(forced, C, counts_base).astype(jnp.int32)


def draw_counts(key, part):
    return shared_counts(key)


def draw_lookups(key, part):
    counts = shared_counts(key)
    key = jax.random.fold_in(key, 21)
    bucket = jax.random.randint(key, (N_OWN, N_GRP, NNZ), 0, N_GRP * N_OWN)
    flat_counts = counts.reshape(N_OWN, N_GRP * N_OWN)
    spread_counts = jnp.broadcast_to(flat_counts[:, None, :], (N_OWN, N_GRP, N_GRP * N_OWN))
    bucket_count = jnp.take_along_axis(spread_counts, bucket, axis=2)
    within = jax.random.randint(jax.random.fold_in(key, 22), (N_OWN, N_GRP, NNZ), 0, 1 << 20) % bucket_count
    slots = (bucket * C + within).astype(jnp.int32)
    position = jnp.arange(NNZ, dtype=jnp.int32)[None, None, :]
    slots = jnp.where(position == 0, 0, slots)
    slots = jnp.where(position == NNZ - 1, H - 1, slots)
    return slots.astype(jnp.int32)


def draw_hot_rows(key, part):
    key = jax.random.fold_in(key, 31)
    return jax.random.randint(key, (N_OWN, N_GRP, N_OWN, C), 0, ROWS_DEV).astype(jnp.int32)


def plant(array, own_key, least, top_value):
    extent = array.shape
    place = [jax.random.randint(jax.random.fold_in(own_key, axis), (), 0, extent[axis]) for axis in range(len(extent))]
    array = array.at[tuple(place)].set(least)
    longest = extent.index(max(extent))
    place[longest] = (place[longest] + 1) % extent[longest]
    return array.at[tuple(place)].set(top_value)


def block_scale(rng, shape, shards, least, largest):
    def one(axis_at, parts):
        draws = jax.random.uniform(jax.random.fold_in(jax.random.fold_in(rng, 6), axis_at), (parts,), jnp.float32, least / len(shards), largest / len(shards))
        return jnp.repeat(jnp.exp(draws), shape[axis_at] // parts).reshape((-1,) + (1,) * (len(shape) - axis_at - 1))

    level = one(*shards[0])
    for cut in shards[1:]:
        level = level * one(*cut)
    return level


def profile(count, total, limit, slope):
    portions = [(1 << 20) // math.isqrt(grade ** slope) + 1 for grade in range(2, count + 1)]
    surplus, given = total - limit - (count - 1), [1] * (count - 1)
    while surplus > 0:
        free = [i for i in range(count - 1) if given[i] < limit]
        whole, left = sum([portions[i] for i in free]), surplus
        for i in free:
            addition = min(limit - given[i], max(1, left * portions[i] // whole), surplus)
            given[i] = given[i] + addition
            surplus = surplus - addition
    return np.array([limit] + given)


def uneven_parts(stream_key, count, total, most, slope):
    if count == 2:
        one = jax.random.randint(stream_key, (), max(1, total - most), min(most, total - 1) + 1)
        return jnp.stack([one, total - one])
    tallies = jnp.asarray(profile(count, total, most, slope), jnp.int32)
    twos = (count - 1) // 2
    giver, receiver = tallies[1:1 + 2 * twos:2], tallies[2:2 + 2 * twos:2]
    margin = jnp.minimum(giver - 1, most - receiver)
    moved = jax.random.randint(jax.random.fold_in(stream_key, 1), (twos,), 0, 1 << 20) % (margin + 1)
    tallies = tallies.at[1:1 + 2 * twos:2].set(giver - moved).at[2:2 + 2 * twos:2].set(receiver + moved)
    return tallies[jax.random.permutation(jax.random.fold_in(stream_key, 2), count)]


def normal_values(stream_key, dims, scale, reach, shards=(), kind=jnp.bfloat16):
    factor_of = block_scale(stream_key, dims, shards, -0.22, 0.18) if shards else 1.0
    entries = jax.random.normal(stream_key, dims, jnp.float32) * scale * factor_of
    return jnp.minimum(jnp.maximum(entries, -reach), reach).astype(kind)


def setup_inputs(seed: int = 0) -> dict:
    splits = jax.random.split(jax.random.key(seed), 11)
    cache = normal_values(splits[0], (N_OWN, H, E), 1.0, 6.0, ((0, 48),), jnp.float32)
    counts = draw_counts(jax.random.fold_in(splits[10], 71), 0)
    hot_rows = draw_hot_rows(jax.random.fold_in(splits[10], 71), 0)
    lookups = draw_lookups(jax.random.fold_in(splits[10], 71), 0)
    bag_lengths = jax.vmap(lambda own: uneven_parts(own, B, NNZ, MOST_BAG, 2))(jax.random.split(splits[4], N_OWN * N_GRP)).reshape((N_OWN, N_GRP, B)).astype(jnp.int32)
    projection = normal_values(splits[5], (E, P_SIZE), E ** -0.5, 0.5)
    grad_out = normal_values(splits[6], (N_OWN, N_GRP, B, P_SIZE), 1.0, 6.0, ((0, 48), (1, 16)))
    table = normal_values(splits[7], (N_OWN, N_GRP, ROWS_DEV, E), 1.0, 6.0, ((0, 48), (1, 16)), jnp.float32)
    accum = jnp.clip(jnp.exp(math.log(64.0) - 2.7725887 * jax.random.uniform(splits[8], (N_OWN, N_GRP, ROWS_DEV, E), jnp.float32) ** block_scale(splits[8], (N_OWN, N_GRP, ROWS_DEV, E), ((0, 48), (1, 16)), -0.2, 0.2)), 4.0, 64.0)
    stale = plant((jax.random.randint(splits[9], (N_OWN, N_GRP, N_OWN, C), 0, 4) < 3).astype(jnp.int32), jax.random.fold_in(splits[9], 1), 0, 1)
    return dict(cache=cache, counts=counts, hot_rows=hot_rows, lookups=lookups, bag_lengths=bag_lengths, projection=projection, grad_out=grad_out, table=table, accum=accum, stale=stale)


learn_rate = 0.3
epsilon = 1e-06

def one_device(cache_rows, lookup, lengths, cotangent, projection):
    bag_ends = jnp.cumsum(lengths).astype(jnp.int32)
    position = jnp.arange(NNZ, dtype=jnp.int32)
    segment = lax.optimization_barrier(jnp.sum((bag_ends[None, :] <= position[:, None]).astype(jnp.int32), axis=1)).astype(jnp.int32)
    gathered = cache_rows[lookup]
    pooled = jax.ops.segment_sum(gathered, segment, num_segments=B).astype(jnp.bfloat16)
    projected = jnp.dot(pooled, projection, preferred_element_type=jnp.float32).astype(jnp.bfloat16)
    grad_pooled = jnp.dot(cotangent, projection.T, preferred_element_type=jnp.float32)
    slot_delta = jnp.zeros((H, E), jnp.float32).at[lookup].add(grad_pooled[segment])
    return (projected, slot_delta)

def one_group(group_args, projection):
    cache_rows, lookup_group, length_group, cot_group = group_args

    def device_step(lookup, lengths, cotangent):
        return one_device(cache_rows, lookup, lengths, cotangent, projection)
    projected, slot_deltas = jax.vmap(device_step)(lookup_group, length_group, cot_group)
    return (projected, lax.optimization_barrier(jnp.sum(slot_deltas, axis=0)))

def owner_step(incoming, row_ids, rows, accumulated, stale_flags):
    flat_ids = row_ids.reshape(-1)
    gradient = jax.ops.segment_sum(incoming.reshape(-1, E), flat_ids, num_segments=ROWS_DEV)
    accum_new = accumulated + gradient * gradient
    table_new = rows - learn_rate * gradient / (jnp.sqrt(accum_new) + epsilon)
    change = (table_new - rows)[flat_ids].reshape(N_OWN, C, E)
    change = change * stale_flags[:, :, None].astype(jnp.float32)
    return (table_new, accum_new, change)

def reference(cache, counts, hot_rows, lookups, bag_lengths, projection, grad_out, table, accum, stale):
    projected, deltas = lax.map(lambda group_args: one_group(group_args, projection), (cache, lookups, bag_lengths, grad_out))
    incoming = deltas.reshape(N_OWN, N_GRP, N_OWN, C, E).transpose(2, 1, 0, 3, 4)
    row_ids = hot_rows.transpose(2, 1, 0, 3)
    table_new, accum_new, change = jax.vmap(jax.vmap(owner_step))(incoming, row_ids, table, accum, stale)
    returned = change.transpose(2, 1, 0, 3, 4).reshape(N_OWN, H, E)
    live_mask = (jnp.arange(C, dtype=jnp.int32)[None, None, None, :] < counts[:, :, :, None]).reshape(N_OWN, H)
    cache_new = cache + jnp.where(live_mask[:, :, None], returned, jnp.float32(0.0))
    return (projected, table_new, accum_new, cache_new)
```

```python
import jax
import jax.numpy as jnp
from jax import lax
from jax.experimental import pallas as pl
from jax.experimental.pallas import tpu as pltpu
from jax.sharding import Mesh
from jax.sharding import PartitionSpec as P

learn_rate = 0.3
epsilon = 1e-06
LOOKUP_ROWS = 16
LENGTH_ROWS = 2
OWN = ("x", "z")
GRP = ("y", "core")
VMEM_BYTES = 40 * 1024 * 1024


def split(values):
    high = values.astype(jnp.bfloat16)
    low = (values - high.astype(jnp.float32)).astype(jnp.bfloat16)
    return jnp.concatenate([high, low], axis=1)


def joined(values):
    width = values.shape[1] // 2
    return values[:, :width] + values[:, width:]


def row_of(ref, first, count):
    return jnp.concatenate([ref[r : r + 1, :] for r in range(first, first + count)], axis=1)


def bag_hot(lengths):
    bags = lengths.shape[1]
    before = lax.broadcasted_iota(jnp.int32, (bags, bags), 0)
    after = lax.broadcasted_iota(jnp.int32, (bags, bags), 1)
    upper = jnp.where(before <= after, 1.0, 0.0).astype(jnp.bfloat16)
    tall = jnp.broadcast_to(lengths, (8, bags)).astype(jnp.bfloat16)
    ends = jnp.dot(tall, upper, preferred_element_type=jnp.float32)[0:1, :]
    starts = ends - lengths
    ends = ends.astype(jnp.int32)
    starts = starts.astype(jnp.int32)
    position = lax.broadcasted_iota(jnp.int32, (LOOKUP_ROWS * 128, bags), 0)
    inside = (position >= starts) & (position < ends)
    return jnp.where(inside, 1.0, 0.0).astype(jnp.bfloat16)


def slot_parts(lookup, span, groups):
    group = jnp.zeros_like(lookup)
    for k in range(1, groups):
        group = group + jnp.where(lookup >= k * span, 1, 0)
    place = lookup - group * span
    rows = lax.broadcasted_iota(jnp.int32, (span, lookup.shape[1]), 0)
    hot = jnp.where(rows == place, 1.0, 0.0).astype(jnp.bfloat16)
    return group, hot


def in_group(group, k):
    return jnp.where(group == k, 1.0, 0.0).astype(jnp.bfloat16)


def pack_kernel(lookup_ref, length_ref, cotangent_ref, projection_ref, out_ref):
    bags = cotangent_ref.shape[0]
    out_ref[:bags, :] = lax.dot_general(
        cotangent_ref[...],
        projection_ref[...],
        (((1,), (1,)), ((), ())),
        preferred_element_type=jnp.float32,
    )
    out_ref[bags : bags + LOOKUP_ROWS, :] = lookup_ref[...].astype(jnp.float32)
    tail = jnp.zeros((8 - LENGTH_ROWS, 128), jnp.float32)
    out_ref[bags + LOOKUP_ROWS :, :] = jnp.concatenate(
        [length_ref[...].astype(jnp.float32), tail], axis=0
    )


def count_kernel(lookup_ref, length_ref, count_ref):
    span = 192
    groups = count_ref.shape[0] // span
    lookup = row_of(lookup_ref, 0, LOOKUP_ROWS)
    bags = bag_hot(row_of(length_ref, 0, LENGTH_ROWS).astype(jnp.float32))
    group, hot = slot_parts(lookup, span, groups)
    step = 4
    for k in range(0, groups, step):
        slots = jnp.concatenate([hot * in_group(group, j) for j in range(k, k + step)], axis=0)
        count = jnp.dot(slots, bags, preferred_element_type=jnp.float32)
        count_ref[k * span : (k + step) * span, :] = count.astype(jnp.bfloat16)


def slot_kernel(core_ref, count_ref, mine_ref, other_ref, out_ref):
    span = out_ref.shape[1]
    chips = out_ref.shape[0]
    core = core_ref[0]
    bags = count_ref.shape[1]
    top = bags + LOOKUP_ROWS
    lookup = row_of(other_ref, bags, LOOKUP_ROWS).astype(jnp.int32)
    other_bags = bag_hot(row_of(other_ref, top, LENGTH_ROWS))
    group, hot = slot_parts(lookup, span, 2 * chips)
    mine = split(mine_ref[:bags, :])
    other = split(other_ref[:bags, :])
    step = 4
    for y in range(0, chips, step):
        slots = jnp.concatenate(
            [hot * in_group(group, 2 * j + core) for j in range(y, y + step)], axis=0
        )
        count = jnp.dot(slots, other_bags, preferred_element_type=jnp.float32)
        delta = jnp.dot(count.astype(jnp.bfloat16), other, preferred_element_type=jnp.float32)
        for j in range(y, y + step):
            own_count = count_ref[pl.ds(pl.multiple_of((2 * j + core) * span, span), span), :]
            here = jnp.dot(own_count, mine, preferred_element_type=jnp.float32)
            out_ref[j, :, :] = joined(here + delta[(j - y) * span : (j - y + 1) * span, :])


def pool_kernel(count_ref, cache_ref, projection_ref, out_ref):
    pooled = lax.dot_general(
        count_ref[...],
        split(cache_ref[...]),
        (((0,), (0,)), ((), ())),
        preferred_element_type=jnp.float32,
    )
    pooled = joined(pooled).astype(jnp.bfloat16)
    out_ref[...] = jnp.dot(pooled, projection_ref[...], preferred_element_type=jnp.float32).astype(
        jnp.bfloat16
    )


def owner_kernel(
    incoming_ref, ids_ref, stale_ref, table_ref, accum_ref, table_new_ref, accum_new_ref, change_ref
):
    table_rows = table_ref.shape[0]
    ids = ids_ref[...]
    rows = lax.broadcasted_iota(jnp.int32, (table_rows, ids.shape[1]), 0)
    hot = jnp.where(rows == ids, 1.0, 0.0)
    gradient = joined(
        jnp.dot(hot.astype(jnp.bfloat16), split(incoming_ref[...]), preferred_element_type=jnp.float32)
    )
    accum_new = accum_ref[...] + gradient * gradient
    accum_new_ref[...] = accum_new
    old = table_ref[...]
    new = old - learn_rate * gradient / (jnp.sqrt(accum_new) + epsilon)
    table_new_ref[...] = new
    wanted = (hot * stale_ref[...].astype(jnp.float32)).astype(jnp.bfloat16)
    change_ref[...] = joined(
        lax.dot_general(
            wanted, split(new - old), (((0,), (0,)), ((), ())), preferred_element_type=jnp.float32
        )
    )


def refresh_kernel(core_ref, counts_ref, cache_ref, change_ref, *rest, flip):
    out_ref = rest[-1]
    chips, _, span, width = out_ref.shape
    owners = counts_ref.shape[1]
    core = core_ref[0]
    if flip:
        core = 1 - core
    first = pl.program_id(0) * chips
    place = lax.broadcasted_iota(jnp.int32, (span, owners), 0) - (
        span // owners
    ) * lax.broadcasted_iota(jnp.int32, (span, owners), 1)
    ones = jnp.ones((owners, width), jnp.bfloat16)
    for y in range(chips):
        counts = counts_ref[pl.ds(2 * (first + y) + core, 1), :]
        live = jnp.where((place >= 0) & (place < counts), 1.0, 0.0).astype(jnp.bfloat16)
        live = jnp.dot(live, ones, preferred_element_type=jnp.float32)
        out_ref[y, 0, :, :] = cache_ref[y, 0, :, :] + jnp.where(
            live > 0.5, change_ref[y, :, :], 0.0
        )


def params():
    return pltpu.CompilerParams(vmem_limit_bytes=VMEM_BYTES)


def whole(*shape):
    return pl.BlockSpec(shape, lambda *_: (0,) * len(shape))


def pack(lookup, lengths, cotangent, projection):
    rows = cotangent.shape[0] + LOOKUP_ROWS + 8
    return pl.pallas_call(
        pack_kernel,
        out_shape=jax.ShapeDtypeStruct((rows, projection.shape[0]), jnp.float32),
        compiler_params=params(),
        cost_estimate=pl.CostEstimate(flops=2 * 256 * 256 * 128, bytes_accessed=400000, transcendentals=0),
        name="pack",
    )(lookup, lengths, cotangent, projection)


def count(lookup, lengths, slots):
    return pl.pallas_call(
        count_kernel,
        out_shape=jax.ShapeDtypeStruct((slots, lengths.size), jnp.bfloat16),
        compiler_params=params(),
        cost_estimate=pl.CostEstimate(flops=2 * 3072 * 2048 * 256, bytes_accessed=1600000, transcendentals=0),
        name="count",
    )(lookup, lengths)


def slot_sums(core, counted, mine, other, chips, span):
    vmem = pl.BlockSpec(memory_space=pltpu.VMEM)
    return pl.pallas_call(
        slot_kernel,
        out_shape=jax.ShapeDtypeStruct((chips, span, mine.shape[1]), jnp.float32),
        in_specs=[pl.BlockSpec(memory_space=pltpu.SMEM), vmem, vmem, vmem],
        out_specs=vmem,
        compiler_params=params(),
        cost_estimate=pl.CostEstimate(flops=3072 * 2048 * 256, bytes_accessed=2600000, transcendentals=0),
        name="slot_sums",
    )(core, counted, mine, other)


def pool(counted, cache_rows, projection):
    return pl.pallas_call(
        pool_kernel,
        out_shape=jax.ShapeDtypeStruct((counted.shape[1], projection.shape[1]), jnp.bfloat16),
        compiler_params=params(),
        cost_estimate=pl.CostEstimate(flops=2 * 3072 * 256 * 256, bytes_accessed=3400000, transcendentals=0),
        name="pool",
    )(counted, cache_rows, projection)


def owner(incoming, ids, stale, table, accum):
    table_like = jax.ShapeDtypeStruct(table.shape, jnp.float32)
    return pl.pallas_call(
        owner_kernel,
        out_shape=(table_like, table_like, jax.ShapeDtypeStruct(incoming.shape, jnp.float32)),
        compiler_params=params(),
        cost_estimate=pl.CostEstimate(flops=4 * 512 * 192 * 256, bytes_accessed=1300000, transcendentals=65536),
        name="owner",
    )(incoming, ids, stale, table, accum)


def refresh(core, counts, cache_rows, change, done=None):
    flip = done is not None
    chips, span, width = change.shape
    step = chips // 2

    def half(i, core_ref):
        return (i, 1 - core_ref[0] if flip else core_ref[0], 0, 0)

    block = pl.BlockSpec((step, 1, span, width), half)
    in_specs = [
        pl.BlockSpec(counts.shape, lambda i, core_ref: (0, 0)),
        block,
        pl.BlockSpec((step, span, width), lambda i, core_ref: (i, 0, 0)),
    ]
    args = [core, counts, cache_rows.reshape(chips, 2, span, width), change]
    if flip:
        in_specs.append(pl.BlockSpec(memory_space=pl.ANY))
        args.append(done)

    def body(*refs):
        refresh_kernel(*refs, flip=flip)

    return pl.pallas_call(
        body,
        grid_spec=pltpu.PrefetchScalarGridSpec(
            num_scalar_prefetch=1, grid=(2,), in_specs=in_specs, out_specs=block
        ),
        out_shape=jax.ShapeDtypeStruct((chips, 2, span, width), jnp.float32),
        input_output_aliases={4: 0} if flip else {},
        compiler_params=params(),
        cost_estimate=pl.CostEstimate(flops=400000, bytes_accessed=2400000, transcendentals=0),
        name="refresh_other" if flip else "refresh_mine",
    )(*args)


def shards(
    cache, counts, hot_rows, lookups, bag_lengths, projection, grad_out, table, accum, stale
):
    n_own = hot_rows.shape[2]
    chips = lax.axis_size("y")
    capacity = hot_rows.shape[3]
    slots, width = cache.shape[1:]
    span = n_own * capacity
    lookup = lookups.reshape(LOOKUP_ROWS, 128)
    lengths = bag_lengths.reshape(LENGTH_ROWS, 128)
    core = lax.axis_index("core").astype(jnp.int32).reshape(1)
    swap = [(0, 1), (1, 0)]

    own_ids = lax.dynamic_index_in_dim(hot_rows[0], lax.axis_index(GRP), 0, keepdims=False)
    row_ids = lax.all_to_all(own_ids, OWN, split_axis=0, concat_axis=0, tiled=True)

    mine = pack(lookup, lengths, grad_out[0, 0], projection)
    other = lax.ppermute(mine, "core", swap)
    counted = count(lookup, lengths, slots)
    half = slot_sums(core, counted, mine, other, chips, span)
    parts = lax.all_to_all(half, "y", split_axis=0, concat_axis=0, tiled=True)
    summed = jnp.sum(parts, axis=0).reshape(n_own, capacity, width)
    incoming = lax.all_to_all(summed, OWN, split_axis=0, concat_axis=0, tiled=True)

    table_new, accum_new, change = owner(
        incoming.reshape(span, width),
        row_ids.reshape(1, span),
        stale.reshape(1, span),
        table[0, 0],
        accum[0, 0],
    )

    returned = lax.all_to_all(
        change.reshape(n_own, capacity, width), OWN, split_axis=0, concat_axis=0, tiled=True
    )
    wide = jnp.broadcast_to(returned.reshape(1, span, width), (chips, span, width))
    near = lax.all_to_all(wide, "y", split_axis=0, concat_axis=0, tiled=True)
    far = lax.ppermute(near, "core", swap)
    refreshed = refresh(core, counts[0], cache[0], near)
    refreshed = refresh(core, counts[0], cache[0], far, done=refreshed)

    projected = pool(counted, cache[0], projection)
    return (
        projected[None, None],
        table_new[None, None],
        accum_new[None, None],
        refreshed.reshape(1, slots, width),
    )


def solution(mesh):
    chips = Mesh(mesh.devices.reshape(4, 12, 8, 2), ("x", "z", "y", "core"))
    return jax.shard_map(
        shards,
        mesh=chips,
        in_specs=(
            P(OWN, None, None),
            P(OWN, None, None),
            P(OWN, None, None, None),
            P(OWN, GRP, None),
            P(OWN, GRP, None),
            P(),
            P(OWN, GRP, None, None),
            P(OWN, GRP, None, None),
            P(OWN, GRP, None, None),
            P(OWN, GRP, None, None),
        ),
        out_specs=(
            P(OWN, GRP, None, None),
            P(OWN, GRP, None, None),
            P(OWN, GRP, None, None),
            P(OWN, None, None),
        ),
        check_vma=False,
    )
```

```python
import jax
import jax.numpy as jnp
from jax import lax
from jax.experimental import pallas as pl
from jax.experimental.pallas import tpu as pltpu
from jax.sharding import Mesh
from jax.sharding import PartitionSpec as P

learn_rate = 0.3
epsilon = 1e-06
LOOKUP_ROWS = 16
LENGTH_ROWS = 2
OWN = ("x", "z")
GRP = ("y", "core")
STEP = 4
VMEM_BYTES = 40 * 1024 * 1024


def split(values):
    high = values.astype(jnp.bfloat16)
    low = (values - high.astype(jnp.float32)).astype(jnp.bfloat16)
    return jnp.concatenate([high, low], axis=1)


def joined(values):
    width = values.shape[1] // 2
    return values[:, :width] + values[:, width:]


def row_of(ref, first, count):
    return jnp.concatenate([ref[r : r + 1, :] for r in range(first, first + count)], axis=1)


def bag_hot(lengths):
    bags = lengths.shape[1]
    before = lax.broadcasted_iota(jnp.int32, (bags, bags), 0)
    after = lax.broadcasted_iota(jnp.int32, (bags, bags), 1)
    upper = jnp.where(before <= after, 1.0, 0.0).astype(jnp.bfloat16)
    tall = jnp.broadcast_to(lengths, (8, bags)).astype(jnp.bfloat16)
    ends = jnp.dot(tall, upper, preferred_element_type=jnp.float32)[0:1, :]
    starts = ends - lengths
    ends = ends.astype(jnp.int32)
    starts = starts.astype(jnp.int32)
    position = lax.broadcasted_iota(jnp.int32, (LOOKUP_ROWS * 128, bags), 0)
    inside = (position >= starts) & (position < ends)
    return jnp.where(inside, 1.0, 0.0).astype(jnp.bfloat16)


def slot_parts(lookup, span, groups):
    group = jnp.zeros_like(lookup)
    for k in range(1, groups):
        group = group + jnp.where(lookup >= k * span, 1, 0)
    place = lookup - group * span
    rows = lax.broadcasted_iota(jnp.int32, (span, lookup.shape[1]), 0)
    hot = jnp.where(rows == place, 1.0, 0.0).astype(jnp.bfloat16)
    return group, hot


def in_group(group, k):
    return jnp.where(group == k, 1.0, 0.0).astype(jnp.bfloat16)


def pack_kernel(lookup_hbm, length_hbm, cotangent_hbm, projection_hbm, out_ref, lookup, length, cotangent, projection, arrived):
    bags = cotangent.shape[0]
    sources = (lookup_hbm, length_hbm, cotangent_hbm, projection_hbm)
    copies = [
        pltpu.make_async_copy(source, target, arrived.at[i])
        for i, (source, target) in enumerate(zip(sources, (lookup, length, cotangent, projection)))
    ]
    for copy in copies:
        copy.start()
    for copy in copies:
        copy.wait()
    out_ref[:bags, :] = lax.dot_general(
        cotangent[...],
        projection[...],
        (((1,), (1,)), ((), ())),
        preferred_element_type=jnp.float32,
    )
    out_ref[bags : bags + LOOKUP_ROWS, :] = lookup[...].astype(jnp.float32)
    tail = jnp.zeros((8 - LENGTH_ROWS, 128), jnp.float32)
    out_ref[bags + LOOKUP_ROWS :, :] = jnp.concatenate(
        [length[...].astype(jnp.float32), tail], axis=0
    )


def unpack(packed_ref):
    bags = packed_ref.shape[0] - LOOKUP_ROWS - 8
    lookup = row_of(packed_ref, bags, LOOKUP_ROWS).astype(jnp.int32)
    return lookup, row_of(packed_ref, bags + LOOKUP_ROWS, LENGTH_ROWS)


def slot_kernel(core_ref, packed_ref, *refs):
    out_ref = refs[-1]
    chips, span, _ = out_ref.shape
    core = core_ref[0]
    lookup, lengths = unpack(packed_ref)
    bags = lengths.shape[1]
    rows = jnp.dot(
        bag_hot(lengths), split(packed_ref[:bags, :]), preferred_element_type=jnp.float32
    ).astype(jnp.bfloat16)
    group, hot = slot_parts(lookup, span, 2 * chips)
    for y in range(0, chips, STEP):
        slots = jnp.concatenate(
            [hot * in_group(group, 2 * j + core) for j in range(y, y + STEP)], axis=0
        )
        delta = joined(jnp.dot(slots, rows, preferred_element_type=jnp.float32))
        delta = delta.reshape(STEP, span, delta.shape[1])
        if len(refs) == 2:
            delta = delta + refs[0][y : y + STEP, :, :]
        out_ref[y : y + STEP, :, :] = delta


def pool_kernel(packed_ref, cache_ref, projection_ref, out_ref, count_ref):
    slots = cache_ref.shape[0]
    span = 192
    groups = slots // span
    lookup, lengths = unpack(packed_ref)
    bags = bag_hot(lengths)
    group, hot = slot_parts(lookup, span, groups)
    for k in range(0, groups, STEP):
        chosen = jnp.concatenate([hot * in_group(group, j) for j in range(k, k + STEP)], axis=0)
        count = jnp.dot(chosen, bags, preferred_element_type=jnp.float32)
        count_ref[k * span : (k + STEP) * span, :] = count.astype(jnp.bfloat16)
    pooled = lax.dot_general(
        count_ref[...],
        split(cache_ref[...]),
        (((0,), (0,)), ((), ())),
        preferred_element_type=jnp.float32,
    )
    pooled = joined(pooled).astype(jnp.bfloat16)
    out_ref[...] = jnp.dot(pooled, projection_ref[...], preferred_element_type=jnp.float32).astype(
        jnp.bfloat16
    )


def combine_kernel(parts_ref, ids_ref, out_ref):
    owners, _ = ids_ref.shape
    capacity = parts_ref.shape[1] // owners
    for c in range(capacity):
        rows = pl.ds(c, owners, stride=capacity)
        total = parts_ref[0, rows, :]
        for y in range(1, parts_ref.shape[0]):
            total = total + parts_ref[y, rows, :]
        out_ref[pl.ds(c, owners, stride=capacity + 1), :] = total
    out_ref[pl.ds(capacity, owners, stride=capacity + 1), :] = ids_ref[...]


def owner_kernel(
    incoming_ref, stale_ref, table_ref, accum_ref, table_new_ref, accum_new_ref, change_ref
):
    holders, capacity = stale_ref.shape
    table_rows = table_ref.shape[0]

    def taken(c):
        return incoming_ref[pl.ds(c, holders, stride=capacity + 1), :]

    ids = taken(capacity)[:, :capacity].astype(jnp.int32)
    stale = stale_ref[...].astype(jnp.float32)
    row = lax.broadcasted_iota(jnp.int32, (holders, table_rows), 1)
    hot = [jnp.where(row == ids[:, c : c + 1], 1.0, 0.0) for c in range(capacity)]
    wanted = [hot[c] * stale[:, c : c + 1] for c in range(capacity)]
    incoming = jnp.concatenate([taken(c) for c in range(capacity)], axis=0)
    gradient = joined(
        lax.dot_general(
            jnp.concatenate(hot, axis=0).astype(jnp.bfloat16),
            split(incoming),
            (((0,), (0,)), ((), ())),
            preferred_element_type=jnp.float32,
        )
    )
    accum_new = accum_ref[...] + gradient * gradient
    accum_new_ref[...] = accum_new
    old = table_ref[...]
    new = old - learn_rate * gradient / (jnp.sqrt(accum_new) + epsilon)
    table_new_ref[...] = new
    change = joined(
        jnp.dot(
            jnp.concatenate(wanted, axis=0).astype(jnp.bfloat16),
            split(new - old),
            preferred_element_type=jnp.float32,
        )
    )
    for c in range(capacity):
        change_ref[pl.ds(c, holders, stride=capacity), :] = change[
            c * holders : (c + 1) * holders, :
        ]


def refresh_kernel(core_ref, counts_ref, cache_ref, change_ref, *rest, flip):
    out_ref = rest[-1]
    chips, _, span, width = out_ref.shape
    owners = counts_ref.shape[1]
    core = core_ref[0]
    if flip:
        core = 1 - core
    first = pl.program_id(0) * chips
    place = lax.broadcasted_iota(jnp.int32, (span, owners), 0) - (
        span // owners
    ) * lax.broadcasted_iota(jnp.int32, (span, owners), 1)
    ones = jnp.ones((owners, width), jnp.bfloat16)
    for y in range(chips):
        counts = counts_ref[pl.ds(2 * (first + y) + core, 1), :]
        live = jnp.where((place >= 0) & (place < counts), 1.0, 0.0).astype(jnp.bfloat16)
        live = jnp.dot(live, ones, preferred_element_type=jnp.float32)
        out_ref[y, 0, :, :] = cache_ref[y, 0, :, :] + jnp.where(
            live > 0.5, change_ref[y, :, :], 0.0
        )


def params(limit=VMEM_BYTES):
    return pltpu.CompilerParams(vmem_limit_bytes=limit)


def cost(flops, moved):
    return pl.CostEstimate(flops=flops, bytes_accessed=moved, transcendentals=0)


def pack(lookup, lengths, cotangent, projection):
    rows = cotangent.shape[0] + LOOKUP_ROWS + 8
    given = (lookup, lengths, cotangent, projection)
    return pl.pallas_call(
        pack_kernel,
        out_shape=jax.ShapeDtypeStruct((rows, projection.shape[0]), jnp.float32),
        in_specs=[pl.BlockSpec(memory_space=pl.ANY)] * 4,
        out_specs=pl.BlockSpec(memory_space=pltpu.VMEM),
        scratch_shapes=[pltpu.VMEM(a.shape, a.dtype) for a in given]
        + [pltpu.SemaphoreType.DMA((4,))],
        compiler_params=params(63 * 1024 * 1024),
        cost_estimate=cost(2 * 256 * 256 * 128, 400000),
        name="pack",
    )(*given)


def slot_sums(core, packed, chips, span, start=None):
    vmem = pl.BlockSpec(memory_space=pltpu.VMEM)
    args = [core, packed] + ([] if start is None else [start])
    return pl.pallas_call(
        slot_kernel,
        out_shape=jax.ShapeDtypeStruct((chips, span, packed.shape[1]), jnp.float32),
        in_specs=[pl.BlockSpec(memory_space=pltpu.SMEM)] + [vmem] * (len(args) - 1),
        out_specs=vmem,
        compiler_params=params(),
        cost_estimate=cost(3072 * 2048 * 256, 1000000),
        name="own_slots" if start is None else "all_slots",
    )(*args)


def pool(packed, cache_rows, projection):
    bags = packed.shape[0] - LOOKUP_ROWS - 8
    return pl.pallas_call(
        pool_kernel,
        out_shape=jax.ShapeDtypeStruct((bags, projection.shape[1]), jnp.bfloat16),
        scratch_shapes=[pltpu.VMEM((cache_rows.shape[0], bags), jnp.bfloat16)],
        compiler_params=params(),
        cost_estimate=cost(2 * 3072 * 2048 * 256, 2000000),
        name="pool",
    )(packed, cache_rows, projection)


def combine(parts, ids):
    chips, span, width = parts.shape
    return pl.pallas_call(
        combine_kernel,
        out_shape=jax.ShapeDtypeStruct((span + ids.shape[0], width), jnp.float32),
        compiler_params=params(),
        cost_estimate=cost(200000, 900000),
        name="combine",
    )(parts, ids)


def owner(incoming, stale, table, accum):
    table_like = jax.ShapeDtypeStruct(table.shape, jnp.float32)
    change = jax.ShapeDtypeStruct((stale.size, table.shape[1]), jnp.float32)
    return pl.pallas_call(
        owner_kernel,
        out_shape=(table_like, table_like, change),
        compiler_params=params(),
        cost_estimate=cost(4 * 512 * 192 * 256, 1300000),
        name="owner",
    )(incoming, stale, table, accum)


def refresh(core, counts, cache_rows, change, done=None):
    flip = done is not None
    chips, span, width = change.shape
    step = chips // 2

    def half(i, core_ref):
        return (i, 1 - core_ref[0] if flip else core_ref[0], 0, 0)

    block = pl.BlockSpec((step, 1, span, width), half)
    in_specs = [
        pl.BlockSpec(counts.shape, lambda i, core_ref: (0, 0)),
        block,
        pl.BlockSpec((step, span, width), lambda i, core_ref: (i, 0, 0)),
    ]
    args = [core, counts, cache_rows.reshape(chips, 2, span, width), change]
    if flip:
        in_specs.append(pl.BlockSpec(memory_space=pl.ANY))
        args.append(done)

    def body(*refs):
        refresh_kernel(*refs, flip=flip)

    return pl.pallas_call(
        body,
        grid_spec=pltpu.PrefetchScalarGridSpec(
            num_scalar_prefetch=1, grid=(2,), in_specs=in_specs, out_specs=block
        ),
        out_shape=jax.ShapeDtypeStruct((chips, 2, span, width), jnp.float32),
        input_output_aliases={4: 0} if flip else {},
        compiler_params=params(),
        cost_estimate=pl.CostEstimate(flops=400000, bytes_accessed=2400000, transcendentals=0),
        name="refresh_other" if flip else "refresh_mine",
    )(*args)


def shards(
    cache, counts, hot_rows, lookups, bag_lengths, projection, grad_out, table, accum, stale
):
    n_own = hot_rows.shape[2]
    chips = lax.axis_size("y")
    capacity = hot_rows.shape[3]
    slots, width = cache.shape[1:]
    span = n_own * capacity
    lookup = lookups.reshape(LOOKUP_ROWS, 128)
    lengths = bag_lengths.reshape(LENGTH_ROWS, 128)
    core = lax.axis_index("core").astype(jnp.int32).reshape(1)
    swap = [(0, 1), (1, 0)]

    mine = pack(lookup, lengths, grad_out[0, 0], projection)
    other = lax.ppermute(mine, "core", swap)
    half = slot_sums(core, mine, chips, span)
    half = slot_sums(core, other, chips, span, half)
    half, late, hot_rows, stale = lax.optimization_barrier((half, mine, hot_rows, stale))
    parts = lax.all_to_all(half, "y", split_axis=0, concat_axis=0, tiled=True)
    ids = lax.dynamic_index_in_dim(hot_rows[0], lax.axis_index(GRP), 0, keepdims=False)
    ids = jnp.pad(ids.astype(jnp.float32), ((0, 0), (0, width - capacity)))
    projected = pool(late, cache[0], projection)
    parts, ids, stale, projected = lax.optimization_barrier((parts, ids, stale[0, 0], projected))
    summed = combine(parts, ids)
    summed = summed.reshape(-1, 1, width)
    incoming = lax.all_to_all(summed, OWN, split_axis=0, concat_axis=0, tiled=True)
    incoming = incoming.reshape(-1, width)
    table_new, accum_new, change = owner(incoming, stale, table[0, 0], accum[0, 0])

    returned = lax.all_to_all(
        change.reshape(n_own, capacity, width), OWN, split_axis=0, concat_axis=0, tiled=True
    )
    wide = jnp.broadcast_to(returned.reshape(1, span, width), (chips, span, width))
    near = lax.all_to_all(wide, "y", split_axis=0, concat_axis=0, tiled=True)
    far = lax.ppermute(near, "core", swap)
    refreshed = refresh(core, counts[0], cache[0], near)
    refreshed = refresh(core, counts[0], cache[0], far, done=refreshed)

    return (
        projected[None, None],
        table_new[None, None],
        accum_new[None, None],
        refreshed.reshape(1, slots, width),
    )


def solution(mesh):
    chips = Mesh(mesh.devices.reshape(4, 12, 8, 2), ("x", "z", "y", "core"))
    return jax.shard_map(
        shards,
        mesh=chips,
        in_specs=(
            P(OWN, None, None),
            P(OWN, None, None),
            P(OWN, None, None, None),
            P(OWN, GRP, None),
            P(OWN, GRP, None),
            P(),
            P(OWN, GRP, None, None),
            P(OWN, GRP, None, None),
            P(OWN, GRP, None, None),
            P(OWN, GRP, None, None),
        ),
        out_specs=(
            P(OWN, GRP, None, None),
            P(OWN, GRP, None, None),
            P(OWN, GRP, None, None),
            P(OWN, None, None),
        ),
        check_vma=False,
    )
```

```python
import functools

import jax
import jax.numpy as jnp
from jax import lax
from jax.experimental import pallas as pl
from jax.experimental.pallas import tpu as pltpu
from jax.sharding import Mesh
from jax.sharding import PartitionSpec as P

learn_rate = 0.3
epsilon = 1e-06
LOOKUP_ROWS = 16
LENGTH_ROWS = 2
OWN = ("x", "z")
GRP = ("y", "core")
STEP = 4
VMEM_BYTES = 40 * 1024 * 1024


def split(values):
    high = values.astype(jnp.bfloat16)
    low = (values - high.astype(jnp.float32)).astype(jnp.bfloat16)
    return jnp.concatenate([high, low], axis=1)


def joined(values):
    width = values.shape[1] // 2
    return values[:, :width] + values[:, width:]


def row_of(ref, first, count):
    return jnp.concatenate([ref[r : r + 1, :] for r in range(first, first + count)], axis=1)


def bag_hot(lengths):
    bags = lengths.shape[1]
    before = lax.broadcasted_iota(jnp.int32, (bags, bags), 0)
    after = lax.broadcasted_iota(jnp.int32, (bags, bags), 1)
    upper = jnp.where(before <= after, 1.0, 0.0).astype(jnp.bfloat16)
    tall = jnp.broadcast_to(lengths, (8, bags)).astype(jnp.bfloat16)
    ends = jnp.dot(tall, upper, preferred_element_type=jnp.float32)[0:1, :]
    starts = ends - lengths
    ends = ends.astype(jnp.int32)
    starts = starts.astype(jnp.int32)
    position = lax.broadcasted_iota(jnp.int32, (LOOKUP_ROWS * 128, bags), 0)
    inside = (position >= starts) & (position < ends)
    return jnp.where(inside, 1.0, 0.0).astype(jnp.bfloat16)


def slot_parts(lookup, span, groups):
    group = jnp.zeros_like(lookup)
    for k in range(1, groups):
        group = group + jnp.where(lookup >= k * span, 1, 0)
    place = lookup - group * span
    rows = lax.broadcasted_iota(jnp.int32, (span, lookup.shape[1]), 0)
    hot = jnp.where(rows == place, 1.0, 0.0).astype(jnp.bfloat16)
    return group, hot


def in_group(group, k):
    return jnp.where(group == k, 1.0, 0.0).astype(jnp.bfloat16)


def pack_kernel(lookup_hbm, length_hbm, cotangent_hbm, projection_hbm, out_ref, lookup, length, cotangent, projection, arrived):
    bags = cotangent.shape[0]
    sources = (lookup_hbm, length_hbm, cotangent_hbm, projection_hbm)
    copies = [
        pltpu.make_async_copy(source, target, arrived.at[i])
        for i, (source, target) in enumerate(zip(sources, (lookup, length, cotangent, projection)))
    ]
    for copy in copies:
        copy.start()
    for copy in copies:
        copy.wait()
    out_ref[:bags, :] = lax.dot_general(
        cotangent[...],
        projection[...],
        (((1,), (1,)), ((), ())),
        preferred_element_type=jnp.float32,
    )
    out_ref[bags : bags + LOOKUP_ROWS, :] = lookup[...].astype(jnp.float32)
    tail = jnp.zeros((8 - LENGTH_ROWS, 128), jnp.float32)
    out_ref[bags + LOOKUP_ROWS :, :] = jnp.concatenate(
        [length[...].astype(jnp.float32), tail], axis=0
    )


def unpack(packed_ref):
    bags = packed_ref.shape[0] - LOOKUP_ROWS - 8
    lookup = row_of(packed_ref, bags, LOOKUP_ROWS).astype(jnp.int32)
    return lookup, row_of(packed_ref, bags + LOOKUP_ROWS, LENGTH_ROWS)


def slot_kernel(core_ref, packed_ref, *refs):
    out_ref = refs[-1]
    chips, span, _ = out_ref.shape
    core = core_ref[0]
    lookup, lengths = unpack(packed_ref)
    bags = lengths.shape[1]
    rows = jnp.dot(
        bag_hot(lengths), split(packed_ref[:bags, :]), preferred_element_type=jnp.float32
    ).astype(jnp.bfloat16)
    group, hot = slot_parts(lookup, span, 2 * chips)
    for y in range(0, chips, STEP):
        slots = jnp.concatenate(
            [hot * in_group(group, 2 * j + core) for j in range(y, y + STEP)], axis=0
        )
        delta = joined(jnp.dot(slots, rows, preferred_element_type=jnp.float32))
        delta = delta.reshape(STEP, span, delta.shape[1])
        if len(refs) == 2:
            delta = delta + refs[0][y : y + STEP, :, :]
        out_ref[y : y + STEP, :, :] = delta


def pool_kernel(packed_ref, cache_ref, projection_ref, out_ref, count_ref):
    slots = cache_ref.shape[0]
    span = 192
    groups = slots // span
    lookup, lengths = unpack(packed_ref)
    bags = bag_hot(lengths)
    group, hot = slot_parts(lookup, span, groups)
    for k in range(0, groups, STEP):
        chosen = jnp.concatenate([hot * in_group(group, j) for j in range(k, k + STEP)], axis=0)
        count = jnp.dot(chosen, bags, preferred_element_type=jnp.float32)
        count_ref[k * span : (k + STEP) * span, :] = count.astype(jnp.bfloat16)
    pooled = lax.dot_general(
        count_ref[...],
        split(cache_ref[...]),
        (((0,), (0,)), ((), ())),
        preferred_element_type=jnp.float32,
    )
    pooled = joined(pooled).astype(jnp.bfloat16)
    out_ref[...] = jnp.dot(pooled, projection_ref[...], preferred_element_type=jnp.float32).astype(
        jnp.bfloat16
    )


def combine_kernel(parts_ref, ids_ref, out_ref):
    owners, _ = ids_ref.shape
    capacity = parts_ref.shape[1] // owners
    for c in range(capacity):
        rows = pl.ds(c, owners, stride=capacity)
        total = parts_ref[0, rows, :]
        for y in range(1, parts_ref.shape[0]):
            total = total + parts_ref[y, rows, :]
        out_ref[pl.ds(c, owners, stride=capacity + 1), :] = total
    out_ref[pl.ds(capacity, owners, stride=capacity + 1), :] = ids_ref[...]


def owner_kernel(
    incoming_ref, stale_ref, table_ref, accum_ref, table_new_ref, accum_new_ref, change_ref
):
    holders, capacity = stale_ref.shape
    table_rows = table_ref.shape[0]

    def taken(c):
        return incoming_ref[pl.ds(c, holders, stride=capacity + 1), :]

    ids = taken(capacity)[:, :capacity].astype(jnp.int32)
    stale = stale_ref[...].astype(jnp.float32)
    row = lax.broadcasted_iota(jnp.int32, (holders, table_rows), 1)
    hot = [jnp.where(row == ids[:, c : c + 1], 1.0, 0.0) for c in range(capacity)]
    wanted = [hot[c] * stale[:, c : c + 1] for c in range(capacity)]
    incoming = jnp.concatenate([taken(c) for c in range(capacity)], axis=0)
    gradient = joined(
        lax.dot_general(
            jnp.concatenate(hot, axis=0).astype(jnp.bfloat16),
            split(incoming),
            (((0,), (0,)), ((), ())),
            preferred_element_type=jnp.float32,
        )
    )
    accum_new = accum_ref[...] + gradient * gradient
    accum_new_ref[...] = accum_new
    old = table_ref[...]
    new = old - learn_rate * gradient / (jnp.sqrt(accum_new) + epsilon)
    table_new_ref[...] = new
    change = joined(
        jnp.dot(
            jnp.concatenate(wanted, axis=0).astype(jnp.bfloat16),
            split(new - old),
            preferred_element_type=jnp.float32,
        )
    )
    for c in range(capacity):
        change_ref[pl.ds(c, holders, stride=capacity), :] = change[
            c * holders : (c + 1) * holders, :
        ]


def spread_kernel(change_ref, counts_ref, out_ref):
    chips, span, width = out_ref.shape
    owners = counts_ref.shape[1]
    place = lax.broadcasted_iota(jnp.int32, (span, owners), 0) - (
        span // owners
    ) * lax.broadcasted_iota(jnp.int32, (span, owners), 1)
    live = jnp.where((place >= 0) & (place < counts_ref[...]), 1.0, 0.0).astype(jnp.bfloat16)
    live = jnp.dot(live, jnp.ones((owners, width), jnp.bfloat16), preferred_element_type=jnp.float32)
    change = jnp.where(live > 0.5, change_ref[...], 0.0)
    for y in range(chips):
        out_ref[y, :, :] = change


def store_kernel(*refs):
    count = len(refs) // 2
    sent = refs[-1]
    copies = [
        pltpu.make_async_copy(refs[i], refs[count + i], sent.at[i]) for i in range(count)
    ]
    for copy in copies:
        copy.start()
    for copy in copies:
        copy.wait()


def refresh_kernel(core_ref, cache_ref, change_ref, *refs, flip):
    out_hbm, ready, sent = refs[-3:]
    chips = change_ref.shape[0]
    core = 1 - core_ref[0] if flip else core_ref[0]
    copies = []
    for y in range(chips):
        ready[y, :, :] = cache_ref[y, core, :, :] + change_ref[y, :, :]
        copies.append(pltpu.make_async_copy(ready.at[y], out_hbm.at[y, core], sent.at[y]))
        copies[-1].start()
    for copy in copies:
        copy.wait()


def params():
    return pltpu.CompilerParams(vmem_limit_bytes=VMEM_BYTES)


def near_by(array):
    return pltpu.with_memory_space_constraint(array, pltpu.VMEM)


def cost(flops, moved):
    return pl.CostEstimate(flops=flops, bytes_accessed=moved, transcendentals=0)


def pack(lookup, lengths, cotangent, projection):
    rows = cotangent.shape[0] + LOOKUP_ROWS + 8
    given = (lookup, lengths, cotangent, projection)
    held = [pltpu.with_memory_space_constraint(a, pltpu.HBM) for a in given]
    return pl.pallas_call(
        pack_kernel,
        out_shape=pltpu.VMEM((rows, projection.shape[0]), jnp.float32),
        in_specs=[pl.BlockSpec(memory_space=pltpu.HBM)] * 4,
        out_specs=pl.BlockSpec(memory_space=pltpu.VMEM),
        scratch_shapes=[pltpu.VMEM(a.shape, a.dtype) for a in given]
        + [pltpu.SemaphoreType.DMA((4,))],
        compiler_params=params(),
        cost_estimate=cost(2 * 256 * 256 * 128, 400000),
        name="pack",
    )(*held)


def slot_sums(core, packed, chips, span, start=None):
    vmem = pl.BlockSpec(memory_space=pltpu.VMEM)
    args = [core] + [near_by(a) for a in ([packed] if start is None else [packed, start])]
    return pl.pallas_call(
        slot_kernel,
        out_shape=pltpu.VMEM((chips, span, packed.shape[1]), jnp.float32),
        in_specs=[pl.BlockSpec(memory_space=pltpu.SMEM)] + [vmem] * (len(args) - 1),
        out_specs=vmem,
        compiler_params=params(),
        cost_estimate=cost(3072 * 2048 * 256, 1000000),
        name="own_slots" if start is None else "all_slots",
    )(*args)


def pool(packed, cache_rows, projection):
    bags = packed.shape[0] - LOOKUP_ROWS - 8
    return pl.pallas_call(
        pool_kernel,
        out_shape=jax.ShapeDtypeStruct((bags, projection.shape[1]), jnp.bfloat16),
        scratch_shapes=[pltpu.VMEM((cache_rows.shape[0], bags), jnp.bfloat16)],
        compiler_params=params(),
        cost_estimate=cost(2 * 3072 * 2048 * 256, 2000000),
        name="pool",
    )(near_by(packed), near_by(cache_rows), projection)


def combine(parts, ids):
    chips, span, width = parts.shape
    return pl.pallas_call(
        combine_kernel,
        out_shape=pltpu.VMEM((span + ids.shape[0], width), jnp.float32),
        compiler_params=params(),
        cost_estimate=cost(200000, 900000),
        name="combine",
    )(near_by(parts), near_by(ids))


def owner(incoming, stale, table, accum):
    table_like = pltpu.VMEM(table.shape, jnp.float32)
    change = pltpu.VMEM((stale.size, table.shape[1]), jnp.float32)
    return pl.pallas_call(
        owner_kernel,
        out_shape=(table_like, table_like, change),
        compiler_params=params(),
        cost_estimate=cost(4 * 512 * 192 * 256, 1300000),
        name="owner",
    )(*[near_by(a) for a in (incoming, stale, table, accum)])


def store(*arrays):
    count = len(arrays)
    return pl.pallas_call(
        store_kernel,
        out_shape=tuple(pltpu.HBM(a.shape, a.dtype) for a in arrays),
        in_specs=[pl.BlockSpec(memory_space=pltpu.VMEM)] * count,
        out_specs=(pl.BlockSpec(memory_space=pltpu.HBM),) * count,
        scratch_shapes=[pltpu.SemaphoreType.DMA((count,))],
        compiler_params=params(),
        cost_estimate=cost(0, 2 * sum(4 * a.size for a in arrays)),
        name="store",
    )(*[near_by(a) for a in arrays])


def spread(change, counts, chips):
    return pl.pallas_call(
        spread_kernel,
        out_shape=pltpu.VMEM((chips,) + change.shape, jnp.float32),
        compiler_params=params(),
        cost_estimate=cost(10000000, 900000),
        name="spread",
    )(near_by(change), near_by(counts))


def refresh(core, cache_rows, change, done=None):
    flip = done is not None
    chips, span, width = change.shape
    vmem = pl.BlockSpec(memory_space=pltpu.VMEM)
    hbm = pl.BlockSpec(memory_space=pltpu.HBM)
    args = [core, near_by(cache_rows.reshape(chips, 2, span, width)), near_by(change)]
    args = args + ([done] if flip else [])
    return pl.pallas_call(
        functools.partial(refresh_kernel, flip=flip),
        out_shape=jax.ShapeDtypeStruct((chips, 2, span, width), jnp.float32),
        in_specs=[pl.BlockSpec(memory_space=pltpu.SMEM), vmem, vmem] + ([hbm] if flip else []),
        out_specs=hbm,
        scratch_shapes=[
            pltpu.VMEM((chips, span, width), jnp.float32),
            pltpu.SemaphoreType.DMA((chips,)),
        ],
        input_output_aliases={3: 0} if flip else {},
        compiler_params=params(),
        cost_estimate=cost(400000, 2400000),
        name="refresh_other" if flip else "refresh_mine",
    )(*args)


def shards(
    cache, counts, hot_rows, lookups, bag_lengths, projection, grad_out, table, accum, stale
):
    n_own = hot_rows.shape[2]
    chips = lax.axis_size("y")
    capacity = hot_rows.shape[3]
    slots, width = cache.shape[1:]
    span = n_own * capacity
    lookup = lookups.reshape(LOOKUP_ROWS, 128)
    lengths = bag_lengths.reshape(LENGTH_ROWS, 128)
    core = lax.axis_index("core").astype(jnp.int32).reshape(1)
    swap = [(0, 1), (1, 0)]

    mine = pack(lookup, lengths, grad_out[0, 0], projection)
    other = lax.ppermute(mine, "core", swap)
    half = slot_sums(core, mine, chips, span)
    half = slot_sums(core, other, chips, span, half)
    half, late, hot_rows, stale, counts = lax.optimization_barrier(
        (half, mine, hot_rows, stale, counts)
    )
    parts = lax.all_to_all(half, "y", split_axis=0, concat_axis=0, tiled=True)
    ids = lax.dynamic_index_in_dim(hot_rows[0], lax.axis_index(GRP), 0, keepdims=False)
    ids = jnp.pad(ids.astype(jnp.float32), ((0, 0), (0, width - capacity)))
    live = lax.dynamic_index_in_dim(counts[0], lax.axis_index(GRP), 0, keepdims=True)
    projected = pool(late, cache[0], projection)
    parts, ids, stale, live, projected = lax.optimization_barrier(
        (parts, ids, stale[0, 0], live, projected)
    )
    summed = combine(parts, ids)
    summed = summed.reshape(-1, 1, width)
    incoming = lax.all_to_all(summed, OWN, split_axis=0, concat_axis=0, tiled=True)
    incoming = incoming.reshape(-1, width)
    table_new, accum_new, change = owner(incoming, stale, table[0, 0], accum[0, 0])

    returned = lax.all_to_all(
        change.reshape(n_own, capacity, width), OWN, split_axis=0, concat_axis=0, tiled=True
    )
    table_new, accum_new = store(table_new, accum_new)
    returned, table_new, accum_new = lax.optimization_barrier((returned, table_new, accum_new))
    wide = spread(returned.reshape(span, width), live, chips)
    near = lax.all_to_all(wide, "y", split_axis=0, concat_axis=0, tiled=True)
    far = lax.ppermute(near, "core", swap)
    refreshed = refresh(core, cache[0], near)
    refreshed = refresh(core, cache[0], far, done=refreshed)

    return (
        projected[None, None],
        table_new[None, None],
        accum_new[None, None],
        refreshed.reshape(1, slots, width),
    )


def solution(mesh):
    chips = Mesh(mesh.devices.reshape(4, 12, 8, 2), ("x", "z", "y", "core"))
    return jax.shard_map(
        shards,
        mesh=chips,
        in_specs=(
            P(OWN, None, None),
            P(OWN, None, None),
            P(OWN, None, None, None),
            P(OWN, GRP, None),
            P(OWN, GRP, None),
            P(),
            P(OWN, GRP, None, None),
            P(OWN, GRP, None, None),
            P(OWN, GRP, None, None),
            P(OWN, GRP, None, None),
        ),
        out_specs=(
            P(OWN, GRP, None, None),
            P(OWN, GRP, None, None),
            P(OWN, GRP, None, None),
            P(OWN, None, None),
        ),
        check_vma=False,
    )
```

```python
import functools

import jax
import jax.numpy as jnp
from jax import lax
from jax.experimental import pallas as pl
from jax.experimental.pallas import tpu as pltpu
from jax.sharding import Mesh
from jax.sharding import PartitionSpec as P

learn_rate = 0.3
epsilon = 1e-06
LOOKUP_ROWS = 16
LENGTH_ROWS = 2
OWN = ("x", "z")
GRP = ("y", "core")
STEP = 4
COPIES = 4
VMEM_BYTES = 40 * 1024 * 1024


def split(values):
    high = values.astype(jnp.bfloat16)
    low = (values - high.astype(jnp.float32)).astype(jnp.bfloat16)
    return jnp.concatenate([high, low], axis=1)


def joined(values):
    width = values.shape[1] // 2
    return values[:, :width] + values[:, width:]


def row_of(ref, first, count):
    return jnp.concatenate([ref[r : r + 1, :] for r in range(first, first + count)], axis=1)


def bag_hot(lengths):
    bags = lengths.shape[1]
    before = lax.broadcasted_iota(jnp.int32, (bags, bags), 0)
    after = lax.broadcasted_iota(jnp.int32, (bags, bags), 1)
    upper = jnp.where(before <= after, 1.0, 0.0).astype(jnp.bfloat16)
    tall = jnp.broadcast_to(lengths, (8, bags)).astype(jnp.bfloat16)
    ends = jnp.dot(tall, upper, preferred_element_type=jnp.float32)[0:1, :]
    starts = ends - lengths
    ends = ends.astype(jnp.int32)
    starts = starts.astype(jnp.int32)
    position = lax.broadcasted_iota(jnp.int32, (LOOKUP_ROWS * 128, bags), 0)
    inside = (position >= starts) & (position < ends)
    return jnp.where(inside, 1.0, 0.0).astype(jnp.bfloat16)


def slot_parts(lookup, span, groups):
    group = jnp.zeros_like(lookup)
    for k in range(1, groups):
        group = group + jnp.where(lookup >= k * span, 1, 0)
    place = lookup - group * span
    rows = lax.broadcasted_iota(jnp.int32, (span, lookup.shape[1]), 0)
    hot = jnp.where(rows == place, 1.0, 0.0).astype(jnp.bfloat16)
    return group, hot


def in_group(group, k):
    return jnp.where(group == k, 1.0, 0.0).astype(jnp.bfloat16)


def pack_kernel(lookup_hbm, length_hbm, cotangent_hbm, projection_hbm, out_ref, lookup, length, cotangent, projection, arrived):
    bags = cotangent.shape[0]
    sources = (lookup_hbm, length_hbm, cotangent_hbm, projection_hbm)
    copies = [
        pltpu.make_async_copy(source, target, arrived.at[i])
        for i, (source, target) in enumerate(zip(sources, (lookup, length, cotangent, projection)))
    ]
    for copy in copies:
        copy.start()
    for copy in copies:
        copy.wait()
    out_ref[:bags, :] = lax.dot_general(
        cotangent[...],
        projection[...],
        (((1,), (1,)), ((), ())),
        preferred_element_type=jnp.float32,
    )
    out_ref[bags : bags + LOOKUP_ROWS, :] = lookup[...].astype(jnp.float32)
    tail = jnp.zeros((8 - LENGTH_ROWS, 128), jnp.float32)
    out_ref[bags + LOOKUP_ROWS :, :] = jnp.concatenate(
        [length[...].astype(jnp.float32), tail], axis=0
    )


def unpack(packed_ref):
    bags = packed_ref.shape[0] - LOOKUP_ROWS - 8
    lookup = row_of(packed_ref, bags, LOOKUP_ROWS).astype(jnp.int32)
    return lookup, row_of(packed_ref, bags + LOOKUP_ROWS, LENGTH_ROWS)


def slot_parts_of(core_ref, packed_ref, chips, span, step):
    core = core_ref[0]
    lookup, lengths = unpack(packed_ref)
    bags = lengths.shape[1]
    rows = jnp.dot(
        bag_hot(lengths), split(packed_ref[:bags, :]), preferred_element_type=jnp.float32
    ).astype(jnp.bfloat16)
    group, hot = slot_parts(lookup, span, 2 * chips)
    for y in range(0, chips, step):
        slots = jnp.concatenate(
            [hot * in_group(group, 2 * j + core) for j in range(y, y + step)], axis=0
        )
        delta = joined(jnp.dot(slots, rows, preferred_element_type=jnp.float32))
        yield pl.ds(y, step), delta.reshape(step, span, delta.shape[1])


def own_kernel(core_ref, packed_ref, out_ref):
    chips, span, _ = out_ref.shape
    for place, delta in slot_parts_of(core_ref, packed_ref, chips, span, STEP):
        out_ref[place, :, :] = delta


def both_kernel(core_ref, packed_ref, start_ref, out_hbm, ready, sent):
    chips, span, _ = start_ref.shape
    copies = []
    for place, delta in slot_parts_of(core_ref, packed_ref, chips, span, chips // COPIES):
        ready[place, :, :] = start_ref[place, :, :] + delta
        copy = pltpu.make_async_copy(ready.at[place], out_hbm.at[place], sent.at[len(copies)])
        copy.start()
        copies.append(copy)
    for copy in copies:
        copy.wait()


def pool_kernel(packed_ref, cache_ref, projection_ref, out_ref, count_ref):
    slots = cache_ref.shape[0]
    span = 192
    groups = slots // span
    lookup, lengths = unpack(packed_ref)
    bags = bag_hot(lengths)
    group, hot = slot_parts(lookup, span, groups)
    for k in range(0, groups, STEP):
        chosen = jnp.concatenate([hot * in_group(group, j) for j in range(k, k + STEP)], axis=0)
        count = jnp.dot(chosen, bags, preferred_element_type=jnp.float32)
        count_ref[k * span : (k + STEP) * span, :] = count.astype(jnp.bfloat16)
    pooled = lax.dot_general(
        count_ref[...],
        split(cache_ref[...]),
        (((0,), (0,)), ((), ())),
        preferred_element_type=jnp.float32,
    )
    pooled = joined(pooled).astype(jnp.bfloat16)
    out_ref[...] = jnp.dot(pooled, projection_ref[...], preferred_element_type=jnp.float32).astype(
        jnp.bfloat16
    )


def combine_kernel(parts_ref, ids_ref, out_ref):
    owners, _ = ids_ref.shape
    capacity = parts_ref.shape[1] // owners
    for c in range(capacity):
        rows = pl.ds(c, owners, stride=capacity)
        total = parts_ref[0, rows, :]
        for y in range(1, parts_ref.shape[0]):
            total = total + parts_ref[y, rows, :]
        out_ref[pl.ds(c, owners, stride=capacity + 1), :] = total
    out_ref[pl.ds(capacity, owners, stride=capacity + 1), :] = ids_ref[...]


def owner_kernel(
    incoming_ref, stale_ref, table_ref, accum_ref, table_new_ref, accum_new_ref, change_ref
):
    holders, capacity = stale_ref.shape
    table_rows = table_ref.shape[0]

    def taken(c):
        return incoming_ref[pl.ds(c, holders, stride=capacity + 1), :]

    ids = taken(capacity)[:, :capacity].astype(jnp.int32)
    stale = stale_ref[...].astype(jnp.float32)
    row = lax.broadcasted_iota(jnp.int32, (holders, table_rows), 1)
    hot = [jnp.where(row == ids[:, c : c + 1], 1.0, 0.0) for c in range(capacity)]
    wanted = [hot[c] * stale[:, c : c + 1] for c in range(capacity)]
    incoming = jnp.concatenate([taken(c) for c in range(capacity)], axis=0)
    gradient = joined(
        lax.dot_general(
            jnp.concatenate(hot, axis=0).astype(jnp.bfloat16),
            split(incoming),
            (((0,), (0,)), ((), ())),
            preferred_element_type=jnp.float32,
        )
    )
    accum_new = accum_ref[...] + gradient * gradient
    accum_new_ref[...] = accum_new
    old = table_ref[...]
    new = old - learn_rate * gradient / (jnp.sqrt(accum_new) + epsilon)
    table_new_ref[...] = new
    change = joined(
        jnp.dot(
            jnp.concatenate(wanted, axis=0).astype(jnp.bfloat16),
            split(new - old),
            preferred_element_type=jnp.float32,
        )
    )
    for c in range(capacity):
        change_ref[pl.ds(c, holders, stride=capacity), :] = change[
            c * holders : (c + 1) * holders, :
        ]


def spread_kernel(change_ref, counts_ref, out_ref):
    chips, span, width = out_ref.shape
    owners = counts_ref.shape[1]
    place = lax.broadcasted_iota(jnp.int32, (span, owners), 0) - (
        span // owners
    ) * lax.broadcasted_iota(jnp.int32, (span, owners), 1)
    live = jnp.where((place >= 0) & (place < counts_ref[...]), 1.0, 0.0).astype(jnp.bfloat16)
    live = jnp.dot(live, jnp.ones((owners, width), jnp.bfloat16), preferred_element_type=jnp.float32)
    change = jnp.where(live > 0.5, change_ref[...], 0.0)
    for y in range(chips):
        out_ref[y, :, :] = change


def store_kernel(*refs):
    count = len(refs) // 2
    sent = refs[-1]
    copies = [
        pltpu.make_async_copy(refs[i], refs[count + i], sent.at[i]) for i in range(count)
    ]
    for copy in copies:
        copy.start()
    for copy in copies:
        copy.wait()


def refresh_kernel(core_ref, cache_ref, change_ref, *refs, flip):
    out_hbm, ready, sent = refs[-3:]
    chips = change_ref.shape[0]
    core = 1 - core_ref[0] if flip else core_ref[0]
    copies = []
    for y in range(chips):
        ready[y, :, :] = cache_ref[y, core, :, :] + change_ref[y, :, :]
        copies.append(pltpu.make_async_copy(ready.at[y], out_hbm.at[y, core], sent.at[y]))
        copies[-1].start()
    for copy in copies:
        copy.wait()


def params():
    return pltpu.CompilerParams(vmem_limit_bytes=VMEM_BYTES)


def near_by(array):
    return pltpu.with_memory_space_constraint(array, pltpu.VMEM)


def cost(flops, moved):
    return pl.CostEstimate(flops=flops, bytes_accessed=moved, transcendentals=0)


def pack(lookup, lengths, cotangent, projection):
    rows = cotangent.shape[0] + LOOKUP_ROWS + 8
    given = (lookup, lengths, cotangent, projection)
    held = [pltpu.with_memory_space_constraint(a, pltpu.HBM) for a in given]
    return pl.pallas_call(
        pack_kernel,
        out_shape=pltpu.VMEM((rows, projection.shape[0]), jnp.float32),
        in_specs=[pl.BlockSpec(memory_space=pltpu.HBM)] * 4,
        out_specs=pl.BlockSpec(memory_space=pltpu.VMEM),
        scratch_shapes=[pltpu.VMEM(a.shape, a.dtype) for a in given]
        + [pltpu.SemaphoreType.DMA((4,))],
        compiler_params=params(),
        cost_estimate=cost(2 * 256 * 256 * 128, 400000),
        name="pack",
    )(*held)


def own_slots(core, packed, chips, span):
    vmem = pl.BlockSpec(memory_space=pltpu.VMEM)
    return pl.pallas_call(
        own_kernel,
        out_shape=pltpu.VMEM((chips, span, packed.shape[1]), jnp.float32),
        in_specs=[pl.BlockSpec(memory_space=pltpu.SMEM), vmem],
        out_specs=vmem,
        compiler_params=params(),
        cost_estimate=cost(3072 * 2048 * 256, 1000000),
        name="own_slots",
    )(core, near_by(packed))


def both_slots(core, packed, start):
    vmem = pl.BlockSpec(memory_space=pltpu.VMEM)
    return pl.pallas_call(
        both_kernel,
        out_shape=pltpu.HBM(start.shape, jnp.float32),
        in_specs=[pl.BlockSpec(memory_space=pltpu.SMEM), vmem, vmem],
        out_specs=pl.BlockSpec(memory_space=pltpu.HBM),
        scratch_shapes=[pltpu.VMEM(start.shape, jnp.float32), pltpu.SemaphoreType.DMA((COPIES,))],
        compiler_params=params(),
        cost_estimate=cost(3072 * 2048 * 256, 1800000),
        name="both_slots",
    )(core, near_by(packed), near_by(start))


def pool(packed, cache_rows, projection):
    bags = packed.shape[0] - LOOKUP_ROWS - 8
    return pl.pallas_call(
        pool_kernel,
        out_shape=jax.ShapeDtypeStruct((bags, projection.shape[1]), jnp.bfloat16),
        scratch_shapes=[pltpu.VMEM((cache_rows.shape[0], bags), jnp.bfloat16)],
        compiler_params=params(),
        cost_estimate=cost(2 * 3072 * 2048 * 256, 2000000),
        name="pool",
    )(near_by(packed), near_by(cache_rows), projection)


def combine(parts, ids):
    chips, span, width = parts.shape
    return pl.pallas_call(
        combine_kernel,
        out_shape=pltpu.VMEM((span + ids.shape[0], width), jnp.float32),
        compiler_params=params(),
        cost_estimate=cost(200000, 900000),
        name="combine",
    )(near_by(parts), near_by(ids))


def owner(incoming, stale, table, accum):
    table_like = pltpu.VMEM(table.shape, jnp.float32)
    change = pltpu.VMEM((stale.size, table.shape[1]), jnp.float32)
    return pl.pallas_call(
        owner_kernel,
        out_shape=(table_like, table_like, change),
        compiler_params=params(),
        cost_estimate=cost(4 * 512 * 192 * 256, 1300000),
        name="owner",
    )(*[near_by(a) for a in (incoming, stale, table, accum)])


def store(*arrays):
    count = len(arrays)
    return pl.pallas_call(
        store_kernel,
        out_shape=tuple(pltpu.HBM(a.shape, a.dtype) for a in arrays),
        in_specs=[pl.BlockSpec(memory_space=pltpu.VMEM)] * count,
        out_specs=(pl.BlockSpec(memory_space=pltpu.HBM),) * count,
        scratch_shapes=[pltpu.SemaphoreType.DMA((count,))],
        compiler_params=params(),
        cost_estimate=cost(0, 2 * sum(4 * a.size for a in arrays)),
        name="store",
    )(*[near_by(a) for a in arrays])


def spread(change, counts, chips):
    return pl.pallas_call(
        spread_kernel,
        out_shape=pltpu.VMEM((chips,) + change.shape, jnp.float32),
        compiler_params=params(),
        cost_estimate=cost(10000000, 900000),
        name="spread",
    )(near_by(change), near_by(counts))


def refresh(core, cache_rows, change, done=None):
    flip = done is not None
    chips, span, width = change.shape
    vmem = pl.BlockSpec(memory_space=pltpu.VMEM)
    hbm = pl.BlockSpec(memory_space=pltpu.HBM)
    args = [core, near_by(cache_rows.reshape(chips, 2, span, width)), near_by(change)]
    args = args + ([done] if flip else [])
    return pl.pallas_call(
        functools.partial(refresh_kernel, flip=flip),
        out_shape=jax.ShapeDtypeStruct((chips, 2, span, width), jnp.float32),
        in_specs=[pl.BlockSpec(memory_space=pltpu.SMEM), vmem, vmem] + ([hbm] if flip else []),
        out_specs=hbm,
        scratch_shapes=[
            pltpu.VMEM((chips, span, width), jnp.float32),
            pltpu.SemaphoreType.DMA((chips,)),
        ],
        input_output_aliases={3: 0} if flip else {},
        compiler_params=params(),
        cost_estimate=cost(400000, 2400000),
        name="refresh_other" if flip else "refresh_mine",
    )(*args)


def shards(
    cache, counts, hot_rows, lookups, bag_lengths, projection, grad_out, table, accum, stale
):
    n_own = hot_rows.shape[2]
    chips = lax.axis_size("y")
    capacity = hot_rows.shape[3]
    slots, width = cache.shape[1:]
    span = n_own * capacity
    lookup = lookups.reshape(LOOKUP_ROWS, 128)
    lengths = bag_lengths.reshape(LENGTH_ROWS, 128)
    core = lax.axis_index("core").astype(jnp.int32).reshape(1)
    swap = [(0, 1), (1, 0)]

    mine = pack(lookup, lengths, grad_out[0, 0], projection)
    other = lax.ppermute(mine, "core", swap)
    half = both_slots(core, other, own_slots(core, mine, chips, span))
    half, late, hot_rows, stale, counts = lax.optimization_barrier(
        (half, mine, hot_rows, stale, counts)
    )
    parts = lax.all_to_all(half, "y", split_axis=0, concat_axis=0, tiled=True)
    ids = lax.dynamic_index_in_dim(hot_rows[0], lax.axis_index(GRP), 0, keepdims=False)
    ids = jnp.pad(ids.astype(jnp.float32), ((0, 0), (0, width - capacity)))
    live = lax.dynamic_index_in_dim(counts[0], lax.axis_index(GRP), 0, keepdims=True)
    projected = pool(late, cache[0], projection)
    parts, ids, stale, live, projected = lax.optimization_barrier(
        (parts, ids, stale[0, 0], live, projected)
    )
    summed = combine(parts, ids)
    summed = summed.reshape(-1, 1, width)
    incoming = lax.all_to_all(summed, OWN, split_axis=0, concat_axis=0, tiled=True)
    incoming = incoming.reshape(-1, width)
    table_new, accum_new, change = owner(incoming, stale, table[0, 0], accum[0, 0])

    returned = lax.all_to_all(
        change.reshape(n_own, capacity, width), OWN, split_axis=0, concat_axis=0, tiled=True
    )
    wide = spread(returned.reshape(span, width), live, chips)
    near = lax.all_to_all(wide, "y", split_axis=0, concat_axis=0, tiled=True)
    far = lax.ppermute(near, "core", swap)
    near, table_new, accum_new = lax.optimization_barrier((near, table_new, accum_new))
    table_new, accum_new = store(table_new, accum_new)
    refreshed = refresh(core, cache[0], near)
    far, table_new, accum_new = lax.optimization_barrier((far, table_new, accum_new))
    refreshed = refresh(core, cache[0], far, done=refreshed)

    return (
        projected[None, None],
        table_new[None, None],
        accum_new[None, None],
        refreshed.reshape(1, slots, width),
    )


def solution(mesh):
    chips = Mesh(mesh.devices.reshape(4, 12, 8, 2), ("x", "z", "y", "core"))
    return jax.shard_map(
        shards,
        mesh=chips,
        in_specs=(
            P(OWN, None, None),
            P(OWN, None, None),
            P(OWN, None, None, None),
            P(OWN, GRP, None),
            P(OWN, GRP, None),
            P(),
            P(OWN, GRP, None, None),
            P(OWN, GRP, None, None),
            P(OWN, GRP, None, None),
            P(OWN, GRP, None, None),
        ),
        out_specs=(
            P(OWN, GRP, None, None),
            P(OWN, GRP, None, None),
            P(OWN, GRP, None, None),
            P(OWN, None, None),
        ),
        check_vma=False,
    )
```

```python
import functools

import jax
import jax.numpy as jnp
from jax import lax
from jax.experimental import pallas as pl
from jax.experimental.pallas import tpu as pltpu
from jax.sharding import Mesh
from jax.sharding import PartitionSpec as P

learn_rate = 0.3
epsilon = 1e-06
LOOKUP_ROWS = 16
LENGTH_ROWS = 2
OWN = ("x", "z")
GRP = ("y", "core")
STEP = 4
VMEM_BYTES = 40 * 1024 * 1024


def split(values):
    high = values.astype(jnp.bfloat16)
    low = (values - high.astype(jnp.float32)).astype(jnp.bfloat16)
    return jnp.concatenate([high, low], axis=1)


def joined(values):
    width = values.shape[1] // 2
    return values[:, :width] + values[:, width:]


def row_of(ref, first, count):
    return jnp.concatenate([ref[r : r + 1, :] for r in range(first, first + count)], axis=1)


def bag_hot(lengths):
    bags = lengths.shape[1]
    before = lax.broadcasted_iota(jnp.int32, (bags, bags), 0)
    after = lax.broadcasted_iota(jnp.int32, (bags, bags), 1)
    upper = jnp.where(before <= after, 1.0, 0.0).astype(jnp.bfloat16)
    tall = jnp.broadcast_to(lengths, (8, bags)).astype(jnp.bfloat16)
    ends = jnp.dot(tall, upper, preferred_element_type=jnp.float32)[0:1, :]
    starts = ends - lengths
    ends = ends.astype(jnp.int32)
    starts = starts.astype(jnp.int32)
    position = lax.broadcasted_iota(jnp.int32, (LOOKUP_ROWS * 128, bags), 0)
    inside = (position >= starts) & (position < ends)
    return jnp.where(inside, 1.0, 0.0).astype(jnp.bfloat16)


def slot_parts(lookup, span, groups):
    group = jnp.zeros_like(lookup)
    for k in range(1, groups):
        group = group + jnp.where(lookup >= k * span, 1, 0)
    place = lookup - group * span
    rows = lax.broadcasted_iota(jnp.int32, (span, lookup.shape[1]), 0)
    hot = jnp.where(rows == place, 1.0, 0.0).astype(jnp.bfloat16)
    return group, hot


def in_group(group, k):
    return jnp.where(group == k, 1.0, 0.0).astype(jnp.bfloat16)


def pack_kernel(lookup_hbm, length_hbm, cotangent_hbm, projection_hbm, out_ref, lookup, length, cotangent, projection, arrived):
    bags = cotangent.shape[0]
    sources = (lookup_hbm, length_hbm, cotangent_hbm, projection_hbm)
    copies = [
        pltpu.make_async_copy(source, target, arrived.at[i])
        for i, (source, target) in enumerate(zip(sources, (lookup, length, cotangent, projection)))
    ]
    for copy in copies:
        copy.start()
    for copy in copies:
        copy.wait()
    out_ref[:bags, :] = lax.dot_general(
        cotangent[...],
        projection[...],
        (((1,), (1,)), ((), ())),
        preferred_element_type=jnp.float32,
    )
    out_ref[bags : bags + LOOKUP_ROWS, :] = lookup[...].astype(jnp.float32)
    tail = jnp.zeros((8 - LENGTH_ROWS, 128), jnp.float32)
    out_ref[bags + LOOKUP_ROWS :, :] = jnp.concatenate(
        [length[...].astype(jnp.float32), tail], axis=0
    )


def unpack(packed_ref):
    bags = packed_ref.shape[0] - LOOKUP_ROWS - 8
    lookup = row_of(packed_ref, bags, LOOKUP_ROWS).astype(jnp.int32)
    return lookup, row_of(packed_ref, bags + LOOKUP_ROWS, LENGTH_ROWS)


def slot_parts_of(core_ref, packed_ref, chips, span, step):
    core = core_ref[0]
    lookup, lengths = unpack(packed_ref)
    bags = lengths.shape[1]
    rows = jnp.dot(
        bag_hot(lengths), split(packed_ref[:bags, :]), preferred_element_type=jnp.float32
    ).astype(jnp.bfloat16)
    group, hot = slot_parts(lookup, span, 2 * chips)
    for y in range(0, chips, step):
        slots = jnp.concatenate(
            [hot * in_group(group, 2 * j + core) for j in range(y, y + step)], axis=0
        )
        delta = joined(jnp.dot(slots, rows, preferred_element_type=jnp.float32))
        yield pl.ds(y, step), delta.reshape(step, span, delta.shape[1])


def own_kernel(core_ref, packed_ref, out_ref):
    chips, span, _ = out_ref.shape
    for place, delta in slot_parts_of(core_ref, packed_ref, chips, span, STEP):
        out_ref[place, :, :] = delta


def both_kernel(core_ref, packed_ref, start_ref, out_ref):
    chips, span, _ = out_ref.shape
    for place, delta in slot_parts_of(core_ref, packed_ref, chips, span, STEP):
        out_ref[place, :, :] = start_ref[place, :, :] + delta


def pool_kernel(core_ref, packed_ref, cache_ref, projection_ref, *refs, turn):
    out_hbm, count_ref, ready, sent = refs[-4:]

    @pl.when(core_ref[0] == turn)
    def _():
        slots = cache_ref.shape[0]
        span = 192
        groups = slots // span
        lookup, lengths = unpack(packed_ref)
        bags = bag_hot(lengths)
        group, hot = slot_parts(lookup, span, groups)
        for k in range(0, groups, STEP):
            chosen = jnp.concatenate([hot * in_group(group, j) for j in range(k, k + STEP)], axis=0)
            count = jnp.dot(chosen, bags, preferred_element_type=jnp.float32)
            count_ref[k * span : (k + STEP) * span, :] = count.astype(jnp.bfloat16)
        pooled = lax.dot_general(
            count_ref[...],
            split(cache_ref[...]),
            (((0,), (0,)), ((), ())),
            preferred_element_type=jnp.float32,
        )
        pooled = joined(pooled).astype(jnp.bfloat16)
        ready[...] = jnp.dot(
            pooled, projection_ref[...], preferred_element_type=jnp.float32
        ).astype(jnp.bfloat16)
        copy = pltpu.make_async_copy(ready, out_hbm, sent.at[0])
        copy.start()
        copy.wait()


def combine_kernel(parts_ref, ids_ref, out_ref):
    owners, _ = ids_ref.shape
    capacity = parts_ref.shape[1] // owners
    for c in range(capacity):
        rows = pl.ds(c, owners, stride=capacity)
        total = parts_ref[0, rows, :]
        for y in range(1, parts_ref.shape[0]):
            total = total + parts_ref[y, rows, :]
        out_ref[pl.ds(c, owners, stride=capacity + 1), :] = total
    out_ref[pl.ds(capacity, owners, stride=capacity + 1), :] = ids_ref[...]


def owner_kernel(
    incoming_ref, stale_ref, table_ref, accum_ref, table_new_ref, accum_new_ref, change_ref
):
    holders, capacity = stale_ref.shape
    table_rows = table_ref.shape[0]

    def taken(c):
        return incoming_ref[pl.ds(c, holders, stride=capacity + 1), :]

    ids = taken(capacity)[:, :capacity].astype(jnp.int32)
    stale = stale_ref[...].astype(jnp.float32)
    row = lax.broadcasted_iota(jnp.int32, (holders, table_rows), 1)
    hot = [jnp.where(row == ids[:, c : c + 1], 1.0, 0.0) for c in range(capacity)]
    wanted = [hot[c] * stale[:, c : c + 1] for c in range(capacity)]
    incoming = jnp.concatenate([taken(c) for c in range(capacity)], axis=0)
    gradient = joined(
        lax.dot_general(
            jnp.concatenate(hot, axis=0).astype(jnp.bfloat16),
            split(incoming),
            (((0,), (0,)), ((), ())),
            preferred_element_type=jnp.float32,
        )
    )
    accum_new = accum_ref[...] + gradient * gradient
    accum_new_ref[...] = accum_new
    old = table_ref[...]
    new = old - learn_rate * gradient / (jnp.sqrt(accum_new) + epsilon)
    table_new_ref[...] = new
    change = joined(
        jnp.dot(
            jnp.concatenate(wanted, axis=0).astype(jnp.bfloat16),
            split(new - old),
            preferred_element_type=jnp.float32,
        )
    )
    for c in range(capacity):
        change_ref[pl.ds(c, holders, stride=capacity), :] = change[
            c * holders : (c + 1) * holders, :
        ]


def spread_kernel(change_ref, counts_ref, out_ref):
    chips, span, width = out_ref.shape
    owners = counts_ref.shape[1]
    place = lax.broadcasted_iota(jnp.int32, (span, owners), 0) - (
        span // owners
    ) * lax.broadcasted_iota(jnp.int32, (span, owners), 1)
    live = jnp.where((place >= 0) & (place < counts_ref[...]), 1.0, 0.0).astype(jnp.bfloat16)
    live = jnp.dot(live, jnp.ones((owners, width), jnp.bfloat16), preferred_element_type=jnp.float32)
    change = jnp.where(live > 0.5, change_ref[...], 0.0)
    for y in range(chips):
        out_ref[y, :, :] = change


def store_kernel(*refs):
    count = len(refs) // 2
    sent = refs[-1]
    copies = [
        pltpu.make_async_copy(refs[i], refs[count + i], sent.at[i]) for i in range(count)
    ]
    for copy in copies:
        copy.start()
    for copy in copies:
        copy.wait()


def refresh_kernel(core_ref, cache_ref, change_ref, *refs, flip):
    out_hbm, ready, sent = refs[-3:]
    chips = change_ref.shape[0]
    core = 1 - core_ref[0] if flip else core_ref[0]
    copies = []
    for y in range(chips):
        ready[y, :, :] = cache_ref[y, core, :, :] + change_ref[y, :, :]
        copies.append(pltpu.make_async_copy(ready.at[y], out_hbm.at[y, core], sent.at[y]))
        copies[-1].start()
    for copy in copies:
        copy.wait()


def params():
    return pltpu.CompilerParams(vmem_limit_bytes=VMEM_BYTES)


def near_by(array):
    return pltpu.with_memory_space_constraint(array, pltpu.VMEM)


def cost(flops, moved):
    return pl.CostEstimate(flops=flops, bytes_accessed=moved, transcendentals=0)


def pack(lookup, lengths, cotangent, projection):
    rows = cotangent.shape[0] + LOOKUP_ROWS + 8
    given = (lookup, lengths, cotangent, projection)
    held = [pltpu.with_memory_space_constraint(a, pltpu.HBM) for a in given]
    return pl.pallas_call(
        pack_kernel,
        out_shape=pltpu.VMEM((rows, projection.shape[0]), jnp.float32),
        in_specs=[pl.BlockSpec(memory_space=pltpu.HBM)] * 4,
        out_specs=pl.BlockSpec(memory_space=pltpu.VMEM),
        scratch_shapes=[pltpu.VMEM(a.shape, a.dtype) for a in given]
        + [pltpu.SemaphoreType.DMA((4,))],
        compiler_params=params(),
        cost_estimate=cost(2 * 256 * 256 * 128, 400000),
        name="pack",
    )(*held)


def own_slots(core, packed, chips, span):
    vmem = pl.BlockSpec(memory_space=pltpu.VMEM)
    return pl.pallas_call(
        own_kernel,
        out_shape=pltpu.VMEM((chips, span, packed.shape[1]), jnp.float32),
        in_specs=[pl.BlockSpec(memory_space=pltpu.SMEM), vmem],
        out_specs=vmem,
        compiler_params=params(),
        cost_estimate=cost(3072 * 2048 * 256, 1000000),
        name="own_slots",
    )(core, near_by(packed))


def both_slots(core, packed, start):
    vmem = pl.BlockSpec(memory_space=pltpu.VMEM)
    return pl.pallas_call(
        both_kernel,
        out_shape=pltpu.VMEM(start.shape, jnp.float32),
        in_specs=[pl.BlockSpec(memory_space=pltpu.SMEM), vmem, vmem],
        out_specs=vmem,
        compiler_params=params(),
        cost_estimate=cost(3072 * 2048 * 256, 1800000),
        name="both_slots",
    )(core, near_by(packed), near_by(start))


def pool(core, packed, cache_rows, projection, turn, done=None):
    bags = packed.shape[0] - LOOKUP_ROWS - 8
    vmem = pl.BlockSpec(memory_space=pltpu.VMEM)
    hbm = pl.BlockSpec(memory_space=pltpu.HBM)
    more = [] if done is None else [done]
    return pl.pallas_call(
        functools.partial(pool_kernel, turn=turn),
        out_shape=pltpu.HBM((bags, projection.shape[1]), jnp.bfloat16),
        in_specs=[pl.BlockSpec(memory_space=pltpu.SMEM), vmem, vmem, vmem] + [hbm] * len(more),
        out_specs=hbm,
        scratch_shapes=[
            pltpu.VMEM((cache_rows.shape[0], bags), jnp.bfloat16),
            pltpu.VMEM((bags, projection.shape[1]), jnp.bfloat16),
            pltpu.SemaphoreType.DMA((1,)),
        ],
        input_output_aliases={4: 0} if more else {},
        compiler_params=params(),
        cost_estimate=cost(2 * 3072 * 2048 * 256, 2000000),
        name="pool_late" if more else "pool_early",
    )(core, near_by(packed), near_by(cache_rows), near_by(projection), *more)


def combine(parts, ids):
    chips, span, width = parts.shape
    return pl.pallas_call(
        combine_kernel,
        out_shape=pltpu.VMEM((span + ids.shape[0], width), jnp.float32),
        compiler_params=params(),
        cost_estimate=cost(200000, 900000),
        name="combine",
    )(near_by(parts), near_by(ids))


def owner(incoming, stale, table, accum):
    table_like = pltpu.VMEM(table.shape, jnp.float32)
    change = pltpu.VMEM((stale.size, table.shape[1]), jnp.float32)
    return pl.pallas_call(
        owner_kernel,
        out_shape=(table_like, table_like, change),
        compiler_params=params(),
        cost_estimate=cost(4 * 512 * 192 * 256, 1300000),
        name="owner",
    )(*[near_by(a) for a in (incoming, stale, table, accum)])


def store(*arrays):
    count = len(arrays)
    return pl.pallas_call(
        store_kernel,
        out_shape=tuple(pltpu.HBM(a.shape, a.dtype) for a in arrays),
        in_specs=[pl.BlockSpec(memory_space=pltpu.VMEM)] * count,
        out_specs=(pl.BlockSpec(memory_space=pltpu.HBM),) * count,
        scratch_shapes=[pltpu.SemaphoreType.DMA((count,))],
        compiler_params=params(),
        cost_estimate=cost(0, 2 * sum(4 * a.size for a in arrays)),
        name="store",
    )(*[near_by(a) for a in arrays])


def spread(change, counts, chips):
    return pl.pallas_call(
        spread_kernel,
        out_shape=pltpu.VMEM((chips,) + change.shape, jnp.float32),
        compiler_params=params(),
        cost_estimate=cost(10000000, 900000),
        name="spread",
    )(near_by(change), near_by(counts))


def refresh(core, cache_rows, change, done=None):
    flip = done is not None
    chips, span, width = change.shape
    vmem = pl.BlockSpec(memory_space=pltpu.VMEM)
    hbm = pl.BlockSpec(memory_space=pltpu.HBM)
    args = [core, near_by(cache_rows.reshape(chips, 2, span, width)), near_by(change)]
    args = args + ([done] if flip else [])
    return pl.pallas_call(
        functools.partial(refresh_kernel, flip=flip),
        out_shape=jax.ShapeDtypeStruct((chips, 2, span, width), jnp.float32),
        in_specs=[pl.BlockSpec(memory_space=pltpu.SMEM), vmem, vmem] + ([hbm] if flip else []),
        out_specs=hbm,
        scratch_shapes=[
            pltpu.VMEM((chips, span, width), jnp.float32),
            pltpu.SemaphoreType.DMA((chips,)),
        ],
        input_output_aliases={3: 0} if flip else {},
        compiler_params=params(),
        cost_estimate=cost(400000, 2400000),
        name="refresh_other" if flip else "refresh_mine",
    )(*args)


def shards(
    cache, counts, hot_rows, lookups, bag_lengths, projection, grad_out, table, accum, stale
):
    n_own = hot_rows.shape[2]
    chips = lax.axis_size("y")
    capacity = hot_rows.shape[3]
    slots, width = cache.shape[1:]
    span = n_own * capacity
    lookup = lookups.reshape(LOOKUP_ROWS, 128)
    lengths = bag_lengths.reshape(LENGTH_ROWS, 128)
    core = lax.axis_index("core").astype(jnp.int32).reshape(1)
    swap = [(0, 1), (1, 0)]

    mine = pack(lookup, lengths, grad_out[0, 0], projection)
    other = lax.ppermute(mine, "core", swap)
    half = both_slots(core, other, own_slots(core, mine, chips, span))
    half, late, hot_rows, stale, counts = lax.optimization_barrier(
        (half, mine, hot_rows, stale, counts)
    )
    ids = lax.dynamic_index_in_dim(hot_rows[0], lax.axis_index(GRP), 0, keepdims=False)
    ids = jnp.pad(ids.astype(jnp.float32), ((0, 0), (0, width - capacity)))
    live = lax.dynamic_index_in_dim(counts[0], lax.axis_index(GRP), 0, keepdims=True)
    projected = pool(core, late, cache[0], projection, 0)
    half, projected, ids, stale, live = lax.optimization_barrier(
        (half, projected, ids, stale[0, 0], live)
    )
    parts = lax.all_to_all(half, "y", split_axis=0, concat_axis=0, tiled=True)
    summed = combine(parts, ids)
    summed = summed.reshape(-1, 1, width)
    incoming = lax.all_to_all(summed, OWN, split_axis=0, concat_axis=0, tiled=True)
    incoming = incoming.reshape(-1, width)
    table_new, accum_new, change = owner(incoming, stale, table[0, 0], accum[0, 0])

    returned = lax.all_to_all(
        change.reshape(n_own, capacity, width), OWN, split_axis=0, concat_axis=0, tiled=True
    )
    wide = spread(returned.reshape(span, width), live, chips)
    near = lax.all_to_all(wide, "y", split_axis=0, concat_axis=0, tiled=True)
    near, projected, late = lax.optimization_barrier((near, projected, late))
    projected = pool(core, late, cache[0], projection, 1, done=projected)
    near, projected = lax.optimization_barrier((near, projected))
    far = lax.ppermute(near, "core", swap)
    near, table_new, accum_new = lax.optimization_barrier((near, table_new, accum_new))
    table_new, accum_new = store(table_new, accum_new)
    refreshed = refresh(core, cache[0], near)
    far, table_new, accum_new = lax.optimization_barrier((far, table_new, accum_new))
    refreshed = refresh(core, cache[0], far, done=refreshed)

    return (
        projected[None, None],
        table_new[None, None],
        accum_new[None, None],
        refreshed.reshape(1, slots, width),
    )


def solution(mesh):
    chips = Mesh(mesh.devices.reshape(4, 12, 8, 2), ("x", "z", "y", "core"))
    return jax.shard_map(
        shards,
        mesh=chips,
        in_specs=(
            P(OWN, None, None),
            P(OWN, None, None),
            P(OWN, None, None, None),
            P(OWN, GRP, None),
            P(OWN, GRP, None),
            P(),
            P(OWN, GRP, None, None),
            P(OWN, GRP, None, None),
            P(OWN, GRP, None, None),
            P(OWN, GRP, None, None),
        ),
        out_specs=(
            P(OWN, GRP, None, None),
            P(OWN, GRP, None, None),
            P(OWN, GRP, None, None),
            P(OWN, None, None),
        ),
        check_vma=False,
    )
```

```python
import functools

import jax
import jax.numpy as jnp
from jax import lax
from jax.experimental import pallas as pl
from jax.experimental.pallas import tpu as pltpu
from jax.sharding import Mesh
from jax.sharding import PartitionSpec as P

learn_rate = 0.3
epsilon = 1e-06
LOOKUP_ROWS = 16
LENGTH_ROWS = 2
OWN = ("x", "z")
GRP = ("y", "core")
STEP = 4
VMEM_BYTES = 40 * 1024 * 1024


def split(values):
    high = values.astype(jnp.bfloat16)
    low = (values - high.astype(jnp.float32)).astype(jnp.bfloat16)
    return jnp.concatenate([high, low], axis=1)


def joined(values):
    width = values.shape[1] // 2
    return values[:, :width] + values[:, width:]


def row_of(ref, first, count):
    return jnp.concatenate([ref[r : r + 1, :] for r in range(first, first + count)], axis=1)


def bag_hot(lengths):
    bags = lengths.shape[1]
    before = lax.broadcasted_iota(jnp.int32, (bags, bags), 0)
    after = lax.broadcasted_iota(jnp.int32, (bags, bags), 1)
    upper = jnp.where(before <= after, 1.0, 0.0).astype(jnp.bfloat16)
    tall = jnp.broadcast_to(lengths, (8, bags)).astype(jnp.bfloat16)
    ends = jnp.dot(tall, upper, preferred_element_type=jnp.float32)[0:1, :]
    starts = ends - lengths
    ends = ends.astype(jnp.int32)
    starts = starts.astype(jnp.int32)
    position = lax.broadcasted_iota(jnp.int32, (LOOKUP_ROWS * 128, bags), 0)
    inside = (position >= starts) & (position < ends)
    return jnp.where(inside, 1.0, 0.0).astype(jnp.bfloat16)


def slot_parts(lookup, span, groups):
    group = jnp.zeros_like(lookup)
    for k in range(1, groups):
        group = group + jnp.where(lookup >= k * span, 1, 0)
    place = lookup - group * span
    rows = lax.broadcasted_iota(jnp.int32, (span, lookup.shape[1]), 0)
    hot = jnp.where(rows == place, 1.0, 0.0).astype(jnp.bfloat16)
    return group, hot


def in_group(group, k):
    return jnp.where(group == k, 1.0, 0.0).astype(jnp.bfloat16)


def pack_kernel(lookup_hbm, length_hbm, cotangent_hbm, projection_hbm, out_ref, lookup, length, cotangent, projection, arrived):
    bags = cotangent.shape[0]
    sources = (lookup_hbm, length_hbm, cotangent_hbm, projection_hbm)
    copies = [
        pltpu.make_async_copy(source, target, arrived.at[i])
        for i, (source, target) in enumerate(zip(sources, (lookup, length, cotangent, projection)))
    ]
    for copy in copies:
        copy.start()
    for copy in copies:
        copy.wait()
    out_ref[:bags, :] = lax.dot_general(
        cotangent[...],
        projection[...],
        (((1,), (1,)), ((), ())),
        preferred_element_type=jnp.float32,
    )
    out_ref[bags : bags + LOOKUP_ROWS, :] = lookup[...].astype(jnp.float32)
    tail = jnp.zeros((8 - LENGTH_ROWS, 128), jnp.float32)
    out_ref[bags + LOOKUP_ROWS :, :] = jnp.concatenate(
        [length[...].astype(jnp.float32), tail], axis=0
    )


def unpack(packed_ref):
    bags = packed_ref.shape[0] - LOOKUP_ROWS - 8
    lookup = row_of(packed_ref, bags, LOOKUP_ROWS).astype(jnp.int32)
    return lookup, row_of(packed_ref, bags + LOOKUP_ROWS, LENGTH_ROWS)


def slot_parts_of(core_ref, packed_ref, chips, span, step):
    core = core_ref[0]
    lookup, lengths = unpack(packed_ref)
    bags = lengths.shape[1]
    rows = jnp.dot(
        bag_hot(lengths), split(packed_ref[:bags, :]), preferred_element_type=jnp.float32
    ).astype(jnp.bfloat16)
    group, hot = slot_parts(lookup, span, 2 * chips)
    for y in range(0, chips, step):
        slots = jnp.concatenate(
            [hot * in_group(group, 2 * j + core) for j in range(y, y + step)], axis=0
        )
        delta = joined(jnp.dot(slots, rows, preferred_element_type=jnp.float32))
        yield pl.ds(y, step), delta.reshape(step, span, delta.shape[1])


def own_kernel(core_ref, packed_ref, out_ref):
    chips, span, _ = out_ref.shape
    for place, delta in slot_parts_of(core_ref, packed_ref, chips, span, STEP):
        out_ref[place, :, :] = delta


def both_kernel(core_ref, packed_ref, start_ref, out_ref):
    chips, span, _ = out_ref.shape
    for place, delta in slot_parts_of(core_ref, packed_ref, chips, span, STEP):
        out_ref[place, :, :] = start_ref[place, :, :] + delta


def pool_kernel(core_ref, packed_ref, cache_ref, projection_ref, *refs, turn):
    out_hbm, count_ref, ready, sent = refs[-4:]

    @pl.when(core_ref[0] == turn)
    def _():
        slots = cache_ref.shape[0]
        span = 192
        groups = slots // span
        lookup, lengths = unpack(packed_ref)
        bags = bag_hot(lengths)
        group, hot = slot_parts(lookup, span, groups)
        for k in range(0, groups, STEP):
            chosen = jnp.concatenate([hot * in_group(group, j) for j in range(k, k + STEP)], axis=0)
            count = jnp.dot(chosen, bags, preferred_element_type=jnp.float32)
            count_ref[k * span : (k + STEP) * span, :] = count.astype(jnp.bfloat16)
        pooled = lax.dot_general(
            count_ref[...],
            split(cache_ref[...]),
            (((0,), (0,)), ((), ())),
            preferred_element_type=jnp.float32,
        )
        pooled = joined(pooled).astype(jnp.bfloat16)
        ready[...] = jnp.dot(
            pooled, projection_ref[...], preferred_element_type=jnp.float32
        ).astype(jnp.bfloat16)
        copy = pltpu.make_async_copy(ready, out_hbm, sent.at[0])
        copy.start()
        copy.wait()


def turned(values, width):
    rows, columns = values.shape
    tall = jnp.concatenate([values, jnp.zeros((8 - rows, columns), values.dtype)], axis=0)
    lane = lax.broadcasted_iota(jnp.int32, (8, width), 1)
    unit = jnp.where(lax.broadcasted_iota(jnp.int32, (8, width), 0) == lane, 1.0, 0.0)
    return lax.dot_general(
        tall.astype(jnp.float32).astype(jnp.bfloat16),
        unit.astype(jnp.bfloat16),
        (((0,), (0,)), ((), ())),
        preferred_element_type=jnp.float32,
    )


def combine_kernel(grp_ref, parts_ref, hot_ref, out_ref):
    _, capacity, owners = hot_ref.shape
    ids = hot_ref[grp_ref[0], :, :]
    width = out_ref.shape[1]
    out_ref[pl.ds(capacity, owners, stride=capacity + 1), :] = 16.0 * turned(
        lax.shift_right_logical(ids, 4), width
    ) + turned(ids & 15, width)
    for c in range(capacity):
        rows = pl.ds(c, owners, stride=capacity)
        total = parts_ref[0, rows, :]
        for y in range(1, parts_ref.shape[0]):
            total = total + parts_ref[y, rows, :]
        out_ref[pl.ds(c, owners, stride=capacity + 1), :] = total


def owner_kernel(
    incoming_ref, stale_ref, table_ref, accum_ref, table_new_ref, accum_new_ref, change_ref
):
    capacity, holders = stale_ref.shape
    table_rows = table_ref.shape[0]

    def taken(c):
        return incoming_ref[pl.ds(c, holders, stride=capacity + 1), :]

    ids = taken(capacity)[:, :capacity].astype(jnp.int32)
    stale = turned(stale_ref[...], table_ref.shape[1])
    row = lax.broadcasted_iota(jnp.int32, (holders, table_rows), 1)
    hot = [jnp.where(row == ids[:, c : c + 1], 1.0, 0.0) for c in range(capacity)]
    wanted = [hot[c] * stale[:, c : c + 1] for c in range(capacity)]
    incoming = jnp.concatenate([taken(c) for c in range(capacity)], axis=0)
    gradient = joined(
        lax.dot_general(
            jnp.concatenate(hot, axis=0).astype(jnp.bfloat16),
            split(incoming),
            (((0,), (0,)), ((), ())),
            preferred_element_type=jnp.float32,
        )
    )
    accum_new = accum_ref[...] + gradient * gradient
    accum_new_ref[...] = accum_new
    old = table_ref[...]
    new = old - learn_rate * gradient / (jnp.sqrt(accum_new) + epsilon)
    table_new_ref[...] = new
    change = joined(
        jnp.dot(
            jnp.concatenate(wanted, axis=0).astype(jnp.bfloat16),
            split(new - old),
            preferred_element_type=jnp.float32,
        )
    )
    for c in range(capacity):
        change_ref[pl.ds(c, holders, stride=capacity), :] = change[
            c * holders : (c + 1) * holders, :
        ]


def spread_kernel(grp_ref, change_ref, counts_ref, out_ref):
    chips, span, width = out_ref.shape
    owners = counts_ref.shape[1]
    place = lax.broadcasted_iota(jnp.int32, (span, owners), 0) - (
        span // owners
    ) * lax.broadcasted_iota(jnp.int32, (span, owners), 1)
    live = jnp.where((place >= 0) & (place < counts_ref[pl.ds(grp_ref[0], 1), :]), 1.0, 0.0).astype(jnp.bfloat16)
    live = jnp.dot(live, jnp.ones((owners, width), jnp.bfloat16), preferred_element_type=jnp.float32)
    change = jnp.where(live > 0.5, change_ref[...], 0.0)
    for y in range(chips):
        out_ref[y, :, :] = change


def store_kernel(*refs):
    count = len(refs) // 2
    sent = refs[-1]
    copies = [
        pltpu.make_async_copy(refs[i], refs[count + i], sent.at[i]) for i in range(count)
    ]
    for copy in copies:
        copy.start()
    for copy in copies:
        copy.wait()


def refresh_kernel(core_ref, cache_ref, change_ref, *refs, flip):
    out_hbm, ready, sent = refs[-3:]
    chips = change_ref.shape[0]
    core = 1 - core_ref[0] if flip else core_ref[0]
    copies = []
    for y in range(chips):
        ready[y, :, :] = cache_ref[y, core, :, :] + change_ref[y, :, :]
        copies.append(pltpu.make_async_copy(ready.at[y], out_hbm.at[y, core], sent.at[y]))
        copies[-1].start()
    for copy in copies:
        copy.wait()


def params():
    return pltpu.CompilerParams(vmem_limit_bytes=VMEM_BYTES)


def near_by(array):
    return pltpu.with_memory_space_constraint(array, pltpu.VMEM)


def cost(flops, moved):
    return pl.CostEstimate(flops=flops, bytes_accessed=moved, transcendentals=0)


def pack(lookup, lengths, cotangent, projection):
    rows = cotangent.shape[0] + LOOKUP_ROWS + 8
    given = (lookup, lengths, cotangent, projection)
    held = [pltpu.with_memory_space_constraint(a, pltpu.HBM) for a in given]
    return pl.pallas_call(
        pack_kernel,
        out_shape=pltpu.VMEM((rows, projection.shape[0]), jnp.float32),
        in_specs=[pl.BlockSpec(memory_space=pltpu.HBM)] * 4,
        out_specs=pl.BlockSpec(memory_space=pltpu.VMEM),
        scratch_shapes=[pltpu.VMEM(a.shape, a.dtype) for a in given]
        + [pltpu.SemaphoreType.DMA((4,))],
        compiler_params=params(),
        cost_estimate=cost(2 * 256 * 256 * 128, 400000),
        name="pack",
    )(*held)


def own_slots(core, packed, chips, span):
    vmem = pl.BlockSpec(memory_space=pltpu.VMEM)
    return pl.pallas_call(
        own_kernel,
        out_shape=pltpu.VMEM((chips, span, packed.shape[1]), jnp.float32),
        in_specs=[pl.BlockSpec(memory_space=pltpu.SMEM), vmem],
        out_specs=vmem,
        compiler_params=params(),
        cost_estimate=cost(3072 * 2048 * 256, 1000000),
        name="own_slots",
    )(core, near_by(packed))


def both_slots(core, packed, start):
    vmem = pl.BlockSpec(memory_space=pltpu.VMEM)
    return pl.pallas_call(
        both_kernel,
        out_shape=pltpu.VMEM(start.shape, jnp.float32),
        in_specs=[pl.BlockSpec(memory_space=pltpu.SMEM), vmem, vmem],
        out_specs=vmem,
        compiler_params=params(),
        cost_estimate=cost(3072 * 2048 * 256, 1800000),
        name="both_slots",
    )(core, near_by(packed), near_by(start))


def pool(core, packed, cache_rows, projection, turn, done=None):
    bags = packed.shape[0] - LOOKUP_ROWS - 8
    vmem = pl.BlockSpec(memory_space=pltpu.VMEM)
    hbm = pl.BlockSpec(memory_space=pltpu.HBM)
    more = [] if done is None else [done]
    return pl.pallas_call(
        functools.partial(pool_kernel, turn=turn),
        out_shape=pltpu.HBM((bags, projection.shape[1]), jnp.bfloat16),
        in_specs=[pl.BlockSpec(memory_space=pltpu.SMEM), vmem, vmem, vmem] + [hbm] * len(more),
        out_specs=hbm,
        scratch_shapes=[
            pltpu.VMEM((cache_rows.shape[0], bags), jnp.bfloat16),
            pltpu.VMEM((bags, projection.shape[1]), jnp.bfloat16),
            pltpu.SemaphoreType.DMA((1,)),
        ],
        input_output_aliases={4: 0} if more else {},
        compiler_params=params(),
        cost_estimate=cost(2 * 3072 * 2048 * 256, 2000000),
        name="pool_late" if more else "pool_early",
    )(core, near_by(packed), near_by(cache_rows), near_by(projection), *more)


def combine(grp, parts, hot):
    chips, span, width = parts.shape
    vmem = pl.BlockSpec(memory_space=pltpu.VMEM)
    return pl.pallas_call(
        combine_kernel,
        out_shape=pltpu.VMEM((span + hot.shape[2], width), jnp.float32),
        in_specs=[pl.BlockSpec(memory_space=pltpu.SMEM), vmem, vmem],
        out_specs=vmem,
        compiler_params=params(),
        cost_estimate=cost(200000, 900000),
        name="combine",
    )(grp, near_by(parts), near_by(hot))


def owner(incoming, stale, table, accum):
    table_like = pltpu.VMEM(table.shape, jnp.float32)
    change = pltpu.VMEM((stale.size, table.shape[1]), jnp.float32)
    return pl.pallas_call(
        owner_kernel,
        out_shape=(table_like, table_like, change),
        compiler_params=params(),
        cost_estimate=cost(4 * 512 * 192 * 256, 1300000),
        name="owner",
    )(*[near_by(a) for a in (incoming, stale, table, accum)])


def store(*arrays):
    count = len(arrays)
    return pl.pallas_call(
        store_kernel,
        out_shape=tuple(pltpu.HBM(a.shape, a.dtype) for a in arrays),
        in_specs=[pl.BlockSpec(memory_space=pltpu.VMEM)] * count,
        out_specs=(pl.BlockSpec(memory_space=pltpu.HBM),) * count,
        scratch_shapes=[pltpu.SemaphoreType.DMA((count,))],
        compiler_params=params(),
        cost_estimate=cost(0, 2 * sum(4 * a.size for a in arrays)),
        name="store",
    )(*[near_by(a) for a in arrays])


def spread(grp, change, counts, chips):
    vmem = pl.BlockSpec(memory_space=pltpu.VMEM)
    return pl.pallas_call(
        spread_kernel,
        out_shape=pltpu.VMEM((chips,) + change.shape, jnp.float32),
        in_specs=[pl.BlockSpec(memory_space=pltpu.SMEM), vmem, vmem],
        out_specs=vmem,
        compiler_params=params(),
        cost_estimate=cost(10000000, 900000),
        name="spread",
    )(grp, near_by(change), near_by(counts))


def refresh(core, cache_rows, change, done=None):
    flip = done is not None
    chips, span, width = change.shape
    vmem = pl.BlockSpec(memory_space=pltpu.VMEM)
    hbm = pl.BlockSpec(memory_space=pltpu.HBM)
    args = [core, near_by(cache_rows.reshape(chips, 2, span, width)), near_by(change)]
    args = args + ([done] if flip else [])
    return pl.pallas_call(
        functools.partial(refresh_kernel, flip=flip),
        out_shape=jax.ShapeDtypeStruct((chips, 2, span, width), jnp.float32),
        in_specs=[pl.BlockSpec(memory_space=pltpu.SMEM), vmem, vmem] + ([hbm] if flip else []),
        out_specs=hbm,
        scratch_shapes=[
            pltpu.VMEM((chips, span, width), jnp.float32),
            pltpu.SemaphoreType.DMA((chips,)),
        ],
        input_output_aliases={3: 0} if flip else {},
        compiler_params=params(),
        cost_estimate=cost(400000, 2400000),
        name="refresh_other" if flip else "refresh_mine",
    )(*args)


def shards(
    cache, counts, hot_rows, lookups, bag_lengths, projection, grad_out, table, accum, stale
):
    n_own = hot_rows.shape[2]
    chips = lax.axis_size("y")
    capacity = hot_rows.shape[3]
    slots, width = cache.shape[1:]
    span = n_own * capacity
    lookup = lookups.reshape(LOOKUP_ROWS, 128)
    lengths = bag_lengths.reshape(LENGTH_ROWS, 128)
    core = lax.axis_index("core").astype(jnp.int32).reshape(1)
    grp = lax.axis_index(GRP).astype(jnp.int32).reshape(1)
    swap = [(0, 1), (1, 0)]

    mine = pack(lookup, lengths, grad_out[0, 0], projection)
    other = lax.ppermute(mine, "core", swap)
    half = both_slots(core, other, own_slots(core, mine, chips, span))
    half, late = lax.optimization_barrier((half, mine))
    projected = pool(core, late, cache[0], projection, 0)
    half, projected = lax.optimization_barrier((half, projected))
    parts = lax.all_to_all(half, "y", split_axis=0, concat_axis=0, tiled=True)
    summed = combine(grp, parts, hot_rows[0].transpose(0, 2, 1))
    summed = summed.reshape(-1, 1, width)
    incoming = lax.all_to_all(summed, OWN, split_axis=0, concat_axis=0, tiled=True)
    incoming = incoming.reshape(-1, width)
    table_new, accum_new, change = owner(incoming, stale[0, 0].T, table[0, 0], accum[0, 0])

    returned = lax.all_to_all(
        change.reshape(n_own, capacity, width), OWN, split_axis=0, concat_axis=0, tiled=True
    )
    wide = spread(grp, returned.reshape(span, width), counts[0], chips)
    near = lax.all_to_all(wide, "y", split_axis=0, concat_axis=0, tiled=True)
    near, projected, late = lax.optimization_barrier((near, projected, late))
    projected = pool(core, late, cache[0], projection, 1, done=projected)
    near, projected = lax.optimization_barrier((near, projected))
    far = lax.ppermute(near, "core", swap)
    near, table_new, accum_new = lax.optimization_barrier((near, table_new, accum_new))
    table_new, accum_new = store(table_new, accum_new)
    refreshed = refresh(core, cache[0], near)
    far, table_new, accum_new = lax.optimization_barrier((far, table_new, accum_new))
    refreshed = refresh(core, cache[0], far, done=refreshed)

    return (
        projected[None, None],
        table_new[None, None],
        accum_new[None, None],
        refreshed.reshape(1, slots, width),
    )


def solution(mesh):
    chips = Mesh(mesh.devices.reshape(4, 12, 8, 2), ("x", "z", "y", "core"))
    return jax.shard_map(
        shards,
        mesh=chips,
        in_specs=(
            P(OWN, None, None),
            P(OWN, None, None),
            P(OWN, None, None, None),
            P(OWN, GRP, None),
            P(OWN, GRP, None),
            P(),
            P(OWN, GRP, None, None),
            P(OWN, GRP, None, None),
            P(OWN, GRP, None, None),
            P(OWN, GRP, None, None),
        ),
        out_specs=(
            P(OWN, GRP, None, None),
            P(OWN, GRP, None, None),
            P(OWN, GRP, None, None),
            P(OWN, None, None),
        ),
        check_vma=False,
    )
```

```python
import functools

import jax
import jax.numpy as jnp
from jax import lax
from jax.experimental import pallas as pl
from jax.experimental.pallas import tpu as pltpu
from jax.sharding import Mesh
from jax.sharding import PartitionSpec as P

learn_rate = 0.3
epsilon = 1e-06
LOOKUP_ROWS = 16
LENGTH_ROWS = 2
OWN = ("x", "z")
GRP = ("y", "core")
STEP = 4
VMEM_BYTES = 40 * 1024 * 1024


def split(values):
    high = values.astype(jnp.bfloat16)
    low = (values - high.astype(jnp.float32)).astype(jnp.bfloat16)
    return jnp.concatenate([high, low], axis=1)


def joined(values):
    width = values.shape[1] // 2
    return values[:, :width] + values[:, width:]


def row_of(ref, first, count):
    return jnp.concatenate([ref[r : r + 1, :] for r in range(first, first + count)], axis=1)


def bag_hot(lengths):
    bags = lengths.shape[1]
    before = lax.broadcasted_iota(jnp.int32, (bags, bags), 0)
    after = lax.broadcasted_iota(jnp.int32, (bags, bags), 1)
    upper = jnp.where(before <= after, 1.0, 0.0).astype(jnp.bfloat16)
    tall = jnp.broadcast_to(lengths, (8, bags)).astype(jnp.bfloat16)
    ends = jnp.dot(tall, upper, preferred_element_type=jnp.float32)[0:1, :]
    starts = ends - lengths
    ends = ends.astype(jnp.int32)
    starts = starts.astype(jnp.int32)
    position = lax.broadcasted_iota(jnp.int32, (LOOKUP_ROWS * 128, bags), 0)
    inside = (position >= starts) & (position < ends)
    return jnp.where(inside, 1.0, 0.0).astype(jnp.bfloat16)


def slot_parts(lookup, span, groups):
    group = jnp.zeros_like(lookup)
    for k in range(1, groups):
        group = group + jnp.where(lookup >= k * span, 1, 0)
    place = lookup - group * span
    rows = lax.broadcasted_iota(jnp.int32, (span, lookup.shape[1]), 0)
    hot = jnp.where(rows == place, 1.0, 0.0).astype(jnp.bfloat16)
    return group, hot


def in_group(group, k):
    return jnp.where(group == k, 1.0, 0.0).astype(jnp.bfloat16)


def pack_kernel(lookup_hbm, length_hbm, cotangent_hbm, projection_hbm, out_ref, lookup, length, cotangent, projection, arrived):
    bags = cotangent.shape[0]
    sources = (lookup_hbm, length_hbm, cotangent_hbm, projection_hbm)
    copies = [
        pltpu.make_async_copy(source, target, arrived.at[i])
        for i, (source, target) in enumerate(zip(sources, (lookup, length, cotangent, projection)))
    ]
    for copy in copies:
        copy.start()
    for copy in copies:
        copy.wait()
    out_ref[:bags, :] = lax.dot_general(
        cotangent[...],
        projection[...],
        (((1,), (1,)), ((), ())),
        preferred_element_type=jnp.float32,
    )
    out_ref[bags : bags + LOOKUP_ROWS, :] = lookup[...].astype(jnp.float32)
    tail = jnp.zeros((8 - LENGTH_ROWS, 128), jnp.float32)
    out_ref[bags + LOOKUP_ROWS :, :] = jnp.concatenate(
        [length[...].astype(jnp.float32), tail], axis=0
    )


def unpack(packed_ref):
    bags = packed_ref.shape[0] - LOOKUP_ROWS - 8
    lookup = row_of(packed_ref, bags, LOOKUP_ROWS).astype(jnp.int32)
    return lookup, row_of(packed_ref, bags + LOOKUP_ROWS, LENGTH_ROWS)


def slot_parts_of(core_ref, packed_ref, chips, span, step):
    core = core_ref[0]
    lookup, lengths = unpack(packed_ref)
    bags = lengths.shape[1]
    rows = jnp.dot(
        bag_hot(lengths), split(packed_ref[:bags, :]), preferred_element_type=jnp.float32
    ).astype(jnp.bfloat16)
    group, hot = slot_parts(lookup, span, 2 * chips)
    for y in range(0, chips, step):
        slots = jnp.concatenate(
            [hot * in_group(group, 2 * j + core) for j in range(y, y + step)], axis=0
        )
        delta = joined(jnp.dot(slots, rows, preferred_element_type=jnp.float32))
        yield pl.ds(y, step), delta.reshape(step, span, delta.shape[1])


def own_kernel(core_ref, packed_ref, out_ref):
    chips, span, _ = out_ref.shape
    for place, delta in slot_parts_of(core_ref, packed_ref, chips, span, STEP):
        out_ref[place, :, :] = delta


def both_kernel(core_ref, packed_ref, start_ref, out_ref):
    chips, span, _ = out_ref.shape
    for place, delta in slot_parts_of(core_ref, packed_ref, chips, span, STEP):
        out_ref[place, :, :] = start_ref[place, :, :] + delta


def turned(values, width):
    rows, columns = values.shape
    tall = jnp.concatenate([values, jnp.zeros((8 - rows, columns), values.dtype)], axis=0)
    lane = lax.broadcasted_iota(jnp.int32, (8, width), 1)
    unit = jnp.where(lax.broadcasted_iota(jnp.int32, (8, width), 0) == lane, 1.0, 0.0)
    return lax.dot_general(
        tall.astype(jnp.float32).astype(jnp.bfloat16),
        unit.astype(jnp.bfloat16),
        (((0,), (0,)), ((), ())),
        preferred_element_type=jnp.float32,
    )


def pool_kernel(core_ref, packed_ref, cache_ref, projection_ref, *refs, turn):
    out_hbm, count_ref, ready, sent = refs[-4:]

    @pl.when(core_ref[0] == turn)
    def _():
        slots = cache_ref.shape[0]
        span = 192
        groups = slots // span
        lookup, lengths = unpack(packed_ref)
        bags = bag_hot(lengths)
        group, hot = slot_parts(lookup, span, groups)
        for k in range(0, groups, STEP):
            chosen = jnp.concatenate([hot * in_group(group, j) for j in range(k, k + STEP)], axis=0)
            count = jnp.dot(chosen, bags, preferred_element_type=jnp.float32)
            count_ref[k * span : (k + STEP) * span, :] = count.astype(jnp.bfloat16)
        pooled = lax.dot_general(
            count_ref[...],
            split(cache_ref[...]),
            (((0,), (0,)), ((), ())),
            preferred_element_type=jnp.float32,
        )
        pooled = joined(pooled).astype(jnp.bfloat16)
        ready[...] = jnp.dot(
            pooled, projection_ref[...], preferred_element_type=jnp.float32
        ).astype(jnp.bfloat16)
        copy = pltpu.make_async_copy(ready, out_hbm, sent.at[0])
        copy.start()
        copy.wait()


def early_kernel(
    core_ref, grp_ref, packed_ref, cache_ref, projection_ref, hot_ref, stale_ref, counts_ref,
    out_hbm, ids_ref, flags_ref, live_ref, *scratch
):
    _, capacity, owners = hot_ref.shape
    width = ids_ref.shape[1]
    ids = hot_ref[grp_ref[0], :, :]
    ids_ref[...] = 16.0 * turned(lax.shift_right_logical(ids, 4), width) + turned(ids & 15, width)
    flags_ref[...] = turned(stale_ref[...], width)
    place = lax.broadcasted_iota(jnp.int32, (owners * capacity, owners), 0) - (
        capacity * lax.broadcasted_iota(jnp.int32, (owners * capacity, owners), 1)
    )
    counts = counts_ref[pl.ds(grp_ref[0], 1), :]
    live = jnp.where((place >= 0) & (place < counts), 1.0, 0.0).astype(jnp.bfloat16)
    ones = jnp.ones((owners, width), jnp.bfloat16)
    live_ref[...] = jnp.dot(live, ones, preferred_element_type=jnp.float32)
    pool_kernel(core_ref, packed_ref, cache_ref, projection_ref, out_hbm, *scratch, turn=0)


def combine_kernel(parts_ref, ids_ref, out_ref):
    owners, _ = ids_ref.shape
    capacity = parts_ref.shape[1] // owners
    out_ref[pl.ds(capacity, owners, stride=capacity + 1), :] = ids_ref[...]
    for c in range(capacity):
        rows = pl.ds(c, owners, stride=capacity)
        total = parts_ref[0, rows, :]
        for y in range(1, parts_ref.shape[0]):
            total = total + parts_ref[y, rows, :]
        out_ref[pl.ds(c, owners, stride=capacity + 1), :] = total


def owner_kernel(
    incoming_ref, stale_ref, table_ref, accum_ref, table_new_ref, accum_new_ref, change_ref
):
    holders = stale_ref.shape[0]
    capacity = incoming_ref.shape[0] // holders - 1
    table_rows = table_ref.shape[0]

    def taken(c):
        return incoming_ref[pl.ds(c, holders, stride=capacity + 1), :]

    ids = taken(capacity)[:, :capacity].astype(jnp.int32)
    stale = stale_ref[...]
    row = lax.broadcasted_iota(jnp.int32, (holders, table_rows), 1)
    hot = [jnp.where(row == ids[:, c : c + 1], 1.0, 0.0) for c in range(capacity)]
    wanted = [hot[c] * stale[:, c : c + 1] for c in range(capacity)]
    incoming = jnp.concatenate([taken(c) for c in range(capacity)], axis=0)
    gradient = joined(
        lax.dot_general(
            jnp.concatenate(hot, axis=0).astype(jnp.bfloat16),
            split(incoming),
            (((0,), (0,)), ((), ())),
            preferred_element_type=jnp.float32,
        )
    )
    accum_new = accum_ref[...] + gradient * gradient
    accum_new_ref[...] = accum_new
    old = table_ref[...]
    new = old - learn_rate * gradient / (jnp.sqrt(accum_new) + epsilon)
    table_new_ref[...] = new
    change = joined(
        jnp.dot(
            jnp.concatenate(wanted, axis=0).astype(jnp.bfloat16),
            split(new - old),
            preferred_element_type=jnp.float32,
        )
    )
    for c in range(capacity):
        change_ref[pl.ds(c, holders, stride=capacity), :] = change[
            c * holders : (c + 1) * holders, :
        ]


def spread_kernel(change_ref, live_ref, out_ref):
    change = jnp.where(live_ref[...] > 0.5, change_ref[...], 0.0)
    for y in range(out_ref.shape[0]):
        out_ref[y, :, :] = change


def store_kernel(*refs):
    count = len(refs) // 2
    sent = refs[-1]
    copies = [
        pltpu.make_async_copy(refs[i], refs[count + i], sent.at[i]) for i in range(count)
    ]
    for copy in copies:
        copy.start()
    for copy in copies:
        copy.wait()


def refresh_kernel(core_ref, cache_ref, change_ref, *refs, flip):
    out_hbm, ready, sent = refs[-3:]
    chips = change_ref.shape[0]
    core = 1 - core_ref[0] if flip else core_ref[0]
    copies = []
    for y in range(chips):
        ready[y, :, :] = cache_ref[y, core, :, :] + change_ref[y, :, :]
        copies.append(pltpu.make_async_copy(ready.at[y], out_hbm.at[y, core], sent.at[y]))
        copies[-1].start()
    for copy in copies:
        copy.wait()


def params():
    return pltpu.CompilerParams(vmem_limit_bytes=VMEM_BYTES)


def near_by(array):
    return pltpu.with_memory_space_constraint(array, pltpu.VMEM)


def cost(flops, moved):
    return pl.CostEstimate(flops=flops, bytes_accessed=moved, transcendentals=0)


def pack(lookup, lengths, cotangent, projection):
    rows = cotangent.shape[0] + LOOKUP_ROWS + 8
    given = (lookup, lengths, cotangent, projection)
    held = [pltpu.with_memory_space_constraint(a, pltpu.HBM) for a in given]
    return pl.pallas_call(
        pack_kernel,
        out_shape=pltpu.VMEM((rows, projection.shape[0]), jnp.float32),
        in_specs=[pl.BlockSpec(memory_space=pltpu.HBM)] * 4,
        out_specs=pl.BlockSpec(memory_space=pltpu.VMEM),
        scratch_shapes=[pltpu.VMEM(a.shape, a.dtype) for a in given]
        + [pltpu.SemaphoreType.DMA((4,))],
        compiler_params=params(),
        cost_estimate=cost(2 * 256 * 256 * 128, 400000),
        name="pack",
    )(*held)


def own_slots(core, packed, chips, span):
    vmem = pl.BlockSpec(memory_space=pltpu.VMEM)
    return pl.pallas_call(
        own_kernel,
        out_shape=pltpu.VMEM((chips, span, packed.shape[1]), jnp.float32),
        in_specs=[pl.BlockSpec(memory_space=pltpu.SMEM), vmem],
        out_specs=vmem,
        compiler_params=params(),
        cost_estimate=cost(3072 * 2048 * 256, 1000000),
        name="own_slots",
    )(core, near_by(packed))


def both_slots(core, packed, start):
    vmem = pl.BlockSpec(memory_space=pltpu.VMEM)
    return pl.pallas_call(
        both_kernel,
        out_shape=pltpu.VMEM(start.shape, jnp.float32),
        in_specs=[pl.BlockSpec(memory_space=pltpu.SMEM), vmem, vmem],
        out_specs=vmem,
        compiler_params=params(),
        cost_estimate=cost(3072 * 2048 * 256, 1800000),
        name="both_slots",
    )(core, near_by(packed), near_by(start))


def pool_scratch(cache_rows, projection, bags):
    return [
        pltpu.VMEM((cache_rows.shape[0], bags), jnp.bfloat16),
        pltpu.VMEM((bags, projection.shape[1]), jnp.bfloat16),
        pltpu.SemaphoreType.DMA((1,)),
    ]


def pool_early(core, grp, packed, cache_rows, projection, hot, stale, counts):
    bags = packed.shape[0] - LOOKUP_ROWS - 8
    _, capacity, owners = hot.shape
    width = cache_rows.shape[1]
    vmem = pl.BlockSpec(memory_space=pltpu.VMEM)
    smem = pl.BlockSpec(memory_space=pltpu.SMEM)
    given = (packed, cache_rows, projection, hot, stale, counts)
    return pl.pallas_call(
        early_kernel,
        out_shape=(
            pltpu.HBM((bags, projection.shape[1]), jnp.bfloat16),
            pltpu.VMEM((owners, width), jnp.float32),
            pltpu.VMEM((owners, width), jnp.float32),
            pltpu.VMEM((owners * capacity, width), jnp.float32),
        ),
        in_specs=[smem, smem] + [vmem] * len(given),
        out_specs=(pl.BlockSpec(memory_space=pltpu.HBM), vmem, vmem, vmem),
        scratch_shapes=pool_scratch(cache_rows, projection, bags),
        compiler_params=params(),
        cost_estimate=cost(2 * 3072 * 2048 * 256, 2000000),
        name="pool_early",
    )(core, grp, *[near_by(a) for a in given])


def pool_late(core, packed, cache_rows, projection, done):
    bags = packed.shape[0] - LOOKUP_ROWS - 8
    vmem = pl.BlockSpec(memory_space=pltpu.VMEM)
    hbm = pl.BlockSpec(memory_space=pltpu.HBM)
    return pl.pallas_call(
        functools.partial(pool_kernel, turn=1),
        out_shape=pltpu.HBM((bags, projection.shape[1]), jnp.bfloat16),
        in_specs=[pl.BlockSpec(memory_space=pltpu.SMEM), vmem, vmem, vmem, hbm],
        out_specs=hbm,
        scratch_shapes=pool_scratch(cache_rows, projection, bags),
        input_output_aliases={4: 0},
        compiler_params=params(),
        cost_estimate=cost(2 * 3072 * 2048 * 256, 2000000),
        name="pool_late",
    )(core, near_by(packed), near_by(cache_rows), near_by(projection), done)


def combine(parts, ids):
    chips, span, width = parts.shape
    return pl.pallas_call(
        combine_kernel,
        out_shape=pltpu.VMEM((span + ids.shape[0], width), jnp.float32),
        compiler_params=params(),
        cost_estimate=cost(200000, 900000),
        name="combine",
    )(near_by(parts), near_by(ids))


def owner(incoming, stale, table, accum):
    table_like = pltpu.VMEM(table.shape, jnp.float32)
    rows = incoming.shape[0] - stale.shape[0]
    change = pltpu.VMEM((rows, table.shape[1]), jnp.float32)
    return pl.pallas_call(
        owner_kernel,
        out_shape=(table_like, table_like, change),
        compiler_params=params(),
        cost_estimate=cost(4 * 512 * 192 * 256, 1300000),
        name="owner",
    )(*[near_by(a) for a in (incoming, stale, table, accum)])


def store(*arrays):
    count = len(arrays)
    return pl.pallas_call(
        store_kernel,
        out_shape=tuple(pltpu.HBM(a.shape, a.dtype) for a in arrays),
        in_specs=[pl.BlockSpec(memory_space=pltpu.VMEM)] * count,
        out_specs=(pl.BlockSpec(memory_space=pltpu.HBM),) * count,
        scratch_shapes=[pltpu.SemaphoreType.DMA((count,))],
        compiler_params=params(),
        cost_estimate=cost(0, 2 * sum(4 * a.size for a in arrays)),
        name="store",
    )(*[near_by(a) for a in arrays])


def spread(change, live, chips):
    return pl.pallas_call(
        spread_kernel,
        out_shape=pltpu.VMEM((chips,) + change.shape, jnp.float32),
        compiler_params=params(),
        cost_estimate=cost(200000, 900000),
        name="spread",
    )(near_by(change), near_by(live))


def refresh(core, cache_rows, change, done=None):
    flip = done is not None
    chips, span, width = change.shape
    vmem = pl.BlockSpec(memory_space=pltpu.VMEM)
    hbm = pl.BlockSpec(memory_space=pltpu.HBM)
    args = [core, near_by(cache_rows.reshape(chips, 2, span, width)), near_by(change)]
    args = args + ([done] if flip else [])
    return pl.pallas_call(
        functools.partial(refresh_kernel, flip=flip),
        out_shape=jax.ShapeDtypeStruct((chips, 2, span, width), jnp.float32),
        in_specs=[pl.BlockSpec(memory_space=pltpu.SMEM), vmem, vmem] + ([hbm] if flip else []),
        out_specs=hbm,
        scratch_shapes=[
            pltpu.VMEM((chips, span, width), jnp.float32),
            pltpu.SemaphoreType.DMA((chips,)),
        ],
        input_output_aliases={3: 0} if flip else {},
        compiler_params=params(),
        cost_estimate=cost(400000, 2400000),
        name="refresh_other" if flip else "refresh_mine",
    )(*args)


def shards(
    cache, counts, hot_rows, lookups, bag_lengths, projection, grad_out, table, accum, stale
):
    n_own = hot_rows.shape[2]
    chips = lax.axis_size("y")
    capacity = hot_rows.shape[3]
    slots, width = cache.shape[1:]
    span = n_own * capacity
    lookup = lookups.reshape(LOOKUP_ROWS, 128)
    lengths = bag_lengths.reshape(LENGTH_ROWS, 128)
    core = lax.axis_index("core").astype(jnp.int32).reshape(1)
    grp = lax.axis_index(GRP).astype(jnp.int32).reshape(1)
    swap = [(0, 1), (1, 0)]

    mine = pack(lookup, lengths, grad_out[0, 0], projection)
    other = lax.ppermute(mine, "core", swap)
    half = both_slots(core, other, own_slots(core, mine, chips, span))
    half, late = lax.optimization_barrier((half, mine))
    projected, ids, flags, live = pool_early(
        core,
        grp,
        late,
        cache[0],
        projection,
        hot_rows[0].transpose(0, 2, 1),
        stale[0, 0].T,
        counts[0],
    )
    half, projected, ids, flags, live = lax.optimization_barrier(
        (half, projected, ids, flags, live)
    )
    parts = lax.all_to_all(half, "y", split_axis=0, concat_axis=0, tiled=True)
    summed = combine(parts, ids)
    summed = summed.reshape(-1, 1, width)
    incoming = lax.all_to_all(summed, OWN, split_axis=0, concat_axis=0, tiled=True)
    incoming = incoming.reshape(-1, width)
    table_new, accum_new, change = owner(incoming, flags, table[0, 0], accum[0, 0])

    returned = lax.all_to_all(
        change.reshape(n_own, capacity, width), OWN, split_axis=0, concat_axis=0, tiled=True
    )
    wide = spread(returned.reshape(span, width), live, chips)
    near = lax.all_to_all(wide, "y", split_axis=0, concat_axis=0, tiled=True)
    near, projected, late = lax.optimization_barrier((near, projected, late))
    projected = pool_late(core, late, cache[0], projection, projected)
    near, projected = lax.optimization_barrier((near, projected))
    far = lax.ppermute(near, "core", swap)
    near, table_new, accum_new = lax.optimization_barrier((near, table_new, accum_new))
    table_new, accum_new = store(table_new, accum_new)
    refreshed = refresh(core, cache[0], near)
    far, table_new, accum_new = lax.optimization_barrier((far, table_new, accum_new))
    refreshed = refresh(core, cache[0], far, done=refreshed)

    return (
        projected[None, None],
        table_new[None, None],
        accum_new[None, None],
        refreshed.reshape(1, slots, width),
    )


def solution(mesh):
    chips = Mesh(mesh.devices.reshape(4, 12, 8, 2), ("x", "z", "y", "core"))
    return jax.shard_map(
        shards,
        mesh=chips,
        in_specs=(
            P(OWN, None, None),
            P(OWN, None, None),
            P(OWN, None, None, None),
            P(OWN, GRP, None),
            P(OWN, GRP, None),
            P(),
            P(OWN, GRP, None, None),
            P(OWN, GRP, None, None),
            P(OWN, GRP, None, None),
            P(OWN, GRP, None, None),
        ),
        out_specs=(
            P(OWN, GRP, None, None),
            P(OWN, GRP, None, None),
            P(OWN, GRP, None, None),
            P(OWN, None, None),
        ),
        check_vma=False,
    )
```

```python
import functools

import jax
import jax.numpy as jnp
from jax import lax
from jax.experimental import pallas as pl
from jax.experimental.pallas import tpu as pltpu
from jax.sharding import Mesh
from jax.sharding import PartitionSpec as P

learn_rate = 0.3
epsilon = 1e-06
LOOKUP_ROWS = 16
LENGTH_ROWS = 2
OWN = ("x", "z")
GRP = ("y", "core")
STEP = 4
VMEM_BYTES = 40 * 1024 * 1024


def split(values):
    high = values.astype(jnp.bfloat16)
    low = (values - high.astype(jnp.float32)).astype(jnp.bfloat16)
    return jnp.concatenate([high, low], axis=1)


def joined(values):
    width = values.shape[1] // 2
    return values[:, :width] + values[:, width:]


def row_of(ref, first, count):
    return jnp.concatenate([ref[r : r + 1, :] for r in range(first, first + count)], axis=1)


def bag_hot(lengths):
    bags = lengths.shape[1]
    before = lax.broadcasted_iota(jnp.int32, (bags, bags), 0)
    after = lax.broadcasted_iota(jnp.int32, (bags, bags), 1)
    upper = jnp.where(before <= after, 1.0, 0.0).astype(jnp.bfloat16)
    tall = jnp.broadcast_to(lengths, (8, bags)).astype(jnp.bfloat16)
    ends = jnp.dot(tall, upper, preferred_element_type=jnp.float32)[0:1, :]
    starts = ends - lengths
    ends = ends.astype(jnp.int32)
    starts = starts.astype(jnp.int32)
    position = lax.broadcasted_iota(jnp.int32, (LOOKUP_ROWS * 128, bags), 0)
    inside = (position >= starts) & (position < ends)
    return jnp.where(inside, 1.0, 0.0).astype(jnp.bfloat16)


def slot_parts(lookup, span, groups):
    group = jnp.zeros_like(lookup)
    for k in range(1, groups):
        group = group + jnp.where(lookup >= k * span, 1, 0)
    place = lookup - group * span
    rows = lax.broadcasted_iota(jnp.int32, (span, lookup.shape[1]), 0)
    hot = jnp.where(rows == place, 1.0, 0.0).astype(jnp.bfloat16)
    return group, hot


def in_group(group, k):
    return jnp.where(group == k, 1.0, 0.0).astype(jnp.bfloat16)


def pack_kernel(lookup_hbm, length_hbm, cotangent_hbm, projection_hbm, out_ref, lookup, length, cotangent, projection, arrived):
    bags = cotangent.shape[0]
    sources = (lookup_hbm, length_hbm, cotangent_hbm, projection_hbm)
    copies = [
        pltpu.make_async_copy(source, target, arrived.at[i])
        for i, (source, target) in enumerate(zip(sources, (lookup, length, cotangent, projection)))
    ]
    for copy in copies:
        copy.start()
    for copy in copies:
        copy.wait()
    out_ref[:bags, :] = lax.dot_general(
        cotangent[...],
        projection[...],
        (((1,), (1,)), ((), ())),
        preferred_element_type=jnp.float32,
    )
    out_ref[bags : bags + LOOKUP_ROWS, :] = lookup[...].astype(jnp.float32)
    tail = jnp.zeros((8 - LENGTH_ROWS, 128), jnp.float32)
    out_ref[bags + LOOKUP_ROWS :, :] = jnp.concatenate(
        [length[...].astype(jnp.float32), tail], axis=0
    )


def unpack(packed_ref):
    bags = packed_ref.shape[0] - LOOKUP_ROWS - 8
    lookup = row_of(packed_ref, bags, LOOKUP_ROWS).astype(jnp.int32)
    return lookup, row_of(packed_ref, bags + LOOKUP_ROWS, LENGTH_ROWS)


def slot_parts_of(core_ref, packed_ref, chips, span, step):
    core = core_ref[0]
    lookup, lengths = unpack(packed_ref)
    bags = lengths.shape[1]
    rows = jnp.dot(
        bag_hot(lengths), split(packed_ref[:bags, :]), preferred_element_type=jnp.float32
    ).astype(jnp.bfloat16)
    group, hot = slot_parts(lookup, span, 2 * chips)
    for y in range(0, chips, step):
        slots = jnp.concatenate(
            [hot * in_group(group, 2 * j + core) for j in range(y, y + step)], axis=0
        )
        delta = joined(jnp.dot(slots, rows, preferred_element_type=jnp.float32))
        yield pl.ds(y, step), delta.reshape(step, span, delta.shape[1])


def own_kernel(core_ref, packed_ref, out_ref):
    chips, span, _ = out_ref.shape
    for place, delta in slot_parts_of(core_ref, packed_ref, chips, span, STEP):
        out_ref[place, :, :] = delta


def both_kernel(core_ref, packed_ref, start_ref, out_ref):
    chips, span, _ = out_ref.shape
    for place, delta in slot_parts_of(core_ref, packed_ref, chips, span, STEP):
        out_ref[place, :, :] = start_ref[place, :, :] + delta


def turned(values, width):
    rows, columns = values.shape
    tall = jnp.concatenate([values, jnp.zeros((8 - rows, columns), values.dtype)], axis=0)
    lane = lax.broadcasted_iota(jnp.int32, (8, width), 1)
    unit = jnp.where(lax.broadcasted_iota(jnp.int32, (8, width), 0) == lane, 1.0, 0.0)
    return lax.dot_general(
        tall.astype(jnp.float32).astype(jnp.bfloat16),
        unit.astype(jnp.bfloat16),
        (((0,), (0,)), ((), ())),
        preferred_element_type=jnp.float32,
    )


def pool_kernel(core_ref, packed_ref, cache_ref, projection_ref, *refs, turn):
    out_hbm, count_ref, ready, sent = refs[-4:]

    @pl.when(core_ref[0] == turn)
    def _():
        slots = cache_ref.shape[0]
        span = 192
        groups = slots // span
        lookup, lengths = unpack(packed_ref)
        bags = bag_hot(lengths)
        group, hot = slot_parts(lookup, span, groups)
        for k in range(0, groups, STEP):
            chosen = jnp.concatenate([hot * in_group(group, j) for j in range(k, k + STEP)], axis=0)
            count = jnp.dot(chosen, bags, preferred_element_type=jnp.float32)
            count_ref[k * span : (k + STEP) * span, :] = count.astype(jnp.bfloat16)
        pooled = lax.dot_general(
            count_ref[...],
            split(cache_ref[...]),
            (((0,), (0,)), ((), ())),
            preferred_element_type=jnp.float32,
        )
        pooled = joined(pooled).astype(jnp.bfloat16)
        ready[...] = jnp.dot(
            pooled, projection_ref[...], preferred_element_type=jnp.float32
        ).astype(jnp.bfloat16)
        copy = pltpu.make_async_copy(ready, out_hbm, sent.at[0])
        copy.start()
        copy.wait()


def early_kernel(
    core_ref, grp_ref, packed_ref, cache_ref, projection_ref, hot_ref, stale_ref, counts_ref,
    out_hbm, ids_ref, flags_ref, live_ref, *scratch
):
    _, capacity, owners = hot_ref.shape
    width = ids_ref.shape[1]
    ids = hot_ref[grp_ref[0], :, :]
    ids_ref[...] = 16.0 * turned(lax.shift_right_logical(ids, 4), width) + turned(ids & 15, width)
    flags_ref[...] = turned(stale_ref[...], width)
    place = lax.broadcasted_iota(jnp.int32, (owners * capacity, owners), 0) - (
        capacity * lax.broadcasted_iota(jnp.int32, (owners * capacity, owners), 1)
    )
    counts = counts_ref[pl.ds(grp_ref[0], 1), :]
    live = jnp.where((place >= 0) & (place < counts), 1.0, 0.0).astype(jnp.bfloat16)
    ones = jnp.ones((owners, width), jnp.bfloat16)
    live_ref[...] = jnp.dot(live, ones, preferred_element_type=jnp.float32)
    pool_kernel(core_ref, packed_ref, cache_ref, projection_ref, out_hbm, *scratch, turn=1)


def combine_kernel(parts_ref, ids_ref, out_ref):
    owners, _ = ids_ref.shape
    capacity = parts_ref.shape[1] // owners
    out_ref[pl.ds(capacity, owners, stride=capacity + 1), :] = ids_ref[...]
    for c in range(capacity):
        rows = pl.ds(c, owners, stride=capacity)
        total = parts_ref[0, rows, :]
        for y in range(1, parts_ref.shape[0]):
            total = total + parts_ref[y, rows, :]
        out_ref[pl.ds(c, owners, stride=capacity + 1), :] = total


def owner_kernel(
    incoming_ref, stale_ref, table_ref, accum_ref, table_new_ref, accum_new_ref, change_ref
):
    holders = stale_ref.shape[0]
    capacity = incoming_ref.shape[0] // holders - 1
    table_rows = table_ref.shape[0]

    def taken(c):
        return incoming_ref[pl.ds(c, holders, stride=capacity + 1), :]

    ids = taken(capacity)[:, :capacity].astype(jnp.int32)
    stale = stale_ref[...]
    row = lax.broadcasted_iota(jnp.int32, (holders, table_rows), 1)
    hot = [jnp.where(row == ids[:, c : c + 1], 1.0, 0.0) for c in range(capacity)]
    wanted = [hot[c] * stale[:, c : c + 1] for c in range(capacity)]
    incoming = jnp.concatenate([taken(c) for c in range(capacity)], axis=0)
    gradient = joined(
        lax.dot_general(
            jnp.concatenate(hot, axis=0).astype(jnp.bfloat16),
            split(incoming),
            (((0,), (0,)), ((), ())),
            preferred_element_type=jnp.float32,
        )
    )
    accum_new = accum_ref[...] + gradient * gradient
    accum_new_ref[...] = accum_new
    old = table_ref[...]
    new = old - learn_rate * gradient / (jnp.sqrt(accum_new) + epsilon)
    table_new_ref[...] = new
    change = joined(
        jnp.dot(
            jnp.concatenate(wanted, axis=0).astype(jnp.bfloat16),
            split(new - old),
            preferred_element_type=jnp.float32,
        )
    )
    for c in range(capacity):
        change_ref[pl.ds(c, holders, stride=capacity), :] = change[
            c * holders : (c + 1) * holders, :
        ]


def spread_kernel(change_ref, live_ref, out_ref):
    change = jnp.where(live_ref[...] > 0.5, change_ref[...], 0.0)
    for y in range(out_ref.shape[0]):
        out_ref[y, :, :] = change


def store_kernel(*refs):
    count = len(refs) // 2
    sent = refs[-1]
    copies = [
        pltpu.make_async_copy(refs[i], refs[count + i], sent.at[i]) for i in range(count)
    ]
    for copy in copies:
        copy.start()
    for copy in copies:
        copy.wait()


def refresh_kernel(core_ref, cache_ref, change_ref, *refs, flip):
    out_hbm, ready, sent = refs[-3:]
    chips = change_ref.shape[0]
    core = 1 - core_ref[0] if flip else core_ref[0]
    copies = []
    for y in range(chips):
        ready[y, :, :] = cache_ref[y, core, :, :] + change_ref[y, :, :]
        copies.append(pltpu.make_async_copy(ready.at[y], out_hbm.at[y, core], sent.at[y]))
        copies[-1].start()
    for copy in copies:
        copy.wait()


def params():
    return pltpu.CompilerParams(vmem_limit_bytes=VMEM_BYTES)


def near_by(array):
    return pltpu.with_memory_space_constraint(array, pltpu.VMEM)


def cost(flops, moved):
    return pl.CostEstimate(flops=flops, bytes_accessed=moved, transcendentals=0)


def pack(lookup, lengths, cotangent, projection):
    rows = cotangent.shape[0] + LOOKUP_ROWS + 8
    given = (lookup, lengths, cotangent, projection)
    held = [pltpu.with_memory_space_constraint(a, pltpu.HBM) for a in given]
    return pl.pallas_call(
        pack_kernel,
        out_shape=pltpu.VMEM((rows, projection.shape[0]), jnp.float32),
        in_specs=[pl.BlockSpec(memory_space=pltpu.HBM)] * 4,
        out_specs=pl.BlockSpec(memory_space=pltpu.VMEM),
        scratch_shapes=[pltpu.VMEM(a.shape, a.dtype) for a in given]
        + [pltpu.SemaphoreType.DMA((4,))],
        compiler_params=params(),
        cost_estimate=cost(2 * 256 * 256 * 128, 400000),
        name="pack",
    )(*held)


def own_slots(core, packed, chips, span):
    vmem = pl.BlockSpec(memory_space=pltpu.VMEM)
    return pl.pallas_call(
        own_kernel,
        out_shape=pltpu.VMEM((chips, span, packed.shape[1]), jnp.float32),
        in_specs=[pl.BlockSpec(memory_space=pltpu.SMEM), vmem],
        out_specs=vmem,
        compiler_params=params(),
        cost_estimate=cost(3072 * 2048 * 256, 1000000),
        name="own_slots",
    )(core, near_by(packed))


def both_slots(core, packed, start):
    vmem = pl.BlockSpec(memory_space=pltpu.VMEM)
    return pl.pallas_call(
        both_kernel,
        out_shape=pltpu.VMEM(start.shape, jnp.float32),
        in_specs=[pl.BlockSpec(memory_space=pltpu.SMEM), vmem, vmem],
        out_specs=vmem,
        compiler_params=params(),
        cost_estimate=cost(3072 * 2048 * 256, 1800000),
        name="both_slots",
    )(core, near_by(packed), near_by(start))


def pool_scratch(cache_rows, projection, bags):
    return [
        pltpu.VMEM((cache_rows.shape[0], bags), jnp.bfloat16),
        pltpu.VMEM((bags, projection.shape[1]), jnp.bfloat16),
        pltpu.SemaphoreType.DMA((1,)),
    ]


def pool_early(core, grp, packed, cache_rows, projection, hot, stale, counts):
    bags = packed.shape[0] - LOOKUP_ROWS - 8
    _, capacity, owners = hot.shape
    width = cache_rows.shape[1]
    vmem = pl.BlockSpec(memory_space=pltpu.VMEM)
    smem = pl.BlockSpec(memory_space=pltpu.SMEM)
    given = (packed, cache_rows, projection, hot, stale, counts)
    return pl.pallas_call(
        early_kernel,
        out_shape=(
            pltpu.HBM((bags, projection.shape[1]), jnp.bfloat16),
            pltpu.VMEM((owners, width), jnp.float32),
            pltpu.VMEM((owners, width), jnp.float32),
            pltpu.VMEM((owners * capacity, width), jnp.float32),
        ),
        in_specs=[smem, smem] + [vmem] * len(given),
        out_specs=(pl.BlockSpec(memory_space=pltpu.HBM), vmem, vmem, vmem),
        scratch_shapes=pool_scratch(cache_rows, projection, bags),
        compiler_params=params(),
        cost_estimate=cost(2 * 3072 * 2048 * 256, 2000000),
        name="pool_early",
    )(core, grp, *[near_by(a) for a in given])


def pool_late(core, packed, cache_rows, projection, done):
    bags = packed.shape[0] - LOOKUP_ROWS - 8
    vmem = pl.BlockSpec(memory_space=pltpu.VMEM)
    hbm = pl.BlockSpec(memory_space=pltpu.HBM)
    return pl.pallas_call(
        functools.partial(pool_kernel, turn=0),
        out_shape=pltpu.HBM((bags, projection.shape[1]), jnp.bfloat16),
        in_specs=[pl.BlockSpec(memory_space=pltpu.SMEM), vmem, vmem, vmem, hbm],
        out_specs=hbm,
        scratch_shapes=pool_scratch(cache_rows, projection, bags),
        input_output_aliases={4: 0},
        compiler_params=params(),
        cost_estimate=cost(2 * 3072 * 2048 * 256, 2000000),
        name="pool_late",
    )(core, near_by(packed), near_by(cache_rows), near_by(projection), done)


def combine(parts, ids):
    chips, span, width = parts.shape
    return pl.pallas_call(
        combine_kernel,
        out_shape=pltpu.VMEM((span + ids.shape[0], width), jnp.float32),
        compiler_params=params(),
        cost_estimate=cost(200000, 900000),
        name="combine",
    )(near_by(parts), near_by(ids))


def owner(incoming, stale, table, accum):
    table_like = pltpu.VMEM(table.shape, jnp.float32)
    rows = incoming.shape[0] - stale.shape[0]
    change = pltpu.VMEM((rows, table.shape[1]), jnp.float32)
    return pl.pallas_call(
        owner_kernel,
        out_shape=(table_like, table_like, change),
        compiler_params=params(),
        cost_estimate=cost(4 * 512 * 192 * 256, 1300000),
        name="owner",
    )(*[near_by(a) for a in (incoming, stale, table, accum)])


def store(*arrays):
    count = len(arrays)
    return pl.pallas_call(
        store_kernel,
        out_shape=tuple(pltpu.HBM(a.shape, a.dtype) for a in arrays),
        in_specs=[pl.BlockSpec(memory_space=pltpu.VMEM)] * count,
        out_specs=(pl.BlockSpec(memory_space=pltpu.HBM),) * count,
        scratch_shapes=[pltpu.SemaphoreType.DMA((count,))],
        compiler_params=params(),
        cost_estimate=cost(0, 2 * sum(4 * a.size for a in arrays)),
        name="store",
    )(*[near_by(a) for a in arrays])


def spread(change, live, chips):
    return pl.pallas_call(
        spread_kernel,
        out_shape=pltpu.VMEM((chips,) + change.shape, jnp.float32),
        compiler_params=params(),
        cost_estimate=cost(200000, 900000),
        name="spread",
    )(near_by(change), near_by(live))


def refresh(core, cache_rows, change, done=None):
    flip = done is not None
    chips, span, width = change.shape
    vmem = pl.BlockSpec(memory_space=pltpu.VMEM)
    hbm = pl.BlockSpec(memory_space=pltpu.HBM)
    args = [core, near_by(cache_rows.reshape(chips, 2, span, width)), near_by(change)]
    args = args + ([done] if flip else [])
    return pl.pallas_call(
        functools.partial(refresh_kernel, flip=flip),
        out_shape=jax.ShapeDtypeStruct((chips, 2, span, width), jnp.float32),
        in_specs=[pl.BlockSpec(memory_space=pltpu.SMEM), vmem, vmem] + ([hbm] if flip else []),
        out_specs=hbm,
        scratch_shapes=[
            pltpu.VMEM((chips, span, width), jnp.float32),
            pltpu.SemaphoreType.DMA((chips,)),
        ],
        input_output_aliases={3: 0} if flip else {},
        compiler_params=params(),
        cost_estimate=cost(400000, 2400000),
        name="refresh_other" if flip else "refresh_mine",
    )(*args)


def shards(
    cache, counts, hot_rows, lookups, bag_lengths, projection, grad_out, table, accum, stale
):
    n_own = hot_rows.shape[2]
    chips = lax.axis_size("y")
    capacity = hot_rows.shape[3]
    slots, width = cache.shape[1:]
    span = n_own * capacity
    lookup = lookups.reshape(LOOKUP_ROWS, 128)
    lengths = bag_lengths.reshape(LENGTH_ROWS, 128)
    core = lax.axis_index("core").astype(jnp.int32).reshape(1)
    grp = lax.axis_index(GRP).astype(jnp.int32).reshape(1)
    swap = [(0, 1), (1, 0)]

    mine = pack(lookup, lengths, grad_out[0, 0], projection)
    other = lax.ppermute(mine, "core", swap)
    half = both_slots(core, other, own_slots(core, mine, chips, span))
    half, late = lax.optimization_barrier((half, mine))
    projected, ids, flags, live = pool_early(
        core,
        grp,
        late,
        cache[0],
        projection,
        hot_rows[0].transpose(0, 2, 1),
        stale[0, 0].T,
        counts[0],
    )
    half, projected, ids, flags, live = lax.optimization_barrier(
        (half, projected, ids, flags, live)
    )
    parts = lax.all_to_all(half, "y", split_axis=0, concat_axis=0, tiled=True)
    summed = combine(parts, ids)
    summed = summed.reshape(-1, 1, width)
    incoming = lax.all_to_all(summed, OWN, split_axis=0, concat_axis=0, tiled=True)
    incoming = incoming.reshape(-1, width)
    table_new, accum_new, change = owner(incoming, flags, table[0, 0], accum[0, 0])

    returned = lax.all_to_all(
        change.reshape(n_own, capacity, width), OWN, split_axis=0, concat_axis=0, tiled=True
    )
    wide = spread(returned.reshape(span, width), live, chips)
    near = lax.all_to_all(wide, "y", split_axis=0, concat_axis=0, tiled=True)
    near, projected, late = lax.optimization_barrier((near, projected, late))
    projected = pool_late(core, late, cache[0], projection, projected)
    near, projected = lax.optimization_barrier((near, projected))
    far = lax.ppermute(near, "core", swap)
    near, table_new, accum_new = lax.optimization_barrier((near, table_new, accum_new))
    table_new, accum_new = store(table_new, accum_new)
    refreshed = refresh(core, cache[0], near)
    far, table_new, accum_new = lax.optimization_barrier((far, table_new, accum_new))
    refreshed = refresh(core, cache[0], far, done=refreshed)

    return (
        projected[None, None],
        table_new[None, None],
        accum_new[None, None],
        refreshed.reshape(1, slots, width),
    )


def solution(mesh):
    chips = Mesh(mesh.devices.reshape(4, 12, 8, 2), ("x", "z", "y", "core"))
    return jax.shard_map(
        shards,
        mesh=chips,
        in_specs=(
            P(OWN, None, None),
            P(OWN, None, None),
            P(OWN, None, None, None),
            P(OWN, GRP, None),
            P(OWN, GRP, None),
            P(),
            P(OWN, GRP, None, None),
            P(OWN, GRP, None, None),
            P(OWN, GRP, None, None),
            P(OWN, GRP, None, None),
        ),
        out_specs=(
            P(OWN, GRP, None, None),
            P(OWN, GRP, None, None),
            P(OWN, GRP, None, None),
            P(OWN, None, None),
        ),
        check_vma=False,
    )
```

```python
import functools

import jax
import jax.numpy as jnp
from jax import lax
from jax.experimental import pallas as pl
from jax.experimental.pallas import tpu as pltpu
from jax.sharding import Mesh
from jax.sharding import PartitionSpec as P

learn_rate = 0.3
epsilon = 1e-06
LOOKUP_ROWS = 16
LENGTH_ROWS = 2
OWN = ("x", "z")
GRP = ("y", "core")
STEP = 4
VMEM_BYTES = 40 * 1024 * 1024


def split(values):
    high = values.astype(jnp.bfloat16)
    low = (values - high.astype(jnp.float32)).astype(jnp.bfloat16)
    return jnp.concatenate([high, low], axis=1)


def joined(values):
    width = values.shape[1] // 2
    return values[:, :width] + values[:, width:]


def row_of(ref, first, count):
    return jnp.concatenate([ref[r : r + 1, :] for r in range(first, first + count)], axis=1)


def bag_hot(lengths):
    bags = lengths.shape[1]
    before = lax.broadcasted_iota(jnp.int32, (bags, bags), 0)
    after = lax.broadcasted_iota(jnp.int32, (bags, bags), 1)
    upper = jnp.where(before <= after, 1.0, 0.0).astype(jnp.bfloat16)
    tall = jnp.broadcast_to(lengths, (8, bags)).astype(jnp.bfloat16)
    ends = jnp.dot(tall, upper, preferred_element_type=jnp.float32)[0:1, :]
    starts = ends - lengths
    ends = ends.astype(jnp.int32)
    starts = starts.astype(jnp.int32)
    position = lax.broadcasted_iota(jnp.int32, (LOOKUP_ROWS * 128, bags), 0)
    inside = (position >= starts) & (position < ends)
    return jnp.where(inside, 1.0, 0.0).astype(jnp.bfloat16)


def slot_parts(lookup, span, groups):
    group = jnp.zeros_like(lookup)
    for k in range(1, groups):
        group = group + jnp.where(lookup >= k * span, 1, 0)
    place = lookup - group * span
    rows = lax.broadcasted_iota(jnp.int32, (span, lookup.shape[1]), 0)
    hot = jnp.where(rows == place, 1.0, 0.0).astype(jnp.bfloat16)
    return group, hot


def in_group(group, k):
    return jnp.where(group == k, 1.0, 0.0).astype(jnp.bfloat16)


def first_kernel(
    core_ref, lookup_hbm, length_hbm, cotangent_hbm, projection_hbm,
    packed_ref, given_ref, start_ref,
    lookup, length, cotangent, projection, arrived,
):
    chips, span, _ = start_ref.shape
    bags = cotangent.shape[0]
    sources = (lookup_hbm, length_hbm, cotangent_hbm, projection_hbm)
    copies = [
        pltpu.make_async_copy(source, target, arrived.at[i])
        for i, (source, target) in enumerate(zip(sources, (lookup, length, cotangent, projection)))
    ]
    for copy in copies:
        copy.start()
    for copy in copies:
        copy.wait()
    packed_ref[:bags, :] = lax.dot_general(
        cotangent[...],
        projection[...],
        (((1,), (1,)), ((), ())),
        preferred_element_type=jnp.float32,
    )
    packed_ref[bags : bags + LOOKUP_ROWS, :] = lookup[...].astype(jnp.float32)
    tail = jnp.zeros((8 - LENGTH_ROWS, 128), jnp.float32)
    packed_ref[bags + LOOKUP_ROWS :, :] = jnp.concatenate(
        [length[...].astype(jnp.float32), tail], axis=0
    )

    @pl.when(core_ref[0] == 0)
    def _():
        for place, delta in slot_parts_of(1, packed_ref, chips, span, STEP):
            given_ref[place, :, :] = delta

    @pl.when(core_ref[0] == 1)
    def _():
        rest = packed_ref.shape[0] - span
        given_ref[0, :, :] = packed_ref[:span, :]
        given_ref[1, :rest, :] = packed_ref[span:, :]
        for place, delta in slot_parts_of(1, packed_ref, chips, span, STEP):
            start_ref[place, :, :] = delta


def unpack(packed_ref):
    bags = packed_ref.shape[0] - LOOKUP_ROWS - 8
    lookup = row_of(packed_ref, bags, LOOKUP_ROWS).astype(jnp.int32)
    return lookup, row_of(packed_ref, bags + LOOKUP_ROWS, LENGTH_ROWS)


def slot_parts_of(core, packed_ref, chips, span, step):
    lookup, lengths = unpack(packed_ref)
    bags = lengths.shape[1]
    rows = jnp.dot(
        bag_hot(lengths), split(packed_ref[:bags, :]), preferred_element_type=jnp.float32
    ).astype(jnp.bfloat16)
    group, hot = slot_parts(lookup, span, 2 * chips)
    for y in range(0, chips, step):
        slots = jnp.concatenate(
            [hot * in_group(group, 2 * j + core) for j in range(y, y + step)], axis=0
        )
        delta = joined(jnp.dot(slots, rows, preferred_element_type=jnp.float32))
        yield pl.ds(y, step), delta.reshape(step, span, delta.shape[1])


def own_kernel(
    core_ref, grp_ref, packed_ref, hot_ref, stale_ref, counts_ref,
    out_ref, ids_ref, flags_ref, live_ref,
):
    chips, span, width = out_ref.shape
    _, capacity, owners = hot_ref.shape
    ids = hot_ref[grp_ref[0], :, :]
    ids_ref[...] = 16.0 * turned(lax.shift_right_logical(ids, 4), width) + turned(ids & 15, width)
    flags_ref[...] = turned(stale_ref[...], width)
    place = lax.broadcasted_iota(jnp.int32, (span, owners), 0) - (
        capacity * lax.broadcasted_iota(jnp.int32, (span, owners), 1)
    )
    counts = counts_ref[pl.ds(grp_ref[0], 1), :]
    live = jnp.where((place >= 0) & (place < counts), 1.0, 0.0).astype(jnp.bfloat16)
    ones = jnp.ones((owners, width), jnp.bfloat16)
    live_ref[...] = jnp.dot(live, ones, preferred_element_type=jnp.float32)

    @pl.when(core_ref[0] == 0)
    def _():
        for place, delta in slot_parts_of(0, packed_ref, chips, span, STEP):
            out_ref[place, :, :] = delta


def both_kernel(core_ref, taken_ref, own_ref, start_ref, out_ref, packed):
    chips, span, _ = out_ref.shape

    @pl.when(core_ref[0] == 0)
    def _():
        packed[:span, :] = taken_ref[0, :, :]
        packed[span:, :] = taken_ref[1, : packed.shape[0] - span, :]
        for place, delta in slot_parts_of(0, packed, chips, span, STEP):
            out_ref[place, :, :] = own_ref[place, :, :] + delta

    @pl.when(core_ref[0] == 1)
    def _():
        out_ref[...] = start_ref[...] + taken_ref[...]


def turned(values, width):
    rows, columns = values.shape
    tall = jnp.concatenate([values, jnp.zeros((8 - rows, columns), values.dtype)], axis=0)
    lane = lax.broadcasted_iota(jnp.int32, (8, width), 1)
    unit = jnp.where(lax.broadcasted_iota(jnp.int32, (8, width), 0) == lane, 1.0, 0.0)
    return lax.dot_general(
        tall.astype(jnp.float32).astype(jnp.bfloat16),
        unit.astype(jnp.bfloat16),
        (((0,), (0,)), ((), ())),
        preferred_element_type=jnp.float32,
    )


def pool_kernel(core_ref, packed_ref, cache_hbm, projection_hbm, *refs, turn):
    out_hbm, count_ref, ready, cache_ref, projection_ref, moved = refs[-6:]

    @pl.when(core_ref[0] == turn)
    def _():
        copies = [
            pltpu.make_async_copy(cache_hbm, cache_ref, moved.at[0]),
            pltpu.make_async_copy(projection_hbm, projection_ref, moved.at[1]),
        ]
        for copy in copies:
            copy.start()
        slots = cache_ref.shape[0]
        span = 192
        groups = slots // span
        lookup, lengths = unpack(packed_ref)
        bags = bag_hot(lengths)
        group, hot = slot_parts(lookup, span, groups)
        for k in range(0, groups, STEP):
            chosen = jnp.concatenate([hot * in_group(group, j) for j in range(k, k + STEP)], axis=0)
            count = jnp.dot(chosen, bags, preferred_element_type=jnp.float32)
            count_ref[k * span : (k + STEP) * span, :] = count.astype(jnp.bfloat16)
        for copy in copies:
            copy.wait()
        pooled = lax.dot_general(
            count_ref[...],
            split(cache_ref[...]),
            (((0,), (0,)), ((), ())),
            preferred_element_type=jnp.float32,
        )
        pooled = joined(pooled).astype(jnp.bfloat16)
        ready[...] = jnp.dot(
            pooled, projection_ref[...], preferred_element_type=jnp.float32
        ).astype(jnp.bfloat16)
        copy = pltpu.make_async_copy(ready, out_hbm, moved.at[2])
        copy.start()
        copy.wait()


def combine_kernel(parts_ref, ids_ref, out_ref):
    owners, _ = ids_ref.shape
    capacity = parts_ref.shape[1] // owners
    out_ref[pl.ds(capacity, owners, stride=capacity + 1), :] = ids_ref[...]
    for c in range(capacity):
        rows = pl.ds(c, owners, stride=capacity)
        total = parts_ref[0, rows, :]
        for y in range(1, parts_ref.shape[0]):
            total = total + parts_ref[y, rows, :]
        out_ref[pl.ds(c, owners, stride=capacity + 1), :] = total


def owner_kernel(
    incoming_ref, stale_ref, table_ref, accum_ref, table_new_ref, accum_new_ref, change_ref
):
    holders = stale_ref.shape[0]
    capacity = incoming_ref.shape[0] // holders - 1
    table_rows = table_ref.shape[0]

    def taken(c):
        return incoming_ref[pl.ds(c, holders, stride=capacity + 1), :]

    ids = taken(capacity)[:, :capacity].astype(jnp.int32)
    stale = stale_ref[...]
    row = lax.broadcasted_iota(jnp.int32, (holders, table_rows), 1)
    hot = [jnp.where(row == ids[:, c : c + 1], 1.0, 0.0) for c in range(capacity)]
    wanted = [hot[c] * stale[:, c : c + 1] for c in range(capacity)]
    incoming = jnp.concatenate([taken(c) for c in range(capacity)], axis=0)
    gradient = joined(
        lax.dot_general(
            jnp.concatenate(hot, axis=0).astype(jnp.bfloat16),
            split(incoming),
            (((0,), (0,)), ((), ())),
            preferred_element_type=jnp.float32,
        )
    )
    accum_new = accum_ref[...] + gradient * gradient
    accum_new_ref[...] = accum_new
    old = table_ref[...]
    new = old - learn_rate * gradient / (jnp.sqrt(accum_new) + epsilon)
    table_new_ref[...] = new
    change = joined(
        jnp.dot(
            jnp.concatenate(wanted, axis=0).astype(jnp.bfloat16),
            split(new - old),
            preferred_element_type=jnp.float32,
        )
    )
    for c in range(capacity):
        change_ref[pl.ds(c, holders, stride=capacity), :] = change[
            c * holders : (c + 1) * holders, :
        ]


def spread_kernel(change_ref, live_ref, out_ref):
    change = jnp.where(live_ref[...] > 0.5, change_ref[...], 0.0)
    for y in range(out_ref.shape[0]):
        out_ref[y, :, :] = change


def store_kernel(*refs):
    count = len(refs) // 2
    sent = refs[-1]
    copies = [
        pltpu.make_async_copy(refs[i], refs[count + i], sent.at[i]) for i in range(count)
    ]
    for copy in copies:
        copy.start()
    for copy in copies:
        copy.wait()


def refresh_kernel(core_ref, cache_ref, change_ref, *refs, flip):
    out_hbm, ready, sent = refs[-3:]
    chips = change_ref.shape[0]
    core = 1 - core_ref[0] if flip else core_ref[0]
    copies = []
    for y in range(chips):
        ready[y, :, :] = cache_ref[y, core, :, :] + change_ref[y, :, :]
        copies.append(pltpu.make_async_copy(ready.at[y], out_hbm.at[y, core], sent.at[y]))
        copies[-1].start()
    for copy in copies:
        copy.wait()


def params():
    return pltpu.CompilerParams(vmem_limit_bytes=VMEM_BYTES)


def near_by(array):
    return pltpu.with_memory_space_constraint(array, pltpu.VMEM)


def cost(flops, moved):
    return pl.CostEstimate(flops=flops, bytes_accessed=moved, transcendentals=0)


def first_slots(core, lookup, lengths, cotangent, projection, chips, span):
    rows = cotangent.shape[0] + LOOKUP_ROWS + 8
    width = projection.shape[0]
    given = (lookup, lengths, cotangent, projection)
    held = [pltpu.with_memory_space_constraint(a, pltpu.HBM) for a in given]
    return pl.pallas_call(
        first_kernel,
        out_shape=(
            pltpu.VMEM((rows, width), jnp.float32),
            pltpu.VMEM((chips, span, width), jnp.float32),
            pltpu.VMEM((chips, span, width), jnp.float32),
        ),
        in_specs=[pl.BlockSpec(memory_space=pltpu.SMEM)]
        + [pl.BlockSpec(memory_space=pltpu.HBM)] * 4,
        out_specs=(pl.BlockSpec(memory_space=pltpu.VMEM),) * 3,
        scratch_shapes=[pltpu.VMEM(a.shape, a.dtype) for a in given]
        + [pltpu.SemaphoreType.DMA((4,))],
        compiler_params=params(),
        cost_estimate=cost(3072 * 2048 * 256, 1000000),
        name="first_slots",
    )(core, *held)


def own_slots(core, grp, packed, chips, hot, stale, counts):
    _, capacity, owners = hot.shape
    span, width = capacity * owners, packed.shape[1]
    vmem = pl.BlockSpec(memory_space=pltpu.VMEM)
    smem = pl.BlockSpec(memory_space=pltpu.SMEM)
    given = (packed, hot, stale, counts)
    return pl.pallas_call(
        own_kernel,
        out_shape=(
            pltpu.VMEM((chips, span, width), jnp.float32),
            pltpu.VMEM((owners, width), jnp.float32),
            pltpu.VMEM((owners, width), jnp.float32),
            pltpu.VMEM((span, width), jnp.float32),
        ),
        in_specs=[smem, smem] + [vmem] * len(given),
        out_specs=(vmem,) * 4,
        compiler_params=params(),
        cost_estimate=cost(3072 * 2048 * 256, 1000000),
        name="own_slots",
    )(core, grp, *[near_by(a) for a in given])


def both_slots(core, taken, own, start, rows):
    vmem = pl.BlockSpec(memory_space=pltpu.VMEM)
    return pl.pallas_call(
        both_kernel,
        out_shape=pltpu.VMEM(start.shape, jnp.float32),
        in_specs=[pl.BlockSpec(memory_space=pltpu.SMEM), vmem, vmem, vmem],
        out_specs=vmem,
        scratch_shapes=[pltpu.VMEM((rows, start.shape[2]), jnp.float32)],
        compiler_params=params(),
        cost_estimate=cost(3072 * 2048 * 256, 1800000),
        name="both_slots",
    )(core, near_by(taken), near_by(own), near_by(start))


def pool(core, packed, cache_rows, projection, turn, done=None):
    bags = packed.shape[0] - LOOKUP_ROWS - 8
    out = pltpu.HBM((bags, projection.shape[1]), jnp.bfloat16)
    hbm = pl.BlockSpec(memory_space=pltpu.HBM)
    held = [cache_rows, projection] + ([] if done is None else [done])
    return pl.pallas_call(
        functools.partial(pool_kernel, turn=turn),
        out_shape=out,
        in_specs=[
            pl.BlockSpec(memory_space=pltpu.SMEM),
            pl.BlockSpec(memory_space=pltpu.VMEM),
        ]
        + [hbm] * len(held),
        out_specs=hbm,
        scratch_shapes=[
            pltpu.VMEM((cache_rows.shape[0], bags), jnp.bfloat16),
            pltpu.VMEM(out.shape, jnp.bfloat16),
            pltpu.VMEM(cache_rows.shape, cache_rows.dtype),
            pltpu.VMEM(projection.shape, projection.dtype),
            pltpu.SemaphoreType.DMA((3,)),
        ],
        input_output_aliases={} if done is None else {4: 0},
        compiler_params=params(),
        cost_estimate=cost(2 * 3072 * 2048 * 256, 2000000),
        name="pool_early" if done is None else "pool_late",
    )(core, near_by(packed), *[pltpu.with_memory_space_constraint(a, pltpu.HBM) for a in held])


def combine(parts, ids):
    chips, span, width = parts.shape
    return pl.pallas_call(
        combine_kernel,
        out_shape=pltpu.VMEM((span + ids.shape[0], width), jnp.float32),
        compiler_params=params(),
        cost_estimate=cost(200000, 900000),
        name="combine",
    )(near_by(parts), near_by(ids))


def owner(incoming, stale, table, accum):
    table_like = pltpu.VMEM(table.shape, jnp.float32)
    rows = incoming.shape[0] - stale.shape[0]
    change = pltpu.VMEM((rows, table.shape[1]), jnp.float32)
    return pl.pallas_call(
        owner_kernel,
        out_shape=(table_like, table_like, change),
        compiler_params=params(),
        cost_estimate=cost(4 * 512 * 192 * 256, 1300000),
        name="owner",
    )(*[near_by(a) for a in (incoming, stale, table, accum)])


def store(*arrays):
    count = len(arrays)
    return pl.pallas_call(
        store_kernel,
        out_shape=tuple(pltpu.HBM(a.shape, a.dtype) for a in arrays),
        in_specs=[pl.BlockSpec(memory_space=pltpu.VMEM)] * count,
        out_specs=(pl.BlockSpec(memory_space=pltpu.HBM),) * count,
        scratch_shapes=[pltpu.SemaphoreType.DMA((count,))],
        compiler_params=params(),
        cost_estimate=cost(0, 2 * sum(4 * a.size for a in arrays)),
        name="store",
    )(*[near_by(a) for a in arrays])


def spread(change, live, chips):
    return pl.pallas_call(
        spread_kernel,
        out_shape=pltpu.VMEM((chips,) + change.shape, jnp.float32),
        compiler_params=params(),
        cost_estimate=cost(200000, 900000),
        name="spread",
    )(near_by(change), near_by(live))


def refresh(core, cache_rows, change, done=None):
    flip = done is not None
    chips, span, width = change.shape
    vmem = pl.BlockSpec(memory_space=pltpu.VMEM)
    hbm = pl.BlockSpec(memory_space=pltpu.HBM)
    args = [core, near_by(cache_rows.reshape(chips, 2, span, width)), near_by(change)]
    args = args + ([done] if flip else [])
    return pl.pallas_call(
        functools.partial(refresh_kernel, flip=flip),
        out_shape=jax.ShapeDtypeStruct((chips, 2, span, width), jnp.float32),
        in_specs=[pl.BlockSpec(memory_space=pltpu.SMEM), vmem, vmem] + ([hbm] if flip else []),
        out_specs=hbm,
        scratch_shapes=[
            pltpu.VMEM((chips, span, width), jnp.float32),
            pltpu.SemaphoreType.DMA((chips,)),
        ],
        input_output_aliases={3: 0} if flip else {},
        compiler_params=params(),
        cost_estimate=cost(400000, 2400000),
        name="refresh_other" if flip else "refresh_mine",
    )(*args)


def shards(
    cache, counts, hot_rows, lookups, bag_lengths, projection, grad_out, table, accum, stale
):
    n_own = hot_rows.shape[2]
    chips = lax.axis_size("y")
    capacity = hot_rows.shape[3]
    slots, width = cache.shape[1:]
    span = n_own * capacity
    lookup = lookups.reshape(LOOKUP_ROWS, 128)
    lengths = bag_lengths.reshape(LENGTH_ROWS, 128)
    core = lax.axis_index("core").astype(jnp.int32).reshape(1)
    grp = lax.axis_index(GRP).astype(jnp.int32).reshape(1)
    swap = [(0, 1), (1, 0)]

    mine, given, start = first_slots(
        core, lookup, lengths, grad_out[0, 0], projection, chips, span
    )
    taken = lax.ppermute(given, "core", swap)
    own, ids, flags, live = own_slots(
        core, grp, mine, chips, hot_rows[0].transpose(0, 2, 1), stale[0, 0].T, counts[0]
    )
    half = both_slots(core, taken, own, start, mine.shape[0])
    half, late = lax.optimization_barrier((half, mine))
    projected = pool(core, late, cache[0], projection, 0)
    half, projected, ids, flags, live = lax.optimization_barrier(
        (half, projected, ids, flags, live)
    )
    parts = lax.all_to_all(half, "y", split_axis=0, concat_axis=0, tiled=True)
    summed = combine(parts, ids)
    summed = summed.reshape(-1, 1, width)
    incoming = lax.all_to_all(summed, OWN, split_axis=0, concat_axis=0, tiled=True)
    incoming = incoming.reshape(-1, width)
    table_new, accum_new, change = owner(incoming, flags, table[0, 0], accum[0, 0])

    returned = lax.all_to_all(
        change.reshape(n_own, capacity, width), OWN, split_axis=0, concat_axis=0, tiled=True
    )
    wide = spread(returned.reshape(span, width), live, chips)
    near = lax.all_to_all(wide, "y", split_axis=0, concat_axis=0, tiled=True)
    near, projected, late = lax.optimization_barrier((near, projected, late))
    projected = pool(core, late, cache[0], projection, 1, done=projected)
    near, projected = lax.optimization_barrier((near, projected))
    far = lax.ppermute(near, "core", swap)
    near, table_new, accum_new = lax.optimization_barrier((near, table_new, accum_new))
    table_new, accum_new = store(table_new, accum_new)
    refreshed = refresh(core, cache[0], near)
    far, table_new, accum_new = lax.optimization_barrier((far, table_new, accum_new))
    refreshed = refresh(core, cache[0], far, done=refreshed)

    return (
        projected[None, None],
        table_new[None, None],
        accum_new[None, None],
        refreshed.reshape(1, slots, width),
    )


def solution(mesh):
    chips = Mesh(mesh.devices.reshape(4, 12, 8, 2), ("x", "z", "y", "core"))
    return jax.shard_map(
        shards,
        mesh=chips,
        in_specs=(
            P(OWN, None, None),
            P(OWN, None, None),
            P(OWN, None, None, None),
            P(OWN, GRP, None),
            P(OWN, GRP, None),
            P(),
            P(OWN, GRP, None, None),
            P(OWN, GRP, None, None),
            P(OWN, GRP, None, None),
            P(OWN, GRP, None, None),
        ),
        out_specs=(
            P(OWN, GRP, None, None),
            P(OWN, GRP, None, None),
            P(OWN, GRP, None, None),
            P(OWN, None, None),
        ),
        check_vma=False,
    )
```

```python
import functools

import jax
import jax.numpy as jnp
from jax import lax
from jax.experimental import pallas as pl
from jax.experimental.pallas import tpu as pltpu
from jax.sharding import Mesh
from jax.sharding import PartitionSpec as P

learn_rate = 0.3
epsilon = 1e-06
LOOKUP_ROWS = 16
LENGTH_ROWS = 2
OWN = ("x", "z")
GRP = ("y", "core")
STEP = 4
GROUPS = 16
VMEM_BYTES = 40 * 1024 * 1024


def split(values):
    high = values.astype(jnp.bfloat16)
    low = (values - high.astype(jnp.float32)).astype(jnp.bfloat16)
    return jnp.concatenate([high, low], axis=1)


def joined(values):
    width = values.shape[1] // 2
    return values[:, :width] + values[:, width:]


def row_of(ref, first, count):
    return jnp.concatenate([ref[r : r + 1, :] for r in range(first, first + count)], axis=1)


def bag_hot(lengths):
    bags = lengths.shape[1]
    before = lax.broadcasted_iota(jnp.int32, (bags, bags), 0)
    after = lax.broadcasted_iota(jnp.int32, (bags, bags), 1)
    upper = jnp.where(before <= after, 1.0, 0.0).astype(jnp.bfloat16)
    tall = jnp.broadcast_to(lengths, (8, bags)).astype(jnp.bfloat16)
    ends = jnp.dot(tall, upper, preferred_element_type=jnp.float32)[0:1, :]
    starts = ends - lengths
    ends = ends.astype(jnp.int32)
    starts = starts.astype(jnp.int32)
    position = lax.broadcasted_iota(jnp.int32, (LOOKUP_ROWS * 128, bags), 0)
    inside = (position >= starts) & (position < ends)
    return jnp.where(inside, 1.0, 0.0).astype(jnp.bfloat16)


def slot_parts(lookup, span, groups):
    group = jnp.zeros_like(lookup)
    for k in range(1, groups):
        group = group + jnp.where(lookup >= k * span, 1, 0)
    place = lookup - group * span
    rows = lax.broadcasted_iota(jnp.int32, (span, lookup.shape[1]), 0)
    hot = jnp.where(rows == place, 1.0, 0.0).astype(jnp.bfloat16)
    return group, hot


def in_group(group, k):
    return jnp.where(group == k, 1.0, 0.0).astype(jnp.bfloat16)


def first_kernel(
    core_ref, lookup_hbm, length_hbm, cotangent_hbm, projection_hbm,
    packed_ref, given_ref, start_ref,
    lookup, length, cotangent, projection, arrived,
):
    some, span, _ = start_ref.shape
    bags = cotangent.shape[0]
    sources = (lookup_hbm, length_hbm, cotangent_hbm, projection_hbm)
    copies = [
        pltpu.make_async_copy(source, target, arrived.at[i])
        for i, (source, target) in enumerate(zip(sources, (lookup, length, cotangent, projection)))
    ]
    for copy in copies:
        copy.start()
    for copy in copies:
        copy.wait()
    packed_ref[:bags, :] = lax.dot_general(
        cotangent[...],
        projection[...],
        (((1,), (1,)), ((), ())),
        preferred_element_type=jnp.float32,
    )
    packed_ref[bags : bags + LOOKUP_ROWS, :] = lookup[...].astype(jnp.float32)
    tail = jnp.zeros((8 - LENGTH_ROWS, 128), jnp.float32)
    packed_ref[bags + LOOKUP_ROWS :, :] = jnp.concatenate(
        [length[...].astype(jnp.float32), tail], axis=0
    )

    rest = packed_ref.shape[0] - span
    given_ref[some, :, :] = packed_ref[:span, :]
    given_ref[some + 1, :rest, :] = packed_ref[span:, :]

    @pl.when(core_ref[0] == 0)
    def _():
        for place, delta in slot_parts_of(1, packed_ref, some, span):
            given_ref[place, :, :] = delta

    @pl.when(core_ref[0] == 1)
    def _():
        for place, delta in slot_parts_of(1, packed_ref, some, span):
            start_ref[place, :, :] = delta


def unpack(packed_ref):
    bags = packed_ref.shape[0] - LOOKUP_ROWS - 8
    lookup = row_of(packed_ref, bags, LOOKUP_ROWS).astype(jnp.int32)
    return lookup, row_of(packed_ref, bags + LOOKUP_ROWS, LENGTH_ROWS)


def slot_parts_of(core, packed_ref, chips, span, first=0):
    lookup, lengths = unpack(packed_ref)
    bags = lengths.shape[1]
    rows = jnp.dot(
        bag_hot(lengths), split(packed_ref[:bags, :]), preferred_element_type=jnp.float32
    ).astype(jnp.bfloat16)
    group, hot = slot_parts(lookup, span, GROUPS)
    for y in range(first, chips, STEP):
        slots = jnp.concatenate(
            [hot * in_group(group, 2 * j + core) for j in range(y, y + STEP)], axis=0
        )
        delta = joined(jnp.dot(slots, rows, preferred_element_type=jnp.float32))
        yield pl.ds(y, STEP), delta.reshape(STEP, span, delta.shape[1])


def own_kernel(
    core_ref, grp_ref, packed_ref, hot_ref, stale_ref, counts_ref,
    out_ref, ids_ref, flags_ref, live_ref,
):
    chips, span, width = out_ref.shape
    _, capacity, owners = hot_ref.shape
    ids = hot_ref[grp_ref[0], :, :]
    ids_ref[...] = 16.0 * turned(lax.shift_right_logical(ids, 4), width) + turned(ids & 15, width)
    flags_ref[...] = turned(stale_ref[...], width)
    place = lax.broadcasted_iota(jnp.int32, (span, owners), 0) - (
        capacity * lax.broadcasted_iota(jnp.int32, (span, owners), 1)
    )
    counts = counts_ref[pl.ds(grp_ref[0], 1), :]
    live = jnp.where((place >= 0) & (place < counts), 1.0, 0.0).astype(jnp.bfloat16)
    ones = jnp.ones((owners, width), jnp.bfloat16)
    live_ref[...] = jnp.dot(live, ones, preferred_element_type=jnp.float32)

    @pl.when(core_ref[0] == 0)
    def _():
        for place, delta in slot_parts_of(0, packed_ref, chips, span):
            out_ref[place, :, :] = delta

    @pl.when(core_ref[0] == 1)
    def _():
        for place, delta in slot_parts_of(1, packed_ref, chips, span, first=chips // 2):
            out_ref[place, :, :] = delta


def both_kernel(core_ref, taken_ref, own_ref, start_ref, out_ref, packed):
    chips, span, _ = out_ref.shape
    some = chips // 2
    packed[:span, :] = taken_ref[some, :, :]
    packed[span:, :] = taken_ref[some + 1, : packed.shape[0] - span, :]

    @pl.when(core_ref[0] == 0)
    def _():
        for place, delta in slot_parts_of(0, packed, chips, span):
            out_ref[place, :, :] = own_ref[place, :, :] + delta

    @pl.when(core_ref[0] == 1)
    def _():
        out_ref[:some, :, :] = start_ref[...] + taken_ref[:some, :, :]
        for place, delta in slot_parts_of(1, packed, chips, span, first=some):
            out_ref[place, :, :] = own_ref[place, :, :] + delta


def turned(values, width):
    rows, columns = values.shape
    tall = jnp.concatenate([values, jnp.zeros((8 - rows, columns), values.dtype)], axis=0)
    lane = lax.broadcasted_iota(jnp.int32, (8, width), 1)
    unit = jnp.where(lax.broadcasted_iota(jnp.int32, (8, width), 0) == lane, 1.0, 0.0)
    return lax.dot_general(
        tall.astype(jnp.float32).astype(jnp.bfloat16),
        unit.astype(jnp.bfloat16),
        (((0,), (0,)), ((), ())),
        preferred_element_type=jnp.float32,
    )


def pool_kernel(core_ref, packed_ref, cache_hbm, projection_hbm, *refs, turn):
    out_hbm, count_ref, ready, cache_ref, projection_ref, moved = refs[-6:]

    @pl.when(core_ref[0] == turn)
    def _():
        copies = [
            pltpu.make_async_copy(cache_hbm, cache_ref, moved.at[0]),
            pltpu.make_async_copy(projection_hbm, projection_ref, moved.at[1]),
        ]
        for copy in copies:
            copy.start()
        slots = cache_ref.shape[0]
        span = 192
        groups = slots // span
        lookup, lengths = unpack(packed_ref)
        bags = bag_hot(lengths)
        group, hot = slot_parts(lookup, span, groups)
        for k in range(0, groups, STEP):
            chosen = jnp.concatenate([hot * in_group(group, j) for j in range(k, k + STEP)], axis=0)
            count = jnp.dot(chosen, bags, preferred_element_type=jnp.float32)
            count_ref[k * span : (k + STEP) * span, :] = count.astype(jnp.bfloat16)
        for copy in copies:
            copy.wait()
        pooled = lax.dot_general(
            count_ref[...],
            split(cache_ref[...]),
            (((0,), (0,)), ((), ())),
            preferred_element_type=jnp.float32,
        )
        pooled = joined(pooled).astype(jnp.bfloat16)
        ready[...] = jnp.dot(
            pooled, projection_ref[...], preferred_element_type=jnp.float32
        ).astype(jnp.bfloat16)
        copy = pltpu.make_async_copy(ready, out_hbm, moved.at[2])
        copy.start()
        copy.wait()


def combine_kernel(parts_ref, ids_ref, out_ref):
    owners, _ = ids_ref.shape
    capacity = parts_ref.shape[1] // owners
    out_ref[pl.ds(capacity, owners, stride=capacity + 1), :] = ids_ref[...]
    for c in range(capacity):
        rows = pl.ds(c, owners, stride=capacity)
        total = parts_ref[0, rows, :]
        for y in range(1, parts_ref.shape[0]):
            total = total + parts_ref[y, rows, :]
        out_ref[pl.ds(c, owners, stride=capacity + 1), :] = total


def owner_kernel(
    incoming_ref, stale_ref, table_ref, accum_ref, table_new_ref, accum_new_ref, change_ref
):
    holders = stale_ref.shape[0]
    capacity = incoming_ref.shape[0] // holders - 1
    table_rows = table_ref.shape[0]

    def taken(c):
        return incoming_ref[pl.ds(c, holders, stride=capacity + 1), :]

    ids = taken(capacity)[:, :capacity].astype(jnp.int32)
    stale = stale_ref[...]
    row = lax.broadcasted_iota(jnp.int32, (holders, table_rows), 1)
    hot = [jnp.where(row == ids[:, c : c + 1], 1.0, 0.0) for c in range(capacity)]
    wanted = [hot[c] * stale[:, c : c + 1] for c in range(capacity)]
    incoming = jnp.concatenate([taken(c) for c in range(capacity)], axis=0)
    gradient = joined(
        lax.dot_general(
            jnp.concatenate(hot, axis=0).astype(jnp.bfloat16),
            split(incoming),
            (((0,), (0,)), ((), ())),
            preferred_element_type=jnp.float32,
        )
    )
    accum_new = accum_ref[...] + gradient * gradient
    accum_new_ref[...] = accum_new
    old = table_ref[...]
    new = old - learn_rate * gradient / (jnp.sqrt(accum_new) + epsilon)
    table_new_ref[...] = new
    change = joined(
        jnp.dot(
            jnp.concatenate(wanted, axis=0).astype(jnp.bfloat16),
            split(new - old),
            preferred_element_type=jnp.float32,
        )
    )
    for c in range(capacity):
        change_ref[pl.ds(c, holders, stride=capacity), :] = change[
            c * holders : (c + 1) * holders, :
        ]


def spread_kernel(change_ref, live_ref, out_ref):
    change = jnp.where(live_ref[...] > 0.5, change_ref[...], 0.0)
    for y in range(out_ref.shape[0]):
        out_ref[y, :, :] = change


def store_kernel(*refs):
    count = len(refs) // 2
    sent = refs[-1]
    copies = [
        pltpu.make_async_copy(refs[i], refs[count + i], sent.at[i]) for i in range(count)
    ]
    for copy in copies:
        copy.start()
    for copy in copies:
        copy.wait()


def refresh_kernel(core_ref, cache_ref, change_ref, *refs, flip):
    out_hbm, ready, sent = refs[-3:]
    chips = change_ref.shape[0]
    core = 1 - core_ref[0] if flip else core_ref[0]
    copies = []
    for y in range(chips):
        ready[y, :, :] = cache_ref[y, core, :, :] + change_ref[y, :, :]
        copies.append(pltpu.make_async_copy(ready.at[y], out_hbm.at[y, core], sent.at[y]))
        copies[-1].start()
    for copy in copies:
        copy.wait()


def params():
    return pltpu.CompilerParams(vmem_limit_bytes=VMEM_BYTES)


def near_by(array):
    return pltpu.with_memory_space_constraint(array, pltpu.VMEM)


def cost(flops, moved):
    return pl.CostEstimate(flops=flops, bytes_accessed=moved, transcendentals=0)


def first_slots(core, lookup, lengths, cotangent, projection, chips, span):
    rows = cotangent.shape[0] + LOOKUP_ROWS + 8
    width = projection.shape[0]
    given = (lookup, lengths, cotangent, projection)
    held = [pltpu.with_memory_space_constraint(a, pltpu.HBM) for a in given]
    return pl.pallas_call(
        first_kernel,
        out_shape=(
            pltpu.VMEM((rows, width), jnp.float32),
            pltpu.VMEM((chips // 2 + 2, span, width), jnp.float32),
            pltpu.VMEM((chips // 2, span, width), jnp.float32),
        ),
        in_specs=[pl.BlockSpec(memory_space=pltpu.SMEM)]
        + [pl.BlockSpec(memory_space=pltpu.HBM)] * 4,
        out_specs=(pl.BlockSpec(memory_space=pltpu.VMEM),) * 3,
        scratch_shapes=[pltpu.VMEM(a.shape, a.dtype) for a in given]
        + [pltpu.SemaphoreType.DMA((4,))],
        compiler_params=params(),
        cost_estimate=cost(3072 * 2048 * 256, 1000000),
        name="first_slots",
    )(core, *held)


def own_slots(core, grp, packed, chips, hot, stale, counts):
    _, capacity, owners = hot.shape
    span, width = capacity * owners, packed.shape[1]
    vmem = pl.BlockSpec(memory_space=pltpu.VMEM)
    smem = pl.BlockSpec(memory_space=pltpu.SMEM)
    given = (packed, hot, stale, counts)
    return pl.pallas_call(
        own_kernel,
        out_shape=(
            pltpu.VMEM((chips, span, width), jnp.float32),
            pltpu.VMEM((owners, width), jnp.float32),
            pltpu.VMEM((owners, width), jnp.float32),
            pltpu.VMEM((span, width), jnp.float32),
        ),
        in_specs=[smem, smem] + [vmem] * len(given),
        out_specs=(vmem,) * 4,
        compiler_params=params(),
        cost_estimate=cost(3072 * 2048 * 256, 1000000),
        name="own_slots",
    )(core, grp, *[near_by(a) for a in given])


def both_slots(core, taken, own, start, rows):
    vmem = pl.BlockSpec(memory_space=pltpu.VMEM)
    return pl.pallas_call(
        both_kernel,
        out_shape=pltpu.VMEM(own.shape, jnp.float32),
        in_specs=[pl.BlockSpec(memory_space=pltpu.SMEM), vmem, vmem, vmem],
        out_specs=vmem,
        scratch_shapes=[pltpu.VMEM((rows, start.shape[2]), jnp.float32)],
        compiler_params=params(),
        cost_estimate=cost(3072 * 2048 * 256, 1800000),
        name="both_slots",
    )(core, near_by(taken), near_by(own), near_by(start))


def pool(core, packed, cache_rows, projection, turn, done=None):
    bags = packed.shape[0] - LOOKUP_ROWS - 8
    out = pltpu.HBM((bags, projection.shape[1]), jnp.bfloat16)
    hbm = pl.BlockSpec(memory_space=pltpu.HBM)
    held = [cache_rows, projection] + ([] if done is None else [done])
    return pl.pallas_call(
        functools.partial(pool_kernel, turn=turn),
        out_shape=out,
        in_specs=[
            pl.BlockSpec(memory_space=pltpu.SMEM),
            pl.BlockSpec(memory_space=pltpu.VMEM),
        ]
        + [hbm] * len(held),
        out_specs=hbm,
        scratch_shapes=[
            pltpu.VMEM((cache_rows.shape[0], bags), jnp.bfloat16),
            pltpu.VMEM(out.shape, jnp.bfloat16),
            pltpu.VMEM(cache_rows.shape, cache_rows.dtype),
            pltpu.VMEM(projection.shape, projection.dtype),
            pltpu.SemaphoreType.DMA((3,)),
        ],
        input_output_aliases={} if done is None else {4: 0},
        compiler_params=params(),
        cost_estimate=cost(2 * 3072 * 2048 * 256, 2000000),
        name="pool_early" if done is None else "pool_late",
    )(core, near_by(packed), *[pltpu.with_memory_space_constraint(a, pltpu.HBM) for a in held])


def combine(parts, ids):
    chips, span, width = parts.shape
    return pl.pallas_call(
        combine_kernel,
        out_shape=pltpu.VMEM((span + ids.shape[0], width), jnp.float32),
        compiler_params=params(),
        cost_estimate=cost(200000, 900000),
        name="combine",
    )(near_by(parts), near_by(ids))


def owner(incoming, stale, table, accum):
    table_like = pltpu.VMEM(table.shape, jnp.float32)
    rows = incoming.shape[0] - stale.shape[0]
    change = pltpu.VMEM((rows, table.shape[1]), jnp.float32)
    return pl.pallas_call(
        owner_kernel,
        out_shape=(table_like, table_like, change),
        compiler_params=params(),
        cost_estimate=cost(4 * 512 * 192 * 256, 1300000),
        name="owner",
    )(*[near_by(a) for a in (incoming, stale, table, accum)])


def store(*arrays):
    count = len(arrays)
    return pl.pallas_call(
        store_kernel,
        out_shape=tuple(pltpu.HBM(a.shape, a.dtype) for a in arrays),
        in_specs=[pl.BlockSpec(memory_space=pltpu.VMEM)] * count,
        out_specs=(pl.BlockSpec(memory_space=pltpu.HBM),) * count,
        scratch_shapes=[pltpu.SemaphoreType.DMA((count,))],
        compiler_params=params(),
        cost_estimate=cost(0, 2 * sum(4 * a.size for a in arrays)),
        name="store",
    )(*[near_by(a) for a in arrays])


def spread(change, live, chips):
    return pl.pallas_call(
        spread_kernel,
        out_shape=pltpu.VMEM((chips,) + change.shape, jnp.float32),
        compiler_params=params(),
        cost_estimate=cost(200000, 900000),
        name="spread",
    )(near_by(change), near_by(live))


def refresh(core, cache_rows, change, done=None):
    flip = done is not None
    chips, span, width = change.shape
    vmem = pl.BlockSpec(memory_space=pltpu.VMEM)
    hbm = pl.BlockSpec(memory_space=pltpu.HBM)
    args = [core, near_by(cache_rows.reshape(chips, 2, span, width)), near_by(change)]
    args = args + ([done] if flip else [])
    return pl.pallas_call(
        functools.partial(refresh_kernel, flip=flip),
        out_shape=jax.ShapeDtypeStruct((chips, 2, span, width), jnp.float32),
        in_specs=[pl.BlockSpec(memory_space=pltpu.SMEM), vmem, vmem] + ([hbm] if flip else []),
        out_specs=hbm,
        scratch_shapes=[
            pltpu.VMEM((chips, span, width), jnp.float32),
            pltpu.SemaphoreType.DMA((chips,)),
        ],
        input_output_aliases={3: 0} if flip else {},
        compiler_params=params(),
        cost_estimate=cost(400000, 2400000),
        name="refresh_other" if flip else "refresh_mine",
    )(*args)


def shards(
    cache, counts, hot_rows, lookups, bag_lengths, projection, grad_out, table, accum, stale
):
    n_own = hot_rows.shape[2]
    chips = lax.axis_size("y")
    capacity = hot_rows.shape[3]
    slots, width = cache.shape[1:]
    span = n_own * capacity
    lookup = lookups.reshape(LOOKUP_ROWS, 128)
    lengths = bag_lengths.reshape(LENGTH_ROWS, 128)
    core = lax.axis_index("core").astype(jnp.int32).reshape(1)
    grp = lax.axis_index(GRP).astype(jnp.int32).reshape(1)
    swap = [(0, 1), (1, 0)]

    mine, given, start = first_slots(
        core, lookup, lengths, grad_out[0, 0], projection, chips, span
    )
    taken = lax.ppermute(given, "core", swap)
    own, ids, flags, live = own_slots(
        core, grp, mine, chips, hot_rows[0].transpose(0, 2, 1), stale[0, 0].T, counts[0]
    )
    half = both_slots(core, taken, own, start, mine.shape[0])
    half, late = lax.optimization_barrier((half, mine))
    projected = pool(core, late, cache[0], projection, 0)
    half, projected, ids, flags, live = lax.optimization_barrier(
        (half, projected, ids, flags, live)
    )
    parts = lax.all_to_all(half, "y", split_axis=0, concat_axis=0, tiled=True)
    summed = combine(parts, ids)
    summed = summed.reshape(-1, 1, width)
    incoming = lax.all_to_all(summed, OWN, split_axis=0, concat_axis=0, tiled=True)
    incoming = incoming.reshape(-1, width)
    table_new, accum_new, change = owner(incoming, flags, table[0, 0], accum[0, 0])

    returned = lax.all_to_all(
        change.reshape(n_own, capacity, width), OWN, split_axis=0, concat_axis=0, tiled=True
    )
    wide = spread(returned.reshape(span, width), live, chips)
    near = lax.all_to_all(wide, "y", split_axis=0, concat_axis=0, tiled=True)
    near, projected, late = lax.optimization_barrier((near, projected, late))
    projected = pool(core, late, cache[0], projection, 1, done=projected)
    near, projected = lax.optimization_barrier((near, projected))
    far = lax.ppermute(near, "core", swap)
    near, table_new, accum_new = lax.optimization_barrier((near, table_new, accum_new))
    table_new, accum_new = store(table_new, accum_new)
    refreshed = refresh(core, cache[0], near)
    far, table_new, accum_new = lax.optimization_barrier((far, table_new, accum_new))
    refreshed = refresh(core, cache[0], far, done=refreshed)

    return (
        projected[None, None],
        table_new[None, None],
        accum_new[None, None],
        refreshed.reshape(1, slots, width),
    )


def solution(mesh):
    chips = Mesh(mesh.devices.reshape(4, 12, 8, 2), ("x", "z", "y", "core"))
    return jax.shard_map(
        shards,
        mesh=chips,
        in_specs=(
            P(OWN, None, None),
            P(OWN, None, None),
            P(OWN, None, None, None),
            P(OWN, GRP, None),
            P(OWN, GRP, None),
            P(),
            P(OWN, GRP, None, None),
            P(OWN, GRP, None, None),
            P(OWN, GRP, None, None),
            P(OWN, GRP, None, None),
        ),
        out_specs=(
            P(OWN, GRP, None, None),
            P(OWN, GRP, None, None),
            P(OWN, GRP, None, None),
            P(OWN, None, None),
        ),
        check_vma=False,
    )
```

```python
import functools

import jax
import jax.numpy as jnp
from jax import lax
from jax.experimental import pallas as pl
from jax.experimental.pallas import tpu as pltpu
from jax.sharding import Mesh
from jax.sharding import PartitionSpec as P

learn_rate = 0.3
epsilon = 1e-06
LOOKUP_ROWS = 16
LENGTH_ROWS = 2
OWN = ("x", "z")
GRP = ("y", "core")
STEP = 4
VMEM_BYTES = 40 * 1024 * 1024


def split(values):
    high = values.astype(jnp.bfloat16)
    low = (values - high.astype(jnp.float32)).astype(jnp.bfloat16)
    return jnp.concatenate([high, low], axis=1)


def joined(values):
    width = values.shape[1] // 2
    return values[:, :width] + values[:, width:]


def row_of(ref, first, count):
    return jnp.concatenate([ref[r : r + 1, :] for r in range(first, first + count)], axis=1)


def bag_hot(lengths):
    bags = lengths.shape[1]
    before = lax.broadcasted_iota(jnp.int32, (bags, bags), 0)
    after = lax.broadcasted_iota(jnp.int32, (bags, bags), 1)
    upper = jnp.where(before <= after, 1.0, 0.0).astype(jnp.bfloat16)
    tall = jnp.broadcast_to(lengths, (8, bags)).astype(jnp.bfloat16)
    ends = jnp.dot(tall, upper, preferred_element_type=jnp.float32)[0:1, :]
    starts = ends - lengths
    ends = ends.astype(jnp.int32)
    starts = starts.astype(jnp.int32)
    position = lax.broadcasted_iota(jnp.int32, (LOOKUP_ROWS * 128, bags), 0)
    inside = (position >= starts) & (position < ends)
    return jnp.where(inside, 1.0, 0.0).astype(jnp.bfloat16)


def slot_parts(lookup, span, groups):
    group = jnp.zeros_like(lookup)
    for k in range(1, groups):
        group = group + jnp.where(lookup >= k * span, 1, 0)
    place = lookup - group * span
    rows = lax.broadcasted_iota(jnp.int32, (span, lookup.shape[1]), 0)
    hot = jnp.where(rows == place, 1.0, 0.0).astype(jnp.bfloat16)
    return group, hot


def in_group(group, k):
    return jnp.where(group == k, 1.0, 0.0).astype(jnp.bfloat16)


def first_kernel(
    core_ref, lookup_hbm, length_hbm, cotangent_hbm, projection_hbm,
    packed_ref, given_ref, start_ref,
    lookup, length, cotangent, projection, arrived,
):
    chips, span, _ = start_ref.shape
    bags = cotangent.shape[0]
    sources = (lookup_hbm, length_hbm, cotangent_hbm, projection_hbm)
    copies = [
        pltpu.make_async_copy(source, target, arrived.at[i])
        for i, (source, target) in enumerate(zip(sources, (lookup, length, cotangent, projection)))
    ]
    for copy in copies:
        copy.start()
    for copy in copies:
        copy.wait()
    packed_ref[:bags, :] = lax.dot_general(
        cotangent[...],
        projection[...],
        (((1,), (1,)), ((), ())),
        preferred_element_type=jnp.float32,
    )
    packed_ref[bags : bags + LOOKUP_ROWS, :] = lookup[...].astype(jnp.float32)
    tail = jnp.zeros((8 - LENGTH_ROWS, 128), jnp.float32)
    packed_ref[bags + LOOKUP_ROWS :, :] = jnp.concatenate(
        [length[...].astype(jnp.float32), tail], axis=0
    )

    @pl.when(core_ref[0] == 0)
    def _():
        for place, delta in slot_parts_of(1, packed_ref, chips, span, STEP):
            given_ref[place, :, :] = delta

    @pl.when(core_ref[0] == 1)
    def _():
        rest = packed_ref.shape[0] - span
        given_ref[0, :, :] = packed_ref[:span, :]
        given_ref[1, :rest, :] = packed_ref[span:, :]
        for place, delta in slot_parts_of(1, packed_ref, chips, span, STEP):
            start_ref[place, :, :] = delta


def unpack(packed_ref):
    bags = packed_ref.shape[0] - LOOKUP_ROWS - 8
    lookup = row_of(packed_ref, bags, LOOKUP_ROWS).astype(jnp.int32)
    return lookup, row_of(packed_ref, bags + LOOKUP_ROWS, LENGTH_ROWS)


def slot_parts_of(core, packed_ref, chips, span, step):
    lookup, lengths = unpack(packed_ref)
    bags = lengths.shape[1]
    rows = jnp.dot(
        bag_hot(lengths), split(packed_ref[:bags, :]), preferred_element_type=jnp.float32
    ).astype(jnp.bfloat16)
    group, hot = slot_parts(lookup, span, 2 * chips)
    for y in range(0, chips, step):
        slots = jnp.concatenate(
            [hot * in_group(group, 2 * j + core) for j in range(y, y + step)], axis=0
        )
        delta = joined(jnp.dot(slots, rows, preferred_element_type=jnp.float32))
        yield pl.ds(y, step), delta.reshape(step, span, delta.shape[1])


def own_kernel(
    core_ref, grp_ref, packed_ref, hot_ref, stale_ref, counts_ref,
    out_ref, ids_ref, flags_ref, live_ref,
):
    chips, span, width = out_ref.shape
    _, capacity, owners = hot_ref.shape
    ids = hot_ref[grp_ref[0], :, :]
    ids_ref[...] = 16.0 * turned(lax.shift_right_logical(ids, 4), width) + turned(ids & 15, width)
    flags_ref[...] = turned(stale_ref[...], width)
    place = lax.broadcasted_iota(jnp.int32, (span, owners), 0) - (
        capacity * lax.broadcasted_iota(jnp.int32, (span, owners), 1)
    )
    counts = counts_ref[pl.ds(grp_ref[0], 1), :]
    live = jnp.where((place >= 0) & (place < counts), 1.0, 0.0).astype(jnp.bfloat16)
    ones = jnp.ones((owners, width), jnp.bfloat16)
    live_ref[...] = jnp.dot(live, ones, preferred_element_type=jnp.float32)

    @pl.when(core_ref[0] == 0)
    def _():
        for place, delta in slot_parts_of(0, packed_ref, chips, span, STEP):
            out_ref[place, :, :] = delta


def both_kernel(core_ref, taken_ref, own_ref, start_ref, out_ref, packed):
    chips, span, _ = out_ref.shape

    @pl.when(core_ref[0] == 0)
    def _():
        packed[:span, :] = taken_ref[0, :, :]
        packed[span:, :] = taken_ref[1, : packed.shape[0] - span, :]
        for place, delta in slot_parts_of(0, packed, chips, span, STEP):
            out_ref[place, :, :] = own_ref[place, :, :] + delta

    @pl.when(core_ref[0] == 1)
    def _():
        out_ref[...] = start_ref[...] + taken_ref[...]


def turned(values, width):
    rows, columns = values.shape
    tall = jnp.concatenate([values, jnp.zeros((8 - rows, columns), values.dtype)], axis=0)
    lane = lax.broadcasted_iota(jnp.int32, (8, width), 1)
    unit = jnp.where(lax.broadcasted_iota(jnp.int32, (8, width), 0) == lane, 1.0, 0.0)
    return lax.dot_general(
        tall.astype(jnp.float32).astype(jnp.bfloat16),
        unit.astype(jnp.bfloat16),
        (((0,), (0,)), ((), ())),
        preferred_element_type=jnp.float32,
    )


def pool_kernel(core_ref, packed_ref, cache_hbm, projection_hbm, *refs, turn):
    out_hbm, count_ref, ready, cache_ref, projection_ref, moved = refs[-6:]

    @pl.when(core_ref[0] == turn)
    def _():
        copies = [
            pltpu.make_async_copy(cache_hbm, cache_ref, moved.at[0]),
            pltpu.make_async_copy(projection_hbm, projection_ref, moved.at[1]),
        ]
        for copy in copies:
            copy.start()
        slots = cache_ref.shape[0]
        span = 192
        groups = slots // span
        lookup, lengths = unpack(packed_ref)
        bags = bag_hot(lengths)
        group, hot = slot_parts(lookup, span, groups)
        for k in range(0, groups, STEP):
            chosen = jnp.concatenate([hot * in_group(group, j) for j in range(k, k + STEP)], axis=0)
            count = jnp.dot(chosen, bags, preferred_element_type=jnp.float32)
            count_ref[k * span : (k + STEP) * span, :] = count.astype(jnp.bfloat16)
            if k == STEP:
                for copy in copies:
                    copy.wait()
        pooled = lax.dot_general(
            count_ref[...],
            split(cache_ref[...]),
            (((0,), (0,)), ((), ())),
            preferred_element_type=jnp.float32,
        )
        pooled = joined(pooled).astype(jnp.bfloat16)
        ready[...] = jnp.dot(
            pooled, projection_ref[...], preferred_element_type=jnp.float32
        ).astype(jnp.bfloat16)
        copy = pltpu.make_async_copy(ready, out_hbm, moved.at[2])
        copy.start()
        copy.wait()


def combine_kernel(parts_ref, ids_ref, out_ref):
    owners, _ = ids_ref.shape
    capacity = parts_ref.shape[1] // owners
    out_ref[pl.ds(capacity, owners, stride=capacity + 1), :] = ids_ref[...]
    for c in range(capacity):
        rows = pl.ds(c, owners, stride=capacity)
        total = parts_ref[0, rows, :]
        for y in range(1, parts_ref.shape[0]):
            total = total + parts_ref[y, rows, :]
        out_ref[pl.ds(c, owners, stride=capacity + 1), :] = total


def owner_kernel(
    incoming_ref, stale_ref, table_ref, accum_ref, table_new_ref, accum_new_ref, change_ref
):
    holders = stale_ref.shape[0]
    capacity = incoming_ref.shape[0] // holders - 1
    table_rows = table_ref.shape[0]

    def taken(c):
        return incoming_ref[pl.ds(c, holders, stride=capacity + 1), :]

    ids = taken(capacity)[:, :capacity].astype(jnp.int32)
    stale = stale_ref[...]
    row = lax.broadcasted_iota(jnp.int32, (holders, table_rows), 1)
    hot = [jnp.where(row == ids[:, c : c + 1], 1.0, 0.0) for c in range(capacity)]
    wanted = [hot[c] * stale[:, c : c + 1] for c in range(capacity)]
    incoming = jnp.concatenate([taken(c) for c in range(capacity)], axis=0)
    gradient = joined(
        lax.dot_general(
            jnp.concatenate(hot, axis=0).astype(jnp.bfloat16),
            split(incoming),
            (((0,), (0,)), ((), ())),
            preferred_element_type=jnp.float32,
        )
    )
    accum_new = accum_ref[...] + gradient * gradient
    accum_new_ref[...] = accum_new
    old = table_ref[...]
    new = old - learn_rate * gradient / (jnp.sqrt(accum_new) + epsilon)
    table_new_ref[...] = new
    change = joined(
        jnp.dot(
            jnp.concatenate(wanted, axis=0).astype(jnp.bfloat16),
            split(new - old),
            preferred_element_type=jnp.float32,
        )
    )
    for c in range(capacity):
        change_ref[pl.ds(c, holders, stride=capacity), :] = change[
            c * holders : (c + 1) * holders, :
        ]


def spread_kernel(change_ref, live_ref, out_ref):
    change = jnp.where(live_ref[...] > 0.5, change_ref[...], 0.0)
    for y in range(out_ref.shape[0]):
        out_ref[y, :, :] = change


def store_kernel(*refs):
    count = len(refs) // 2
    sent = refs[-1]
    copies = [
        pltpu.make_async_copy(refs[i], refs[count + i], sent.at[i]) for i in range(count)
    ]
    for copy in copies:
        copy.start()
    for copy in copies:
        copy.wait()


def refresh_kernel(core_ref, cache_ref, change_ref, *refs, flip):
    out_hbm, ready, sent = refs[-3:]
    chips = change_ref.shape[0]
    core = 1 - core_ref[0] if flip else core_ref[0]
    copies = []
    for y in range(chips):
        ready[y, :, :] = cache_ref[y, core, :, :] + change_ref[y, :, :]
        copies.append(pltpu.make_async_copy(ready.at[y], out_hbm.at[y, core], sent.at[y]))
        copies[-1].start()
    for copy in copies:
        copy.wait()


def params():
    return pltpu.CompilerParams(vmem_limit_bytes=VMEM_BYTES)


def near_by(array):
    return pltpu.with_memory_space_constraint(array, pltpu.VMEM)


def cost(flops, moved):
    return pl.CostEstimate(flops=flops, bytes_accessed=moved, transcendentals=0)


def first_slots(core, lookup, lengths, cotangent, projection, chips, span):
    rows = cotangent.shape[0] + LOOKUP_ROWS + 8
    width = projection.shape[0]
    given = (lookup, lengths, cotangent, projection)
    held = [pltpu.with_memory_space_constraint(a, pltpu.HBM) for a in given]
    return pl.pallas_call(
        first_kernel,
        out_shape=(
            pltpu.VMEM((rows, width), jnp.float32),
            pltpu.VMEM((chips, span, width), jnp.float32),
            pltpu.VMEM((chips, span, width), jnp.float32),
        ),
        in_specs=[pl.BlockSpec(memory_space=pltpu.SMEM)]
        + [pl.BlockSpec(memory_space=pltpu.HBM)] * 4,
        out_specs=(pl.BlockSpec(memory_space=pltpu.VMEM),) * 3,
        scratch_shapes=[pltpu.VMEM(a.shape, a.dtype) for a in given]
        + [pltpu.SemaphoreType.DMA((4,))],
        compiler_params=params(),
        cost_estimate=cost(3072 * 2048 * 256, 1000000),
        name="first_slots",
    )(core, *held)


def own_slots(core, grp, packed, chips, hot, stale, counts):
    _, capacity, owners = hot.shape
    span, width = capacity * owners, packed.shape[1]
    vmem = pl.BlockSpec(memory_space=pltpu.VMEM)
    smem = pl.BlockSpec(memory_space=pltpu.SMEM)
    given = (packed, hot, stale, counts)
    return pl.pallas_call(
        own_kernel,
        out_shape=(
            pltpu.VMEM((chips, span, width), jnp.float32),
            pltpu.VMEM((owners, width), jnp.float32),
            pltpu.VMEM((owners, width), jnp.float32),
            pltpu.VMEM((span, width), jnp.float32),
        ),
        in_specs=[smem, smem] + [vmem] * len(given),
        out_specs=(vmem,) * 4,
        compiler_params=params(),
        cost_estimate=cost(3072 * 2048 * 256, 1000000),
        name="own_slots",
    )(core, grp, *[near_by(a) for a in given])


def both_slots(core, taken, own, start, rows):
    vmem = pl.BlockSpec(memory_space=pltpu.VMEM)
    return pl.pallas_call(
        both_kernel,
        out_shape=pltpu.VMEM(start.shape, jnp.float32),
        in_specs=[pl.BlockSpec(memory_space=pltpu.SMEM), vmem, vmem, vmem],
        out_specs=vmem,
        scratch_shapes=[pltpu.VMEM((rows, start.shape[2]), jnp.float32)],
        compiler_params=params(),
        cost_estimate=cost(3072 * 2048 * 256, 1800000),
        name="both_slots",
    )(core, near_by(taken), near_by(own), near_by(start))


def pool(core, packed, cache_rows, projection, turn, done=None):
    bags = packed.shape[0] - LOOKUP_ROWS - 8
    out = pltpu.HBM((bags, projection.shape[1]), jnp.bfloat16)
    hbm = pl.BlockSpec(memory_space=pltpu.HBM)
    held = [cache_rows, projection] + ([] if done is None else [done])
    return pl.pallas_call(
        functools.partial(pool_kernel, turn=turn),
        out_shape=out,
        in_specs=[
            pl.BlockSpec(memory_space=pltpu.SMEM),
            pl.BlockSpec(memory_space=pltpu.VMEM),
        ]
        + [hbm] * len(held),
        out_specs=hbm,
        scratch_shapes=[
            pltpu.VMEM((cache_rows.shape[0], bags), jnp.bfloat16),
            pltpu.VMEM(out.shape, jnp.bfloat16),
            pltpu.VMEM(cache_rows.shape, cache_rows.dtype),
            pltpu.VMEM(projection.shape, projection.dtype),
            pltpu.SemaphoreType.DMA((3,)),
        ],
        input_output_aliases={} if done is None else {4: 0},
        compiler_params=params(),
        cost_estimate=cost(2 * 3072 * 2048 * 256, 2000000),
        name="pool_early" if done is None else "pool_late",
    )(core, near_by(packed), *[pltpu.with_memory_space_constraint(a, pltpu.HBM) for a in held])


def combine(parts, ids):
    chips, span, width = parts.shape
    return pl.pallas_call(
        combine_kernel,
        out_shape=pltpu.VMEM((span + ids.shape[0], width), jnp.float32),
        compiler_params=params(),
        cost_estimate=cost(200000, 900000),
        name="combine",
    )(near_by(parts), near_by(ids))


def owner(incoming, stale, table, accum):
    table_like = pltpu.VMEM(table.shape, jnp.float32)
    rows = incoming.shape[0] - stale.shape[0]
    change = pltpu.VMEM((rows, table.shape[1]), jnp.float32)
    return pl.pallas_call(
        owner_kernel,
        out_shape=(table_like, table_like, change),
        compiler_params=params(),
        cost_estimate=cost(4 * 512 * 192 * 256, 1300000),
        name="owner",
    )(*[near_by(a) for a in (incoming, stale, table, accum)])


def store(*arrays):
    count = len(arrays)
    return pl.pallas_call(
        store_kernel,
        out_shape=tuple(pltpu.HBM(a.shape, a.dtype) for a in arrays),
        in_specs=[pl.BlockSpec(memory_space=pltpu.VMEM)] * count,
        out_specs=(pl.BlockSpec(memory_space=pltpu.HBM),) * count,
        scratch_shapes=[pltpu.SemaphoreType.DMA((count,))],
        compiler_params=params(),
        cost_estimate=cost(0, 2 * sum(4 * a.size for a in arrays)),
        name="store",
    )(*[near_by(a) for a in arrays])


def spread(change, live, chips):
    return pl.pallas_call(
        spread_kernel,
        out_shape=pltpu.VMEM((chips,) + change.shape, jnp.float32),
        compiler_params=params(),
        cost_estimate=cost(200000, 900000),
        name="spread",
    )(near_by(change), near_by(live))


def refresh(core, cache_rows, change, done=None):
    flip = done is not None
    chips, span, width = change.shape
    vmem = pl.BlockSpec(memory_space=pltpu.VMEM)
    hbm = pl.BlockSpec(memory_space=pltpu.HBM)
    args = [core, near_by(cache_rows.reshape(chips, 2, span, width)), near_by(change)]
    args = args + ([done] if flip else [])
    return pl.pallas_call(
        functools.partial(refresh_kernel, flip=flip),
        out_shape=jax.ShapeDtypeStruct((chips, 2, span, width), jnp.float32),
        in_specs=[pl.BlockSpec(memory_space=pltpu.SMEM), vmem, vmem] + ([hbm] if flip else []),
        out_specs=hbm,
        scratch_shapes=[
            pltpu.VMEM((chips, span, width), jnp.float32),
            pltpu.SemaphoreType.DMA((chips,)),
        ],
        input_output_aliases={3: 0} if flip else {},
        compiler_params=params(),
        cost_estimate=cost(400000, 2400000),
        name="refresh_other" if flip else "refresh_mine",
    )(*args)


def shards(
    cache, counts, hot_rows, lookups, bag_lengths, projection, grad_out, table, accum, stale
):
    n_own = hot_rows.shape[2]
    chips = lax.axis_size("y")
    capacity = hot_rows.shape[3]
    slots, width = cache.shape[1:]
    span = n_own * capacity
    lookup = lookups.reshape(LOOKUP_ROWS, 128)
    lengths = bag_lengths.reshape(LENGTH_ROWS, 128)
    core = lax.axis_index("core").astype(jnp.int32).reshape(1)
    grp = lax.axis_index(GRP).astype(jnp.int32).reshape(1)
    swap = [(0, 1), (1, 0)]

    mine, given, start = first_slots(
        core, lookup, lengths, grad_out[0, 0], projection, chips, span
    )
    taken = lax.ppermute(given, "core", swap)
    own, ids, flags, live = own_slots(
        core, grp, mine, chips, hot_rows[0].transpose(0, 2, 1), stale[0, 0].T, counts[0]
    )
    half = both_slots(core, taken, own, start, mine.shape[0])
    half, late = lax.optimization_barrier((half, mine))
    projected = pool(core, late, cache[0], projection, 0)
    half, projected, ids, flags, live = lax.optimization_barrier(
        (half, projected, ids, flags, live)
    )
    parts = lax.all_to_all(half, "y", split_axis=0, concat_axis=0, tiled=True)
    summed = combine(parts, ids)
    summed = summed.reshape(-1, 1, width)
    incoming = lax.all_to_all(summed, OWN, split_axis=0, concat_axis=0, tiled=True)
    incoming = incoming.reshape(-1, width)
    table_new, accum_new, change = owner(incoming, flags, table[0, 0], accum[0, 0])

    returned = lax.all_to_all(
        change.reshape(n_own, capacity, width), OWN, split_axis=0, concat_axis=0, tiled=True
    )
    wide = spread(returned.reshape(span, width), live, chips)
    near = lax.all_to_all(wide, "y", split_axis=0, concat_axis=0, tiled=True)
    near, projected, late = lax.optimization_barrier((near, projected, late))
    projected = pool(core, late, cache[0], projection, 1, done=projected)
    near, projected = lax.optimization_barrier((near, projected))
    far = lax.ppermute(near, "core", swap)
    near, table_new, accum_new = lax.optimization_barrier((near, table_new, accum_new))
    table_new, accum_new = store(table_new, accum_new)
    refreshed = refresh(core, cache[0], near)
    far, table_new, accum_new = lax.optimization_barrier((far, table_new, accum_new))
    refreshed = refresh(core, cache[0], far, done=refreshed)

    return (
        projected[None, None],
        table_new[None, None],
        accum_new[None, None],
        refreshed.reshape(1, slots, width),
    )


def solution(mesh):
    chips = Mesh(mesh.devices.reshape(4, 12, 8, 2), ("x", "z", "y", "core"))
    return jax.shard_map(
        shards,
        mesh=chips,
        in_specs=(
            P(OWN, None, None),
            P(OWN, None, None),
            P(OWN, None, None, None),
            P(OWN, GRP, None),
            P(OWN, GRP, None),
            P(),
            P(OWN, GRP, None, None),
            P(OWN, GRP, None, None),
            P(OWN, GRP, None, None),
            P(OWN, GRP, None, None),
        ),
        out_specs=(
            P(OWN, GRP, None, None),
            P(OWN, GRP, None, None),
            P(OWN, GRP, None, None),
            P(OWN, None, None),
        ),
        check_vma=False,
    )
```
